128 devices in a mesh: lat: 8 (over x, core), lon: 16 (over y, z).
Axes of the slice: x: 4, y: 4, z: 4, core: 2. Of those that a mesh axis runs over, the one named last changes fastest.
Arguments:
- grid_in: bfloat16 [65536, 227], P(('lat', 'lon')), may hold values from -6 to 6
- grid_export: int32 [16384], P(('lat', 'lon')), may hold values from 0 to 511
- mesh_init: bfloat16 [20480, 512], P(('lat', 'lon')), may hold values from -6 to 6
- encode_senders: int32 [1024, 128], P(('lat', 'lon')), may hold values from 0 to 511, as said below
- encode_slots: int32 [1024], P(('lat', 'lon')), may hold values from 0 to 8, as said below
- encode_receivers: int32 [1024, 128], P(('lat', 'lon')), may hold values from 0 to 159
- encode_live: int32 [128], P(('lat', 'lon')), may hold values from 4 to 8, as said below
- mesh_export: int32 [16384], P(('lat', 'lon')), may hold values from 0 to 159
- process_senders: int32 [1024, 128], P(('lat', 'lon')), may hold values from 0 to 159, as said below
- process_slots: int32 [1024], P(('lat', 'lon')), may hold values from 0 to 8, as said below
- process_receivers: int32 [1024, 128], P(('lat', 'lon')), may hold values from 0 to 159
- process_live: int32 [128], P(('lat', 'lon')), may hold values from 4 to 8, as said below
- grid_weight: bfloat16 [227, 512], replicated, may hold values from -0.375 to 0.375
- sender_weight: bfloat16 [512, 512], replicated, may hold values from -0.25 to 0.25
- receiver_weight: bfloat16 [512, 512], replicated, may hold values from -0.25 to 0.25
- message_weight: bfloat16 [512, 512], replicated, may hold values from -0.25 to 0.25
- update_weight: bfloat16 [512, 512], replicated, may hold values from -0.25 to 0.25
- encode_gain: float32 [512], replicated, may hold values from 0.1 to 1.9
- edge_sender: bfloat16 [512, 512], replicated, may hold values from -0.25 to 0.25
- edge_receiver: bfloat16 [512, 512], replicated, may hold values from -0.25 to 0.25
- edge_message: bfloat16 [512, 512], replicated, may hold values from -0.25 to 0.25
- node_update: bfloat16 [512, 512], replicated, may hold values from -0.25 to 0.25
- node_gain: float32 [512], replicated, may hold values from 0.1 to 1.9
- cotangent: bfloat16 [20480, 512], P(('lat', 'lon')), may hold values from -6 to 6
Outputs:
- mesh_out: bfloat16 [20480, 512], P(('lat', 'lon'))
- grid_grad: float32 [227, 512], replicated
- sender_grad: float32 [512, 512], replicated
- edge_grad: float32 [512, 512], replicated
The draws below stay inside these ranges and needn't reach their ends.
Inputs may be any that keep to these rules, and one draw needn't show every extreme that they name: `encode_slots`: slot of the tile a block's senders lie in: 3 i + j for the tile i - 1 bands and j - 1 sectors away; no slot reaches past the first or the last band. `encode_senders`: in a block of slot 4 a grid row of the tile itself; in other blocks a position below 128 in the source tile's grid_export list. Only a tile's first encode_live blocks hold edges; some tile fills all 8. `process_slots`: slot of the tile a block's senders lie in: 3 i + j for the tile i - 1 bands and j - 1 sectors away; no slot reaches past the first or the last band. `process_senders`: in a block of slot 4 a mesh row of the tile itself; in other blocks a position below 128 in the source tile's mesh_export list. Only a tile's first process_live blocks hold edges; some tile fills all 8.
All inputs are finite; a program needn't handle non-finite values.
Results may differ from the reference program's by a relative error of at most 0.023.
Values may be sent and summed in bfloat16 or wider, within the bound.
No kernel may reach another device: no remote copies, remote signals or barrier semaphores. Data moves between devices by JAX's collectives and lax.ppermute only.
A program may use at most 128 MiB of HBM per device.

```python
import jax
import jax.numpy as jnp
from jax import lax

VARS = 227
LATENT = 512
G_DEV = 512
M_DEV = 160
XR = 128
MXR = 128
TB = 8
PTB = 8
BLOCK_ROWS = 128
TILES = 128
GRID = 65536
MESH = 20480
GBLOCKS = 1024
PBLOCKS = 1024
N_LAT = 8
N_LON = 16


def source_slots(key, per_tile):
    total = N_LAT * N_LON * per_tile
    drawn = jax.random.randint(key, (total,), 0, 18)
    others = drawn - 10
    others = others + (others >= 4).astype(jnp.int32)
    slots = jnp.where(drawn < 10, 4, others)
    bands = jnp.arange(total) // per_tile // N_LON
    outside = (bands == 0) & (slots < 3) | (bands == N_LAT - 1) & (slots >= 6)
    return jnp.where(outside, 4, slots).astype(jnp.int32)


def encode_table(key):
    return source_slots(jax.random.fold_in(key, 5), TB)


def process_table(key):
    return source_slots(jax.random.fold_in(key, 6), PTB)


def pick_senders(key, slots, own_rows, copy_rows):
    first_key, second_key = jax.random.split(key)
    own = jax.random.randint(first_key, (slots.shape[0], BLOCK_ROWS), 0, own_rows)
    copied = jax.random.randint(second_key, (slots.shape[0], BLOCK_ROWS), 0, copy_rows)
    return jnp.where(slots[:, None] == 4, own, copied).astype(jnp.int32)


def live_counts(key, capacity):
    tiles = N_LAT * N_LON
    first_key, second_key = jax.random.split(key)
    counts = jax.random.randint(first_key, (tiles,), capacity // 2, capacity + 1)
    fullest = jax.random.randint(second_key, (), 0, tiles)
    return jnp.where(jnp.arange(tiles) == fullest, capacity, counts).astype(jnp.int32)


def draw_encode_slots(key, part):
    slots = encode_table(key)
    return slots


def draw_encode_senders(key, part):
    slots = encode_table(key)
    key = jax.random.fold_in(key, 22)
    return pick_senders(key, slots, G_DEV, XR)


def draw_encode_live(key, part):
    key = jax.random.fold_in(key, 23)
    return live_counts(key, TB)


def draw_process_slots(key, part):
    slots = process_table(key)
    return slots


def draw_process_senders(key, part):
    slots = process_table(key)
    key = jax.random.fold_in(key, 32)
    return pick_senders(key, slots, M_DEV, MXR)


def draw_process_live(key, part):
    key = jax.random.fold_in(key, 33)
    return live_counts(key, PTB)


def place_ends(result, own_key, least, top_value):
    longest = result.shape.index(max(result.shape))
    spots = []
    for shift in (0, 1):
        where = [jax.random.randint(jax.random.fold_in(own_key, axis), (), 0, length) for axis, length in enumerate(result.shape)]
        where[longest] = (where[longest] + shift) % result.shape[longest]
        spots.append(tuple(where))
    return result.at[spots[0]].set(least).at[spots[1]].set(top_value)


def steps_of(stream_key, shape, cuts, smallest, high):
    level, own = 1.0, jax.random.fold_in(stream_key, 6)
    for axis_at, parts in cuts:
        steps = jnp.exp(jax.random.uniform(jax.random.fold_in(own, axis_at), (parts,), jnp.float32, smallest / len(cuts), high / len(cuts)))
        level = level * jnp.repeat(steps, shape[axis_at] // parts).reshape([-1 if axis == axis_at else 1 for axis in range(len(shape))])
    return level


def gaussian(rng, shape, deviation, most, cuts=(), held_as=jnp.bfloat16):
    array = jax.random.normal(rng, shape, jnp.float32) * deviation
    if len(cuts) > 0:
        array = steps_of(rng, shape, cuts, -0.22, 0.18) * array
    return jnp.clip(array, min=-most, max=most).astype(held_as)


def setup_inputs(seed: int = 0) -> dict:
    seeds = jax.random.split(jax.random.key(seed), 25)
    return {
        "grid_in": gaussian(seeds[0], (GRID, VARS), 1.0, 6.0, ((0, 128),)),
        "grid_export": place_ends(jax.random.randint(seeds[1], (TILES * XR,), 0, G_DEV), jax.random.fold_in(seeds[1], 1), 0, G_DEV - 1).astype(jnp.int32),
        "mesh_init": gaussian(seeds[2], (MESH, LATENT), 1.0, 6.0, ((0, 128),)),
        "encode_senders": draw_encode_senders(jax.random.fold_in(seeds[24], 71), 0),
        "encode_slots": draw_encode_slots(jax.random.fold_in(seeds[24], 71), 0),
        "encode_receivers": place_ends(jax.random.randint(seeds[5], (GBLOCKS, BLOCK_ROWS), 0, M_DEV), jax.random.fold_in(seeds[5], 1), 0, M_DEV - 1).astype(jnp.int32),
        "encode_live": draw_encode_live(jax.random.fold_in(seeds[24], 71), 0),
        "mesh_export": place_ends(jax.random.randint(seeds[7], (TILES * MXR,), 0, M_DEV), jax.random.fold_in(seeds[7], 1), 0, M_DEV - 1).astype(jnp.int32),
        "process_senders": draw_process_senders(jax.random.fold_in(seeds[24], 71), 0),
        "process_slots": draw_process_slots(jax.random.fold_in(seeds[24], 71), 0),
        "process_receivers": place_ends(jax.random.randint(seeds[10], (PBLOCKS, BLOCK_ROWS), 0, M_DEV), jax.random.fold_in(seeds[10], 1), 0, M_DEV - 1).astype(jnp.int32),
        "process_live": draw_process_live(jax.random.fold_in(seeds[24], 71), 0),
        "grid_weight": gaussian(seeds[12], (VARS, LATENT), VARS ** -0.5, 0.375),
        "sender_weight": gaussian(seeds[13], (LATENT, LATENT), LATENT ** -0.5, 0.25),
        "receiver_weight": gaussian(seeds[14], (LATENT, LATENT), LATENT ** -0.5, 0.25),
        "message_weight": gaussian(seeds[15], (LATENT, LATENT), LATENT ** -0.5, 0.25),
        "update_weight": gaussian(seeds[16], (LATENT, LATENT), LATENT ** -0.5, 0.25),
        "encode_gain": jnp.clip(1.0 + 0.18 * jax.random.normal(seeds[17], (LATENT,), jnp.float32), 0.1, 1.9),
        "edge_sender": gaussian(seeds[18], (LATENT, LATENT), LATENT ** -0.5, 0.25),
        "edge_receiver": gaussian(seeds[19], (LATENT, LATENT), LATENT ** -0.5, 0.25),
        "edge_message": gaussian(seeds[20], (LATENT, LATENT), LATENT ** -0.5, 0.25),
        "node_update": gaussian(seeds[21], (LATENT, LATENT), LATENT ** -0.5, 0.25),
        "node_gain": jnp.clip(1.0 + 0.18 * jax.random.normal(seeds[22], (LATENT,), jnp.float32), 0.1, 1.9),
        "cotangent": gaussian(seeds[23], (MESH, LATENT), 1.0, 6.0, ((0, 128),)),
    }


norm_epsilon = 1e-05
blocks_per_turn = 4

def layer_norm(values):
    center = values - lax.optimization_barrier(jnp.mean(values, axis=-1, keepdims=True))
    scale = lax.rsqrt(lax.optimization_barrier(jnp.mean(center * center, axis=-1, keepdims=True)) + norm_epsilon)
    return center * scale

def norm_back(values, upstream):
    center = values - lax.optimization_barrier(jnp.mean(values, axis=-1, keepdims=True))
    scale = lax.rsqrt(lax.optimization_barrier(jnp.mean(center * center, axis=-1, keepdims=True)) + norm_epsilon)
    normed = center * scale
    inner = lax.optimization_barrier(jnp.mean(upstream * normed, axis=-1, keepdims=True))
    return scale * (upstream - lax.optimization_barrier(jnp.mean(upstream, axis=-1, keepdims=True)) - normed * inner)

def silu_slope(values):
    sigmoid_part = jax.nn.sigmoid(values)
    return sigmoid_part * (1.0 + values * (1.0 - sigmoid_part))

def back_dot(left, weight):
    return lax.dot_general(left, weight, (((1,), (1,)), ((), ())), preferred_element_type=jnp.float32)

def cross_dot(left, right):
    return lax.dot_general(left, right, (((0,), (0,)), ((), ())), preferred_element_type=jnp.float32)

def table_rows(senders, slots, own_rows, copy_rows):
    shifted = own_rows + slots[:, None] * copy_rows + senders
    return jnp.where(slots[:, None] == 4, senders, shifted).astype(jnp.int32)

def turn_rows(senders, receivers, live_blocks, block_turn):
    first_block = (block_turn * blocks_per_turn).astype(jnp.int32)
    sender_rows = lax.dynamic_slice_in_dim(senders, first_block, blocks_per_turn, 0).reshape(-1)
    receiver_rows = lax.dynamic_slice_in_dim(receivers, first_block, blocks_per_turn, 0).reshape(-1)
    alive = first_block + jnp.arange(blocks_per_turn).astype(jnp.int32) < live_blocks
    alive = jnp.repeat(alive, senders.shape[1]).astype(jnp.float32)[:, None]
    return (sender_rows, receiver_rows, alive)

def edge_forward(table, receiver_proj, weight, senders, receivers, live_blocks):
    turns = (live_blocks + blocks_per_turn - 1) // blocks_per_turn

    def one_turn(block_turn, summed):
        sender_rows, receiver_rows, alive = turn_rows(senders, receivers, live_blocks, block_turn)
        mixed = jnp.take(table, sender_rows, axis=0).astype(jnp.float32) + jnp.take(receiver_proj, receiver_rows, axis=0)
        active = jax.nn.silu(mixed).astype(jnp.bfloat16)
        message = layer_norm(jnp.dot(active, weight, preferred_element_type=jnp.float32)) * alive
        return summed.at[receiver_rows].add(message)
    return lax.fori_loop(jnp.int32(0), turns.astype(jnp.int32), one_turn, jnp.zeros(receiver_proj.shape, jnp.float32))

def edge_backward(table, receiver_proj, weight, senders, receivers, live_blocks, upstream, want_receiver):
    turns = (live_blocks + blocks_per_turn - 1) // blocks_per_turn

    def one_turn(block_turn, carry):
        table_grad, receiver_grad = carry
        sender_rows, receiver_rows, alive = turn_rows(senders, receivers, live_blocks, block_turn)
        mixed = jnp.take(table, sender_rows, axis=0).astype(jnp.float32) + jnp.take(receiver_proj, receiver_rows, axis=0)
        active = jax.nn.silu(mixed).astype(jnp.bfloat16)
        product = jnp.dot(active, weight, preferred_element_type=jnp.float32)
        product_grad = norm_back(product, jnp.take(upstream, receiver_rows, axis=0) * alive).astype(jnp.bfloat16)
        mixed_grad = back_dot(product_grad, weight) * silu_slope(mixed)
        table_grad = table_grad.at[sender_rows].add(mixed_grad)
        if want_receiver:
            receiver_grad = receiver_grad.at[receiver_rows].add(mixed_grad)
        return (table_grad, receiver_grad)
    start_carry = (jnp.zeros(table.shape, jnp.float32), jnp.zeros(receiver_proj.shape, jnp.float32))
    return lax.fori_loop(jnp.int32(0), turns.astype(jnp.int32), one_turn, start_carry)

def apply_update(base, summed, weight, gain):
    projected = jnp.dot(summed.astype(jnp.bfloat16), weight, preferred_element_type=jnp.float32)
    return (base.astype(jnp.float32) + layer_norm(projected) * gain).astype(jnp.bfloat16)

def update_back(summed, weight, gain, upstream):
    projected = jnp.dot(summed.astype(jnp.bfloat16), weight, preferred_element_type=jnp.float32)
    return back_dot(norm_back(projected, upstream * gain).astype(jnp.bfloat16), weight)

def neighbours(rows):
    tiles = N_LAT * N_LON
    layout = rows.reshape((N_LAT, N_LON) + rows.shape[1:])
    pieces = [jnp.roll(layout, (1 - lat_step, 1 - lon_step), (0, 1)) for lat_step in range(3) for lon_step in range(3)]
    return jnp.stack(pieces, 2).reshape(tiles, 9 * rows.shape[1], rows.shape[2])

def returned(backs, copy_rows):
    tiles = N_LAT * N_LON
    layout = backs.reshape(N_LAT, N_LON, 3, 3, copy_rows, backs.shape[-1])
    pieces = [jnp.roll(layout[:, :, 2 - lat_step, 2 - lon_step], (1 - lat_step, 1 - lon_step), (0, 1)) for lat_step in range(3) for lon_step in range(3)]
    return jnp.stack(pieces, 2).reshape(tiles, 9 * copy_rows, backs.shape[-1])

def reference(grid_in, grid_export, mesh_init, encode_senders, encode_slots, encode_receivers, encode_live, mesh_export, process_senders, process_slots, process_receivers, process_live, grid_weight, sender_weight, receiver_weight, message_weight, update_weight, encode_gain, edge_sender, edge_receiver, edge_message, node_update, node_gain, cotangent):
    tiles = N_LAT * N_LON
    grid_tiles = grid_in.reshape(tiles, G_DEV, VARS)
    grid_picks = grid_export.reshape(tiles, XR)
    mesh_tiles = mesh_init.reshape(tiles, M_DEV, LATENT)
    mesh_picks = mesh_export.reshape(tiles, MXR)
    enc_senders = encode_senders.reshape(tiles, TB, BLOCK_ROWS)
    enc_slots = encode_slots.reshape(tiles, TB)
    enc_receivers = encode_receivers.reshape(tiles, TB, BLOCK_ROWS)
    proc_senders = process_senders.reshape(tiles, PTB, BLOCK_ROWS)
    proc_slots = process_slots.reshape(tiles, PTB)
    proc_receivers = process_receivers.reshape(tiles, PTB, BLOCK_ROWS)
    upstream_tiles = cotangent.reshape(tiles, M_DEV, LATENT)

    def embed_tile(operands):
        grid_rows, picks = operands
        hidden = jax.nn.silu(jnp.dot(grid_rows, grid_weight, preferred_element_type=jnp.float32)).astype(jnp.bfloat16)
        return (hidden, jnp.take(hidden, picks, axis=0))
    hidden_all, exported = lax.map(embed_tile, (grid_tiles, grid_picks))
    grid_copies = neighbours(exported)

    def encode_tile(operands):
        hidden, copies, base, senders, slots, receivers, live_blocks = operands
        table = jnp.concatenate([hidden, copies], 0)
        sender_proj = jnp.dot(table, sender_weight, preferred_element_type=jnp.float32).astype(jnp.bfloat16)
        receiver_proj = jnp.dot(base, receiver_weight, preferred_element_type=jnp.float32)
        rows = table_rows(senders, slots, G_DEV, XR)
        summed = edge_forward(sender_proj, receiver_proj, message_weight, rows, receivers, live_blocks)
        return (apply_update(base, summed, update_weight, encode_gain), summed)
    mesh_state, encode_sums = lax.map(encode_tile, (hidden_all, grid_copies, mesh_tiles, enc_senders, enc_slots, enc_receivers, encode_live))
    mesh_copies = neighbours(jax.vmap(lambda state_rows, pick_rows: jnp.take(state_rows, pick_rows, axis=0))(mesh_state, mesh_picks))

    def process_tile(operands):
        state, copies, senders, slots, receivers, live_blocks, upstream_rows = operands
        table = jnp.concatenate([state, copies], 0)
        edge_table = jnp.dot(table, edge_sender, preferred_element_type=jnp.float32).astype(jnp.bfloat16)
        receiver_terms = jnp.dot(state, edge_receiver, preferred_element_type=jnp.float32)
        rows = table_rows(senders, slots, M_DEV, MXR)
        summed = edge_forward(edge_table, receiver_terms, edge_message, rows, receivers, live_blocks)
        output = apply_update(state, summed, node_update, node_gain)
        flow = upstream_rows.astype(jnp.float32)
        summed_grad = update_back(summed, node_update, node_gain, flow)
        table_grad, receiver_grad = edge_backward(edge_table, receiver_terms, edge_message, rows, receivers, live_blocks, summed_grad, True)
        table_grad_b = table_grad.astype(jnp.bfloat16)
        state_grad = flow + back_dot(receiver_grad.astype(jnp.bfloat16), edge_receiver)
        copy_grad = back_dot(table_grad_b, edge_sender)
        return (output, cross_dot(table, table_grad_b), state_grad + copy_grad[:M_DEV], copy_grad[M_DEV:])
    outputs, edge_terms, state_grads, mesh_backs = lax.map(process_tile, (mesh_state, mesh_copies, proc_senders, proc_slots, proc_receivers, process_live, upstream_tiles))
    mesh_came = returned(mesh_backs, MXR)

    def encode_back_tile(operands):
        hidden, copies, base, senders, slots, receivers, live_blocks, state_grad, came, picks, summed = operands
        state_grad = state_grad.at[picks].add(came.reshape(9, MXR, LATENT).sum(0))
        summed_grad = update_back(summed, update_weight, encode_gain, state_grad)
        table = jnp.concatenate([hidden, copies], 0)
        sender_proj = jnp.dot(table, sender_weight, preferred_element_type=jnp.float32).astype(jnp.bfloat16)
        receiver_proj = jnp.dot(base, receiver_weight, preferred_element_type=jnp.float32)
        rows = table_rows(senders, slots, G_DEV, XR)
        table_grad, unused_grad = edge_backward(sender_proj, receiver_proj, message_weight, rows, receivers, live_blocks, summed_grad, False)
        table_grad_b = table_grad.astype(jnp.bfloat16)
        copy_grad = back_dot(table_grad_b, sender_weight)
        return (cross_dot(table, table_grad_b), copy_grad[:G_DEV], copy_grad[G_DEV:])
    sender_terms, own_grads, grid_backs = lax.map(encode_back_tile, (hidden_all, grid_copies, mesh_tiles, enc_senders, enc_slots, enc_receivers, encode_live, state_grads, mesh_came, mesh_picks, encode_sums))
    grid_came = returned(grid_backs, XR)

    def embed_back_tile(operands):
        grid_rows, picks, own_grad, came = operands
        pre_own = jnp.dot(grid_rows, grid_weight, preferred_element_type=jnp.float32)
        own_term = cross_dot(grid_rows, (own_grad * silu_slope(pre_own)).astype(jnp.bfloat16))
        export_pre = jnp.tile(jnp.take(pre_own, picks, axis=0), (9, 1))
        export_rows = jnp.tile(jnp.take(grid_rows, picks, axis=0), (9, 1))
        return own_term + cross_dot(export_rows, (came * silu_slope(export_pre)).astype(jnp.bfloat16))
    grid_terms = lax.map(embed_back_tile, (grid_tiles, grid_picks, own_grads, grid_came))
    mesh_out = outputs.reshape(tiles * M_DEV, LATENT)
    return (mesh_out, lax.optimization_barrier(jnp.sum(grid_terms, axis=0)), lax.optimization_barrier(jnp.sum(sender_terms, axis=0)), lax.optimization_barrier(jnp.sum(edge_terms, axis=0)))
```

```python
import jax
import jax.numpy as jnp
from jax import lax
from jax.experimental import pallas as pl
from jax.experimental.pallas import tpu as pltpu
from jax.sharding import PartitionSpec as P

norm_epsilon = 1e-05
blocks_per_turn = 4
lanes = 128
f32 = jnp.float32
bf16 = jnp.bfloat16


def dot(left, right):
    return jnp.dot(left, right, preferred_element_type=f32)


def back_dot(left, weight):
    return lax.dot_general(left, weight, (((1,), (1,)), ((), ())), preferred_element_type=f32)


def cross_dot(left, right):
    return lax.dot_general(left, right, (((0,), (0,)), ((), ())), preferred_element_type=f32)


def sigmoid(values):
    return 0.5 * jnp.tanh(0.5 * values) + 0.5


def row_mean(values):
    return jnp.mean(values, axis=-1, keepdims=True)


def normalise(values):
    center = values - row_mean(values)
    scale = lax.rsqrt(row_mean(center * center) + norm_epsilon)
    return center * scale, scale


def norm_back(normed, scale, upstream):
    inner = row_mean(upstream * normed)
    return scale * (upstream - row_mean(upstream) - normed * inner)


def lane_hot(row, width):
    spread = jnp.transpose(jnp.broadcast_to(row.astype(f32), (lanes, lanes)))
    column = lax.broadcasted_iota(jnp.int32, (lanes, lanes), 1).astype(f32)
    parts = [
        jnp.where(spread == column + float(start), 1.0, 0.0).astype(bf16)
        for start in range(0, width, lanes)
    ]
    return jnp.concatenate(parts, 1)


def row_hot(row, count):
    index = lax.broadcasted_iota(jnp.int32, (count, lanes), 0)
    return jnp.where(index == row, 1.0, 0.0).astype(bf16)


def live_row(rows, block, live):
    return jnp.where(block < live, rows[pl.ds(block, 1), :], -1)


def window(slots, block, own_rows, copy_rows):
    slot = slots[block]
    return pl.multiple_of(jnp.where(slot == 4, 0, own_rows + slot * copy_rows), lanes)


def encode_kernel(
    live_ref,
    slots,
    grid_own,
    grid_near,
    base,
    senders,
    receivers,
    export,
    grid_weight,
    sender_weight,
    receiver_weight,
    message_weight,
    update_weight,
    gain,
    state,
    picked,
    inputs,
    hidden,
    pre_slope,
    mix_slope,
    normed_out,
    scale_out,
    update_normed,
    update_scale,
    table,
    projected,
    total,
):
    own, copies = grid_own.shape[0], grid_near.shape[0]
    nodes = base.shape[0]
    live = live_ref[0]
    table[0:own, :] = grid_own[...]
    table[own : own + copies, :] = grid_near[...]
    table[own + copies :, :] = jnp.zeros_like(table[own + copies :, :])
    projected[0:nodes, :] = dot(base[...], receiver_weight[...]).astype(bf16)
    projected[nodes:, :] = jnp.zeros_like(projected[nodes:, :])
    total[...] = jnp.zeros_like(total)
    turn_rows = blocks_per_turn * lanes

    def turn(step, carry):
        gathered, received, placed = [], [], []
        for part in range(blocks_per_turn):
            block = step * blocks_per_turn + part
            start = window(slots, block, own, lanes)
            pick = lane_hot(senders[pl.ds(block, 1), :], own)
            gathered.append(dot(pick, table[pl.ds(start, own), :]).astype(bf16))
            ends = live_row(receivers, block, live)
            received.append(lane_hot(ends, projected.shape[0]))
            placed.append(row_hot(ends, nodes))
        here = pl.ds(pl.multiple_of(step * turn_rows, turn_rows), turn_rows)
        rows = jnp.concatenate(gathered, 0)
        inputs[here, :] = rows
        pre = dot(rows, grid_weight[...])
        gate = sigmoid(pre)
        pre_slope[here, :] = (gate * (1.0 + pre * (1.0 - gate))).astype(bf16)
        embedded = (pre * gate).astype(bf16)
        hidden[here, :] = embedded
        sent = dot(embedded, sender_weight[...]).astype(bf16).astype(f32)
        mix = sent + dot(jnp.concatenate(received, 0), projected[...])
        gate = sigmoid(mix)
        mix_slope[here, :] = (gate * (1.0 + mix * (1.0 - gate))).astype(bf16)
        product = dot((mix * gate).astype(bf16), message_weight[...])
        normed, scale = normalise(product)
        normed = normed.astype(bf16)
        normed_out[here, :] = normed
        scale_out[here, :] = jnp.broadcast_to(scale, (turn_rows, lanes))
        total[...] += dot(jnp.concatenate(placed, 1), normed)
        return carry

    lax.fori_loop(0, senders.shape[0] // blocks_per_turn, turn, 0)
    update = dot(total[...].astype(bf16), update_weight[...])
    normed, scale = normalise(update)
    update_normed[...] = normed
    update_scale[...] = jnp.broadcast_to(scale, update_scale.shape)
    new_state = (base[...].astype(f32) + normed * gain[...]).astype(bf16)
    state[...] = new_state
    padded_state = jnp.concatenate(
        [new_state, jnp.zeros((256 - nodes, new_state.shape[1]), bf16)], 0
    )
    picked[...] = dot(lane_hot(export[...], 256), padded_state).astype(bf16)


def process_kernel(
    live_ref,
    slots,
    state,
    near,
    senders,
    receivers,
    edge_sender,
    edge_receiver,
    edge_message,
    node_update,
    gain,
    cotangent,
    mesh_out,
    own_grad,
    leaving,
    sender_rows,
    mix_grad_out,
    receiver_grad,
    table,
    terms,
    total,
    slope,
    normed_all,
    scale_all,
    upstream,
    table_grad,
    receiver_total,
):
    nodes, copies = state.shape[0], near.shape[0]
    reach = 256
    live = live_ref[0]
    table[0:nodes, :] = state[...]
    table[nodes:reach, :] = jnp.zeros_like(table[nodes:reach, :])
    table[reach : reach + copies, :] = near[...]
    table[reach + copies :, :] = jnp.zeros_like(table[reach + copies :, :])
    terms[0:nodes, :] = dot(state[...], edge_receiver[...]).astype(bf16)
    terms[nodes:, :] = jnp.zeros_like(terms[nodes:, :])
    total[...] = jnp.zeros_like(total)
    turn_rows = blocks_per_turn * lanes
    turns = senders.shape[0] // blocks_per_turn

    def forward(step, carry):
        gathered, received, placed = [], [], []
        for part in range(blocks_per_turn):
            block = step * blocks_per_turn + part
            start = window(slots, block, reach, lanes)
            pick = lane_hot(senders[pl.ds(block, 1), :], reach)
            gathered.append(dot(pick, table[pl.ds(start, reach), :]).astype(bf16))
            ends = live_row(receivers, block, live)
            received.append(lane_hot(ends, reach))
            placed.append(row_hot(ends, nodes))
        here = pl.ds(pl.multiple_of(step * turn_rows, turn_rows), turn_rows)
        rows = jnp.concatenate(gathered, 0)
        sender_rows[here, :] = rows
        sent = dot(rows, edge_sender[...]).astype(bf16).astype(f32)
        mix = sent + dot(jnp.concatenate(received, 0), terms[...])
        gate = sigmoid(mix)
        slope[here, :] = gate * (1.0 + mix * (1.0 - gate))
        product = dot((mix * gate).astype(bf16), edge_message[...])
        normed, scale = normalise(product)
        normed_all[here, :] = normed
        scale_all[here, :] = jnp.broadcast_to(scale, (turn_rows, lanes))
        total[...] += dot(jnp.concatenate(placed, 1), normed.astype(bf16))
        return carry

    lax.fori_loop(0, turns, forward, 0)
    update = dot(total[...].astype(bf16), node_update[...])
    normed, scale = normalise(update)
    mesh_out[...] = (state[...].astype(f32) + normed * gain[...]).astype(bf16)
    update_grad = norm_back(normed, scale, cotangent[...].astype(f32) * gain[...])
    upstream[0:nodes, :] = back_dot(update_grad.astype(bf16), node_update[...]).astype(bf16)
    upstream[nodes:, :] = jnp.zeros_like(upstream[nodes:, :])
    table_grad[...] = jnp.zeros_like(table_grad)
    receiver_total[...] = jnp.zeros_like(receiver_total)

    def backward(step, carry):
        received, placed = [], []
        for part in range(blocks_per_turn):
            ends = live_row(receivers, step * blocks_per_turn + part, live)
            received.append(lane_hot(ends, reach))
            placed.append(row_hot(ends, nodes))
        here = pl.ds(pl.multiple_of(step * turn_rows, turn_rows), turn_rows)
        arriving = dot(jnp.concatenate(received, 0), upstream[...])
        product_grad = norm_back(normed_all[here, :], scale_all[here, 0:1], arriving)
        mix_grad = back_dot(product_grad.astype(bf16), edge_message[...]) * slope[here, :]
        mix_grad = mix_grad.astype(bf16)
        mix_grad_out[here, :] = mix_grad
        receiver_total[...] += dot(jnp.concatenate(placed, 1), mix_grad)
        for part in range(blocks_per_turn):
            block = step * blocks_per_turn + part
            start = window(slots, block, reach, lanes)
            place = row_hot(senders[pl.ds(block, 1), :], nodes)
            table_grad[pl.ds(start, nodes), :] += dot(
                place, mix_grad[part * lanes : (part + 1) * lanes, :]
            )
        return carry

    lax.fori_loop(0, turns, backward, 0)
    own_grad[...] = table_grad[0:nodes, :]
    leaving[...] = table_grad[reach : reach + copies, :].astype(bf16)
    receiver_grad[...] = receiver_total[...].astype(bf16)


def encode_back_kernel(
    live_ref,
    receivers,
    export,
    state_part,
    own_grad,
    kept,
    from_left,
    from_right,
    edge_sender,
    update_normed,
    update_scale,
    gain,
    update_weight,
    normed_all,
    scale_all,
    mix_slope,
    pre_slope,
    message_weight,
    sender_weight,
    mix_grad_out,
    pre_grad_out,
    upstream,
):
    nodes = state_part.shape[0]
    live = live_ref[0]
    arrived = kept[...].astype(f32) + from_left[...].astype(f32) + from_right[...].astype(f32)
    table_grad = own_grad[...] + dot(row_hot(export[...], nodes), arrived.astype(bf16))
    state_grad = state_part[...] + back_dot(table_grad.astype(bf16), edge_sender[...])
    update_grad = norm_back(update_normed[...], update_scale[:, 0:1], state_grad * gain[...])
    upstream[0:nodes, :] = back_dot(update_grad.astype(bf16), update_weight[...]).astype(bf16)
    upstream[nodes:, :] = jnp.zeros_like(upstream[nodes:, :])
    turn_rows = blocks_per_turn * lanes

    def turn(step, carry):
        received = [
            lane_hot(live_row(receivers, step * blocks_per_turn + part, live), upstream.shape[0])
            for part in range(blocks_per_turn)
        ]
        here = pl.ds(pl.multiple_of(step * turn_rows, turn_rows), turn_rows)
        arriving = dot(jnp.concatenate(received, 0), upstream[...])
        product_grad = norm_back(
            normed_all[here, :].astype(f32), scale_all[here, 0:1], arriving
        ).astype(bf16)
        mix_grad = back_dot(product_grad, message_weight[...]) * mix_slope[here, :].astype(f32)
        mix_grad = mix_grad.astype(bf16)
        mix_grad_out[here, :] = mix_grad
        pre_grad = back_dot(mix_grad, sender_weight[...]) * pre_slope[here, :].astype(f32)
        pre_grad_out[here, :] = pre_grad.astype(bf16)
        return carry

    lax.fori_loop(0, receivers.shape[0] // blocks_per_turn, turn, 0)


def call(kernel, operands, outs, scratch, scalars=1, flops=0):
    smem = pl.BlockSpec(memory_space=pltpu.SMEM)
    vmem = pl.BlockSpec(memory_space=pltpu.VMEM)
    return pl.pallas_call(
        kernel,
        out_shape=[jax.ShapeDtypeStruct(shape, dtype) for shape, dtype in outs],
        in_specs=[smem] * scalars + [vmem] * (len(operands) - scalars),
        out_specs=[vmem] * len(outs),
        scratch_shapes=[pltpu.VMEM(shape, dtype) for shape, dtype in scratch],
        compiler_params=pltpu.CompilerParams(vmem_limit_bytes=40 * 1024 * 1024),
        cost_estimate=pl.CostEstimate(flops=flops, bytes_accessed=8 << 20, transcendentals=0),
    )(*operands)


def shifted(x, axis, step):
    size = lax.axis_size(axis)
    if axis == "lon":
        pairs = [(i, (i + step) % size) for i in range(size)]
    else:
        pairs = [(i, i + step) for i in range(size) if 0 <= i + step < size]
    return lax.ppermute(x, axis, pairs)


def around(rows):
    for axis in ("lat", "lon"):
        before, after = shifted(rows, axis, 1), shifted(rows, axis, -1)
        dim = 0 if axis == "lat" else 1
        rows = jnp.stack([before, rows, after], dim)
    return rows.reshape(9 * rows.shape[2], rows.shape[3])


def partner(x, axis, flip):
    return lax.ppermute(x, axis, [(i, i ^ flip) for i in range(lax.axis_size(axis))])


def add(left, right):
    return (left.astype(f32) + right.astype(f32)).astype(bf16)


halving = (("lat", 1, 0), ("lat", 2, 1), ("lat", 6, 2))
doubling = (("lon", 1), ("lon", 3), ("lon", 4), ("lon", 12))


def summed(values):
    index = lax.axis_index("lat")
    bits = (index & 1, ((index >> 1) ^ (index >> 2)) & 1, (index >> 2) & 1)
    for axis, flip, bit in halving:
        half = values.shape[0] // 2
        mine = lax.dynamic_slice_in_dim(values, bits[bit] * half, half, 0)
        other = lax.dynamic_slice_in_dim(values, (1 - bits[bit]) * half, half, 0)
        values = add(mine, partner(other, axis, flip))
    for axis, flip in doubling:
        values = add(values, partner(values, axis, flip))
    for axis, flip, bit in halving[::-1]:
        got = partner(values, axis, flip)
        low = bits[bit] == 0
        values = jnp.concatenate([jnp.where(low, values, got), jnp.where(low, got, values)], 0)
    return values


def local(
    grid_in,
    grid_export,
    mesh_init,
    encode_senders,
    encode_slots,
    encode_receivers,
    encode_live,
    mesh_export,
    process_senders,
    process_slots,
    process_receivers,
    process_live,
    grid_weight,
    sender_weight,
    receiver_weight,
    message_weight,
    update_weight,
    encode_gain,
    edge_sender,
    edge_receiver,
    edge_message,
    node_update,
    node_gain,
    cotangent,
):
    grid_count, variables = grid_in.shape
    nodes, width = mesh_init.shape
    copies = mesh_export.shape[0]
    edges = encode_senders.shape[0] * encode_senders.shape[1]
    depth = 256
    grid_rows = jnp.pad(grid_in, ((0, 0), (0, depth - variables)))
    select = (grid_export[:, None] == jnp.arange(grid_count)[None, :]).astype(bf16)
    grid_near = around(dot(select, grid_rows).astype(bf16))
    grid_weight = jnp.pad(grid_weight, ((0, depth - variables), (0, 0)))
    export = mesh_export[None]
    encode_gain, node_gain = encode_gain[None], node_gain[None]
    (
        state,
        picked,
        inputs,
        hidden,
        pre_slope,
        mix_slope,
        normed,
        scale,
        update_normed,
        update_scale,
    ) = call(
        encode_kernel,
        (
            encode_live,
            encode_slots,
            grid_rows,
            grid_near,
            mesh_init,
            encode_senders,
            encode_receivers,
            export,
            grid_weight,
            sender_weight,
            receiver_weight,
            message_weight,
            update_weight,
            encode_gain,
        ),
        [
            ((nodes, width), bf16),
            ((copies, width), bf16),
            ((edges, depth), bf16),
            ((edges, width), bf16),
            ((edges, width), bf16),
            ((edges, width), bf16),
            ((edges, width), bf16),
            ((edges, lanes), f32),
            ((nodes, width), f32),
            ((nodes, lanes), f32),
        ],
        [
            ((grid_count + 9 * lanes + grid_count - lanes, depth), bf16),
            ((256, width), bf16),
            ((nodes, width), f32),
        ],
        scalars=2,
    )
    near = around(picked)
    mesh_out, own_grad, leaving, sender_rows, mix_grad, receiver_grad = call(
        process_kernel,
        (
            process_live,
            process_slots,
            state,
            near,
            process_senders,
            process_receivers,
            edge_sender,
            edge_receiver,
            edge_message,
            node_update,
            node_gain,
            cotangent,
        ),
        [
            ((nodes, width), bf16),
            ((nodes, width), f32),
            ((9 * copies, width), bf16),
            ((edges, width), bf16),
            ((edges, width), bf16),
            ((nodes, width), bf16),
        ],
        [
            ((256 + 9 * copies + 128, width), bf16),
            ((256, width), bf16),
            ((nodes, width), f32),
            ((edges, width), f32),
            ((edges, width), f32),
            ((edges, lanes), f32),
            ((256, width), bf16),
            ((256 + 9 * copies + 128, width), f32),
            ((nodes, width), f32),
        ],
        scalars=2,
    )
    leaving = leaving.reshape(3, 3 * copies, width)
    from_above = shifted(leaving[0], "lat", -1)
    from_below = shifted(leaving[2], "lat", 1)
    columns = (
        leaving[1].astype(f32) + from_above.astype(f32) + from_below.astype(f32)
    ).astype(bf16).reshape(3, copies, width)
    from_right = shifted(columns[0], "lon", -1)
    from_left = shifted(columns[2], "lon", 1)
    state_part = cotangent.astype(f32) + back_dot(receiver_grad, edge_receiver)
    edge_grad = cross_dot(sender_rows, mix_grad).astype(bf16)
    mix_grad, pre_grad = call(
        encode_back_kernel,
        (
            encode_live,
            encode_receivers,
            export,
            state_part,
            own_grad,
            columns[1],
            from_left,
            from_right,
            edge_sender,
            update_normed,
            update_scale,
            encode_gain,
            update_weight,
            normed,
            scale,
            mix_slope,
            pre_slope,
            message_weight,
            sender_weight,
        ),
        [((edges, width), bf16), ((edges, width), bf16)],
        [((256, width), bf16)],
    )
    sender_grad = cross_dot(hidden, mix_grad).astype(bf16)
    grid_grad = cross_dot(inputs, pre_grad).astype(bf16)
    totals = summed(jnp.concatenate([sender_grad, edge_grad, grid_grad], 0)).astype(f32)
    return (
        mesh_out,
        totals[2 * width : 2 * width + variables],
        totals[:width],
        totals[width : 2 * width],
    )


def solution(mesh):
    tiles, shared = P(("lat", "lon")), P()
    wide = P(("lat", "lon"), None)
    return jax.shard_map(
        local,
        mesh=mesh,
        in_specs=(
            (wide, tiles, wide, wide, tiles, wide, tiles, tiles, wide, tiles, wide, tiles)
            + (shared,) * 11
            + (wide,)
        ),
        out_specs=(wide, shared, shared, shared),
        check_vma=False,
    )
```

```python
import jax
import jax.numpy as jnp
from jax import lax
from jax.experimental import pallas as pl
from jax.experimental.pallas import tpu as pltpu
from jax.sharding import PartitionSpec as P

norm_epsilon = 1e-05
blocks_per_turn = 4
lanes = 128
f32 = jnp.float32
bf16 = jnp.bfloat16


def dot(left, right):
    return jnp.dot(left, right, preferred_element_type=f32)


def back_dot(left, weight):
    return lax.dot_general(left, weight, (((1,), (1,)), ((), ())), preferred_element_type=f32)


def cross_dot(left, right):
    return lax.dot_general(left, right, (((0,), (0,)), ((), ())), preferred_element_type=f32)


def sigmoid(values):
    return 0.5 * jnp.tanh(0.5 * values) + 0.5


def row_mean(values):
    return jnp.mean(values, axis=-1, keepdims=True)


def normalise(values):
    center = values - row_mean(values)
    scale = lax.rsqrt(row_mean(center * center) + norm_epsilon)
    return center * scale, scale


def norm_back(normed, scale, upstream):
    inner = row_mean(upstream * normed)
    return scale * (upstream - row_mean(upstream) - normed * inner)


def lane_hot(row, width):
    spread = jnp.transpose(jnp.broadcast_to(row.astype(f32), (lanes, lanes)))
    column = lax.broadcasted_iota(jnp.int32, (lanes, lanes), 1).astype(f32)
    parts = [
        jnp.where(spread == column + float(start), 1.0, 0.0).astype(bf16)
        for start in range(0, width, lanes)
    ]
    return jnp.concatenate(parts, 1)


def row_hot(row, count):
    index = lax.broadcasted_iota(jnp.int32, (count, lanes), 0)
    return jnp.where(index == row, 1.0, 0.0).astype(bf16)


def live_row(rows, block, live):
    return jnp.where(block < live, rows[pl.ds(block, 1), :], -1)


def window(starts, block):
    return pl.multiple_of(starts[block], lanes)


def fill(table, own, near):
    table[0 : own.shape[0], :] = own[...]
    first = own.shape[0] + -own.shape[0] % lanes
    if first > own.shape[0]:
        table[own.shape[0] : first, :] = jnp.zeros_like(table[own.shape[0] : first, :])
    for part in near:
        table[first : first + part.shape[0], :] = part[...]
        first += part.shape[0]
    table[first:, :] = jnp.zeros_like(table[first:, :])


def encode_kernel(
    live_ref,
    starts,
    grid_own,
    near_left,
    near_right,
    near_inner,
    near_inner_corners,
    near_outer,
    near_outer_corners,
    base,
    senders,
    receivers,
    export,
    grid_weight,
    sender_weight,
    receiver_weight,
    message_weight,
    update_weight,
    gain,
    state,
    picked,
    inputs,
    hidden,
    pre_slope,
    mix_slope,
    normed_out,
    scale_out,
    update_normed,
    update_scale,
    table,
    projected,
    total,
):
    own = grid_own.shape[0]
    nodes = base.shape[0]
    live = live_ref[0]
    fill(
        table,
        grid_own,
        (near_left, near_right, near_inner, near_inner_corners, near_outer, near_outer_corners),
    )
    projected[0:nodes, :] = dot(base[...], receiver_weight[...]).astype(bf16)
    projected[nodes:, :] = jnp.zeros_like(projected[nodes:, :])
    total[...] = jnp.zeros_like(total)
    turn_rows = blocks_per_turn * lanes

    def turn(step, carry):
        gathered, received, placed = [], [], []
        for part in range(blocks_per_turn):
            block = step * blocks_per_turn + part
            start = window(starts, block)
            pick = lane_hot(senders[pl.ds(block, 1), :], own)
            gathered.append(dot(pick, table[pl.ds(start, own), :]).astype(bf16))
            ends = live_row(receivers, block, live)
            received.append(lane_hot(ends, projected.shape[0]))
            placed.append(row_hot(ends, nodes))
        here = pl.ds(pl.multiple_of(step * turn_rows, turn_rows), turn_rows)
        rows = jnp.concatenate(gathered, 0)
        inputs[here, :] = rows
        pre = dot(rows, grid_weight[...])
        gate = sigmoid(pre)
        pre_slope[here, :] = (gate * (1.0 + pre * (1.0 - gate))).astype(bf16)
        embedded = (pre * gate).astype(bf16)
        hidden[here, :] = embedded
        sent = dot(embedded, sender_weight[...]).astype(bf16).astype(f32)
        mix = sent + dot(jnp.concatenate(received, 0), projected[...])
        gate = sigmoid(mix)
        mix_slope[here, :] = (gate * (1.0 + mix * (1.0 - gate))).astype(bf16)
        product = dot((mix * gate).astype(bf16), message_weight[...])
        normed, scale = normalise(product)
        normed = normed.astype(bf16)
        normed_out[here, :] = normed
        scale_out[here, :] = jnp.broadcast_to(scale, (turn_rows, lanes))
        total[...] += dot(jnp.concatenate(placed, 1), normed)
        return carry

    lax.fori_loop(0, senders.shape[0] // blocks_per_turn, turn, 0)
    update = dot(total[...].astype(bf16), update_weight[...])
    normed, scale = normalise(update)
    update_normed[...] = normed
    update_scale[...] = jnp.broadcast_to(scale, update_scale.shape)
    new_state = (base[...].astype(f32) + normed * gain[...]).astype(bf16)
    state[...] = new_state
    padded_state = jnp.concatenate(
        [new_state, jnp.zeros((256 - nodes, new_state.shape[1]), bf16)], 0
    )
    picked[...] = dot(lane_hot(export[...], 256), padded_state).astype(bf16)


def process_kernel(
    live_ref,
    starts,
    state,
    near_left,
    near_right,
    near_inner,
    near_inner_corners,
    near_outer,
    near_outer_corners,
    senders,
    receivers,
    edge_sender,
    edge_receiver,
    edge_message,
    node_update,
    gain,
    cotangent,
    mesh_out,
    own_grad,
    to_lon,
    to_inner,
    to_outer,
    sender_rows,
    mix_grad_out,
    receiver_grad,
    table,
    terms,
    total,
    slope,
    normed_all,
    scale_all,
    upstream,
    table_grad,
    receiver_total,
):
    nodes = state.shape[0]
    reach = 256
    live = live_ref[0]
    fill(
        table,
        state,
        (near_left, near_right, near_inner, near_inner_corners, near_outer, near_outer_corners),
    )
    terms[0:nodes, :] = dot(state[...], edge_receiver[...]).astype(bf16)
    terms[nodes:, :] = jnp.zeros_like(terms[nodes:, :])
    total[...] = jnp.zeros_like(total)
    turn_rows = blocks_per_turn * lanes
    turns = senders.shape[0] // blocks_per_turn

    def forward(step, carry):
        gathered, received, placed = [], [], []
        for part in range(blocks_per_turn):
            block = step * blocks_per_turn + part
            start = window(starts, block)
            pick = lane_hot(senders[pl.ds(block, 1), :], reach)
            gathered.append(dot(pick, table[pl.ds(start, reach), :]).astype(bf16))
            ends = live_row(receivers, block, live)
            received.append(lane_hot(ends, reach))
            placed.append(row_hot(ends, nodes))
        here = pl.ds(pl.multiple_of(step * turn_rows, turn_rows), turn_rows)
        rows = jnp.concatenate(gathered, 0)
        sender_rows[here, :] = rows
        sent = dot(rows, edge_sender[...]).astype(bf16).astype(f32)
        mix = sent + dot(jnp.concatenate(received, 0), terms[...])
        gate = sigmoid(mix)
        slope[here, :] = gate * (1.0 + mix * (1.0 - gate))
        product = dot((mix * gate).astype(bf16), edge_message[...])
        normed, scale = normalise(product)
        normed_all[here, :] = normed
        scale_all[here, :] = jnp.broadcast_to(scale, (turn_rows, lanes))
        total[...] += dot(jnp.concatenate(placed, 1), normed.astype(bf16))
        return carry

    lax.fori_loop(0, turns, forward, 0)
    update = dot(total[...].astype(bf16), node_update[...])
    normed, scale = normalise(update)
    mesh_out[...] = (state[...].astype(f32) + normed * gain[...]).astype(bf16)
    update_grad = norm_back(normed, scale, cotangent[...].astype(f32) * gain[...])
    upstream[0:nodes, :] = back_dot(update_grad.astype(bf16), node_update[...]).astype(bf16)
    upstream[nodes:, :] = jnp.zeros_like(upstream[nodes:, :])
    table_grad[...] = jnp.zeros_like(table_grad)
    receiver_total[...] = jnp.zeros_like(receiver_total)

    def backward(step, carry):
        received, placed = [], []
        for part in range(blocks_per_turn):
            ends = live_row(receivers, step * blocks_per_turn + part, live)
            received.append(lane_hot(ends, reach))
            placed.append(row_hot(ends, nodes))
        here = pl.ds(pl.multiple_of(step * turn_rows, turn_rows), turn_rows)
        arriving = dot(jnp.concatenate(received, 0), upstream[...])
        product_grad = norm_back(normed_all[here, :], scale_all[here, 0:1], arriving)
        mix_grad = back_dot(product_grad.astype(bf16), edge_message[...]) * slope[here, :]
        mix_grad = mix_grad.astype(bf16)
        mix_grad_out[here, :] = mix_grad
        receiver_total[...] += dot(jnp.concatenate(placed, 1), mix_grad)
        for part in range(blocks_per_turn):
            block = step * blocks_per_turn + part
            start = window(starts, block)
            place = row_hot(senders[pl.ds(block, 1), :], nodes)
            table_grad[pl.ds(start, nodes), :] += dot(
                place, mix_grad[part * lanes : (part + 1) * lanes, :]
            )
        return carry

    lax.fori_loop(0, turns, backward, 0)
    own_grad[...] = table_grad[0:nodes, :]
    first = reach
    for part in (to_lon, to_inner, to_outer):
        part[...] = table_grad[first : first + part.shape[0], :].astype(bf16)
        first += part.shape[0]
    receiver_grad[...] = receiver_total[...].astype(bf16)


def encode_back_kernel(
    live_ref,
    receivers,
    export,
    state_part,
    own_grad,
    from_inner,
    from_outer,
    from_left,
    from_right,
    edge_sender,
    update_normed,
    update_scale,
    gain,
    update_weight,
    normed_all,
    scale_all,
    mix_slope,
    pre_slope,
    message_weight,
    sender_weight,
    mix_grad_out,
    pre_grad_out,
    upstream,
):
    nodes = state_part.shape[0]
    live = live_ref[0]
    arrived = from_left[...].astype(f32) + from_right[...].astype(f32)
    copies = arrived.shape[0]
    arrived += from_inner[0:copies, :].astype(f32) + from_outer[0:copies, :].astype(f32)
    table_grad = own_grad[...] + dot(row_hot(export[...], nodes), arrived.astype(bf16))
    state_grad = state_part[...] + back_dot(table_grad.astype(bf16), edge_sender[...])
    update_grad = norm_back(update_normed[...], update_scale[:, 0:1], state_grad * gain[...])
    upstream[0:nodes, :] = back_dot(update_grad.astype(bf16), update_weight[...]).astype(bf16)
    upstream[nodes:, :] = jnp.zeros_like(upstream[nodes:, :])
    turn_rows = blocks_per_turn * lanes

    def turn(step, carry):
        received = [
            lane_hot(live_row(receivers, step * blocks_per_turn + part, live), upstream.shape[0])
            for part in range(blocks_per_turn)
        ]
        here = pl.ds(pl.multiple_of(step * turn_rows, turn_rows), turn_rows)
        arriving = dot(jnp.concatenate(received, 0), upstream[...])
        product_grad = norm_back(
            normed_all[here, :].astype(f32), scale_all[here, 0:1], arriving
        ).astype(bf16)
        mix_grad = back_dot(product_grad, message_weight[...]) * mix_slope[here, :].astype(f32)
        mix_grad = mix_grad.astype(bf16)
        mix_grad_out[here, :] = mix_grad
        pre_grad = back_dot(mix_grad, sender_weight[...]) * pre_slope[here, :].astype(f32)
        pre_grad_out[here, :] = pre_grad.astype(bf16)
        return carry

    lax.fori_loop(0, receivers.shape[0] // blocks_per_turn, turn, 0)


def call(kernel, operands, outs, scratch, scalars, mib):
    smem = pl.BlockSpec(memory_space=pltpu.SMEM)
    vmem = pl.BlockSpec(memory_space=pltpu.VMEM)
    return pl.pallas_call(
        kernel,
        out_shape=[jax.ShapeDtypeStruct(shape, dtype) for shape, dtype in outs],
        in_specs=[smem] * scalars + [vmem] * (len(operands) - scalars),
        out_specs=[vmem] * len(outs),
        scratch_shapes=[pltpu.VMEM(shape, dtype) for shape, dtype in scratch],
        compiler_params=pltpu.CompilerParams(vmem_limit_bytes=mib << 20),
        cost_estimate=pl.CostEstimate(flops=4 << 30, bytes_accessed=8 << 20, transcendentals=0),
    )(*operands)


def shifted(x, step):
    size = lax.axis_size("lon")
    return lax.ppermute(x, "lon", [(i, (i + step) % size) for i in range(size)])


def partner(x, axis, flip):
    return lax.ppermute(x, axis, [(i, i ^ flip) for i in range(lax.axis_size(axis))])


def inner(x):
    return partner(x, "lat", 1)


def outer(x):
    ends = range(1, lax.axis_size("lat") - 1, 2)
    return lax.ppermute(x, "lat", [(i, i + 1) for i in ends] + [(i + 1, i) for i in ends])


def around(rows):
    left, right = shifted(rows, 1), shifted(rows, -1)
    corners = jnp.concatenate([left, right], 0)
    return left, right, inner(rows), inner(corners), outer(rows), outer(corners)


even_places = (6, 5, 7, 0, -1, 1, 3, 2, 4)
odd_places = (3, 2, 4, 0, -1, 1, 6, 5, 7)


def start_rows(slots, own):
    places = jnp.where(
        lax.axis_index("lat") % 2 == 0, jnp.array(even_places), jnp.array(odd_places)
    )
    pick = slots[:, None] == jnp.arange(9)[None, :]
    place = jnp.sum(jnp.where(pick, places[None, :], 0), 1).astype(jnp.int32)
    return jnp.where(place < 0, 0, own + lanes * place)


flips = (1, 3, 2)


def total(values):
    own, one, three, two = [part.astype(f32) for part in values]
    return ((own + one) + (two + three)).astype(bf16)


def summed(values):
    index = lax.axis_index("lat")
    core, chip = index & 1, index >> 1
    half = values.shape[0] // 2
    mine = lax.dynamic_slice_in_dim(values, core * half, half, 0)
    other = lax.dynamic_slice_in_dim(values, (1 - core) * half, half, 0)
    values = (mine.astype(f32) + inner(other).astype(f32)).astype(bf16)
    quarter = half // 4
    parts = [
        lax.dynamic_slice_in_dim(values, (chip ^ flip) * quarter, quarter, 0) for flip in (0,) + flips
    ]
    values = total(
        [parts[0]] + [partner(part, "lat", 2 * flip) for part, flip in zip(parts[1:], flips)]
    )
    for scale in (1, 4):
        values = total([values] + [partner(values, "lon", scale * flip) for flip in flips])
    one, three, two = [partner(values, "lat", 2 * flip) for flip in flips]
    low, high = (chip & 1) == 0, chip < 2
    first = jnp.where(low, values, one), jnp.where(low, one, values)
    second = jnp.where(low, two, three), jnp.where(low, three, two)
    values = jnp.concatenate(
        [jnp.where(high, a, b) for a, b in zip(first + second, second + first)], 0
    )
    got = inner(values)
    return jnp.where(core == 0, values, got), jnp.where(core == 0, got, values)


def local(
    grid_in,
    grid_export,
    mesh_init,
    encode_senders,
    encode_slots,
    encode_receivers,
    encode_live,
    mesh_export,
    process_senders,
    process_slots,
    process_receivers,
    process_live,
    grid_weight,
    sender_weight,
    receiver_weight,
    message_weight,
    update_weight,
    encode_gain,
    edge_sender,
    edge_receiver,
    edge_message,
    node_update,
    node_gain,
    cotangent,
):
    grid_count, variables = grid_in.shape
    nodes, width = mesh_init.shape
    copies = mesh_export.shape[0]
    edges = encode_senders.shape[0] * encode_senders.shape[1]
    depth = 256
    grid_rows = jnp.pad(grid_in, ((0, 0), (0, depth - variables)))
    select = (grid_export[:, None] == jnp.arange(grid_count)[None, :]).astype(bf16)
    grid_picked = jnp.pad(dot(select, grid_in).astype(bf16), ((0, 0), (0, depth - variables)))
    grid_near = around(grid_picked)
    grid_weight = jnp.pad(grid_weight, ((0, depth - variables), (0, 0)))
    export = mesh_export[None]
    encode_gain, node_gain = encode_gain[None], node_gain[None]
    (
        state,
        picked,
        inputs,
        hidden,
        pre_slope,
        mix_slope,
        normed,
        scale,
        update_normed,
        update_scale,
    ) = call(
        encode_kernel,
        (
            encode_live,
            start_rows(encode_slots, grid_count),
            grid_rows,
            *grid_near,
            mesh_init,
            encode_senders,
            encode_receivers,
            export,
            grid_weight,
            sender_weight,
            receiver_weight,
            message_weight,
            update_weight,
            encode_gain,
        ),
        [
            ((nodes, width), bf16),
            ((copies, width), bf16),
            ((edges, depth), bf16),
            ((edges, width), bf16),
            ((edges, width), bf16),
            ((edges, width), bf16),
            ((edges, width), bf16),
            ((edges, lanes), f32),
            ((nodes, width), f32),
            ((nodes, lanes), f32),
        ],
        [
            ((grid_count + 8 * lanes + grid_count - lanes, depth), bf16),
            ((256, width), bf16),
            ((nodes, width), f32),
        ],
        2,
        16,
    )
    near = around(picked)
    mesh_out, own_grad, to_lon, to_inner, to_outer, sender_rows, mix_grad, receiver_grad = call(
        process_kernel,
        (
            process_live,
            start_rows(process_slots, 256),
            state,
            *near,
            process_senders,
            process_receivers,
            edge_sender,
            edge_receiver,
            edge_message,
            node_update,
            node_gain,
            cotangent,
        ),
        [
            ((nodes, width), bf16),
            ((nodes, width), f32),
            ((2 * copies, width), bf16),
            ((3 * copies, width), bf16),
            ((3 * copies, width), bf16),
            ((edges, width), bf16),
            ((edges, width), bf16),
            ((nodes, width), bf16),
        ],
        [
            ((256 + 8 * copies + 128, width), bf16),
            ((256, width), bf16),
            ((nodes, width), f32),
            ((edges, width), f32),
            ((edges, width), f32),
            ((edges, lanes), f32),
            ((256, width), bf16),
            ((256 + 8 * copies + 128, width), f32),
            ((nodes, width), f32),
        ],
        2,
        24,
    )
    from_inner, from_outer = inner(to_inner), outer(to_outer)
    to_left, to_right = [
        (
            to_lon[side * copies : (side + 1) * copies].astype(f32)
            + from_inner[(side + 1) * copies : (side + 2) * copies].astype(f32)
            + from_outer[(side + 1) * copies : (side + 2) * copies].astype(f32)
        ).astype(bf16)
        for side in (0, 1)
    ]
    from_right, from_left = shifted(to_left, -1), shifted(to_right, 1)
    state_part = cotangent.astype(f32) + back_dot(receiver_grad, edge_receiver)
    edge_grad = cross_dot(sender_rows, mix_grad).astype(bf16)
    mix_grad, pre_grad = call(
        encode_back_kernel,
        (
            encode_live,
            encode_receivers,
            export,
            state_part,
            own_grad,
            from_inner,
            from_outer,
            from_left,
            from_right,
            edge_sender,
            update_normed,
            update_scale,
            encode_gain,
            update_weight,
            normed,
            scale,
            mix_slope,
            pre_slope,
            message_weight,
            sender_weight,
        ),
        [((edges, width), bf16), ((edges, width), bf16)],
        [((256, width), bf16)],
        1,
        12,
    )
    sender_grad = cross_dot(hidden, mix_grad).astype(bf16)
    grid_grad = cross_dot(inputs, pre_grad).astype(bf16)
    halves = summed(jnp.concatenate([sender_grad, edge_grad, grid_grad], 0))
    totals = jnp.concatenate(halves, 0).astype(f32)
    return (
        mesh_out,
        totals[2 * width : 2 * width + variables],
        totals[:width],
        totals[width : 2 * width],
    )


def solution(mesh):
    tiles, shared = P(("lat", "lon")), P()
    wide = P(("lat", "lon"), None)
    return jax.shard_map(
        local,
        mesh=mesh,
        in_specs=(
            (wide, tiles, wide, wide, tiles, wide, tiles, tiles, wide, tiles, wide, tiles)
            + (shared,) * 11
            + (wide,)
        ),
        out_specs=(wide, shared, shared, shared),
        check_vma=False,
    )
```

```python
import jax
import jax.numpy as jnp
from jax import lax
from jax.experimental import pallas as pl
from jax.experimental.pallas import tpu as pltpu
from jax.sharding import PartitionSpec as P

norm_epsilon = 1e-05
blocks_per_turn = 4
lanes = 128
f32 = jnp.float32
bf16 = jnp.bfloat16


def dot(left, right):
    return jnp.dot(left, right, preferred_element_type=f32)


def back_dot(left, weight):
    return lax.dot_general(left, weight, (((1,), (1,)), ((), ())), preferred_element_type=f32)


def cross_dot(left, right):
    return lax.dot_general(left, right, (((0,), (0,)), ((), ())), preferred_element_type=f32)


def sigmoid(values):
    return 0.5 * jnp.tanh(0.5 * values) + 0.5


def row_mean(values):
    return jnp.mean(values, axis=-1, keepdims=True)


def normalise(values):
    center = values - row_mean(values)
    scale = lax.rsqrt(row_mean(center * center) + norm_epsilon)
    return center * scale, scale


def norm_back(normed, scale, upstream):
    inner = row_mean(upstream * normed)
    return scale * (upstream - row_mean(upstream) - normed * inner)


def lane_hot(row, width):
    spread = jnp.transpose(jnp.broadcast_to(row.astype(f32), (lanes, lanes)))
    column = lax.broadcasted_iota(jnp.int32, (lanes, lanes), 1).astype(f32)
    parts = [
        jnp.where(spread == column + float(start), 1.0, 0.0).astype(bf16)
        for start in range(0, width, lanes)
    ]
    return jnp.concatenate(parts, 1)


def row_hot(row, count):
    index = lax.broadcasted_iota(jnp.int32, (count, lanes), 0)
    return jnp.where(index == row, 1.0, 0.0).astype(bf16)


def live_row(rows, block, live):
    return jnp.where(block < live, rows[pl.ds(block, 1), :], -1)


def window(slots, block, own_rows, core):
    slot = slots[block]
    band = jnp.where(slot >= 6, 2, jnp.where(slot >= 3, 1, 0))
    sector = slot - 3 * band
    side = jnp.where(sector == 1, 0, jnp.where(sector == 0, 1, 2))
    inside = (band == 2) == (core == 0)
    place = jnp.where(band == 1, jnp.where(sector == 0, 0, 1), jnp.where(inside, 2, 5) + side)
    return pl.multiple_of(jnp.where(slot == 4, 0, own_rows + lanes * place), lanes)


def fill(table, own, near):
    table[0 : own.shape[0], :] = own[...]
    first = own.shape[0] + -own.shape[0] % lanes
    if first > own.shape[0]:
        table[own.shape[0] : first, :] = jnp.zeros_like(table[own.shape[0] : first, :])
    for part in near:
        table[first : first + part.shape[0], :] = part[...]
        first += part.shape[0]
    table[first:, :] = jnp.zeros_like(table[first:, :])


def send(source, target, sem):
    pltpu.make_async_copy(source, target, sem).start()


def finish(source, target, sem):
    pltpu.make_async_copy(source, target, sem).wait()


def encode_kernel(
    live_ref,
    place_ref,
    slots,
    grid_own,
    near_left,
    near_right,
    near_inner,
    near_inner_corners,
    near_outer,
    near_outer_corners,
    base,
    senders,
    receivers,
    export,
    grid_weight,
    sender_weight,
    receiver_weight,
    message_weight,
    update_weight,
    gain,
    state,
    picked,
    inputs_out,
    hidden_out,
    pre_slope_out,
    mix_slope_out,
    normed_out,
    scale_out,
    update_normed_out,
    update_scale_out,
    table,
    projected,
    total,
    inputs,
    hidden,
    pre_slope,
    mix_slope,
    normed_all,
    scale_all,
    update_normed,
    update_scale,
    sems,
    last_sems,
):
    own = grid_own.shape[0]
    nodes = base.shape[0]
    live, core = live_ref[0], place_ref[0]
    fill(
        table,
        grid_own,
        (near_left, near_right, near_inner, near_inner_corners, near_outer, near_outer_corners),
    )
    projected[0:nodes, :] = dot(base[...], receiver_weight[...]).astype(bf16)
    projected[nodes:, :] = jnp.zeros_like(projected[nodes:, :])
    total[...] = jnp.zeros_like(total)
    turn_rows = blocks_per_turn * lanes
    turns = senders.shape[0] // blocks_per_turn
    saved = (
        (inputs, inputs_out),
        (hidden, hidden_out),
        (pre_slope, pre_slope_out),
        (mix_slope, mix_slope_out),
        (normed_all, normed_out),
        (scale_all, scale_out),
    )

    def turn(step, carry):
        gathered, received, placed = [], [], []
        for part in range(blocks_per_turn):
            block = step * blocks_per_turn + part
            start = window(slots, block, own, core)
            pick = lane_hot(senders[pl.ds(block, 1), :], own)
            gathered.append(dot(pick, table[pl.ds(start, own), :]).astype(bf16))
            ends = live_row(receivers, block, live)
            received.append(lane_hot(ends, projected.shape[0]))
            placed.append(row_hot(ends, nodes))
        here = pl.ds(pl.multiple_of(step * turn_rows, turn_rows), turn_rows)
        rows = jnp.concatenate(gathered, 0)
        inputs[here, :] = rows
        pre = dot(rows, grid_weight[...])
        gate = sigmoid(pre)
        pre_slope[here, :] = (gate * (1.0 + pre * (1.0 - gate))).astype(bf16)
        embedded = (pre * gate).astype(bf16)
        hidden[here, :] = embedded
        sent = dot(embedded, sender_weight[...]).astype(bf16).astype(f32)
        mix = sent + dot(jnp.concatenate(received, 0), projected[...])
        gate = sigmoid(mix)
        mix_slope[here, :] = (gate * (1.0 + mix * (1.0 - gate))).astype(bf16)
        product = dot((mix * gate).astype(bf16), message_weight[...])
        normed, scale = normalise(product)
        normed = normed.astype(bf16)
        normed_all[here, :] = normed
        scale_all[here, :] = jnp.broadcast_to(scale, (turn_rows, lanes))
        total[...] += dot(jnp.concatenate(placed, 1), normed)
        for index, (source, target) in enumerate(saved):
            send(source.at[here, :], target.at[here, :], sems.at[index, step])
        return carry

    lax.fori_loop(0, turns, turn, 0)
    update = dot(total[...].astype(bf16), update_weight[...])
    normed, scale = normalise(update)
    update_normed[...] = normed
    update_scale[...] = jnp.broadcast_to(scale, update_scale.shape)
    send(update_normed, update_normed_out, last_sems.at[0])
    send(update_scale, update_scale_out, last_sems.at[1])
    new_state = (base[...].astype(f32) + normed * gain[...]).astype(bf16)
    state[...] = new_state
    padded_state = jnp.concatenate(
        [new_state, jnp.zeros((256 - nodes, new_state.shape[1]), bf16)], 0
    )
    picked[...] = dot(lane_hot(export[...], 256), padded_state).astype(bf16)
    for step in range(turns):
        here = pl.ds(step * turn_rows, turn_rows)
        for index, (source, target) in enumerate(saved):
            finish(source.at[here, :], target.at[here, :], sems.at[index, step])
    finish(update_normed, update_normed_out, last_sems.at[0])
    finish(update_scale, update_scale_out, last_sems.at[1])


def process_kernel(
    live_ref,
    place_ref,
    slots,
    state,
    near_left,
    near_right,
    near_inner,
    near_inner_corners,
    near_outer,
    near_outer_corners,
    senders,
    receivers,
    edge_sender,
    edge_receiver,
    edge_message,
    node_update,
    gain,
    cotangent,
    mesh_hbm,
    own_grad,
    to_lon,
    to_inner,
    to_outer,
    sender_rows_out,
    mix_grad_out,
    receiver_grad,
    table,
    terms,
    total,
    slope,
    normed_all,
    scale_all,
    upstream,
    table_grad,
    receiver_total,
    mesh_out,
    sender_rows,
    mix_grads,
    sems,
    last_sems,
):
    nodes = state.shape[0]
    reach = 256
    live, core = live_ref[0], place_ref[0]
    fill(
        table,
        state,
        (near_left, near_right, near_inner, near_inner_corners, near_outer, near_outer_corners),
    )
    terms[0:nodes, :] = dot(state[...], edge_receiver[...]).astype(bf16)
    terms[nodes:, :] = jnp.zeros_like(terms[nodes:, :])
    total[...] = jnp.zeros_like(total)
    turn_rows = blocks_per_turn * lanes
    turns = senders.shape[0] // blocks_per_turn

    def forward(step, carry):
        gathered, received, placed = [], [], []
        for part in range(blocks_per_turn):
            block = step * blocks_per_turn + part
            start = window(slots, block, reach, core)
            pick = lane_hot(senders[pl.ds(block, 1), :], reach)
            gathered.append(dot(pick, table[pl.ds(start, reach), :]).astype(bf16))
            ends = live_row(receivers, block, live)
            received.append(lane_hot(ends, reach))
            placed.append(row_hot(ends, nodes))
        here = pl.ds(pl.multiple_of(step * turn_rows, turn_rows), turn_rows)
        rows = jnp.concatenate(gathered, 0)
        sender_rows[here, :] = rows
        sent = dot(rows, edge_sender[...]).astype(bf16).astype(f32)
        mix = sent + dot(jnp.concatenate(received, 0), terms[...])
        gate = sigmoid(mix)
        slope[here, :] = gate * (1.0 + mix * (1.0 - gate))
        product = dot((mix * gate).astype(bf16), edge_message[...])
        normed, scale = normalise(product)
        normed_all[here, :] = normed
        scale_all[here, :] = jnp.broadcast_to(scale, (turn_rows, lanes))
        total[...] += dot(jnp.concatenate(placed, 1), normed.astype(bf16))
        send(sender_rows.at[here, :], sender_rows_out.at[here, :], sems.at[0, step])
        return carry

    lax.fori_loop(0, turns, forward, 0)
    update = dot(total[...].astype(bf16), node_update[...])
    normed, scale = normalise(update)
    mesh_out[...] = (state[...].astype(f32) + normed * gain[...]).astype(bf16)
    send(mesh_out, mesh_hbm, last_sems.at[0])
    update_grad = norm_back(normed, scale, cotangent[...].astype(f32) * gain[...])
    upstream[0:nodes, :] = back_dot(update_grad.astype(bf16), node_update[...]).astype(bf16)
    upstream[nodes:, :] = jnp.zeros_like(upstream[nodes:, :])
    table_grad[...] = jnp.zeros_like(table_grad)
    receiver_total[...] = jnp.zeros_like(receiver_total)

    def backward(step, carry):
        received, placed = [], []
        for part in range(blocks_per_turn):
            ends = live_row(receivers, step * blocks_per_turn + part, live)
            received.append(lane_hot(ends, reach))
            placed.append(row_hot(ends, nodes))
        here = pl.ds(pl.multiple_of(step * turn_rows, turn_rows), turn_rows)
        arriving = dot(jnp.concatenate(received, 0), upstream[...])
        product_grad = norm_back(normed_all[here, :], scale_all[here, 0:1], arriving)
        mix_grad = back_dot(product_grad.astype(bf16), edge_message[...]) * slope[here, :]
        mix_grad = mix_grad.astype(bf16)
        mix_grads[here, :] = mix_grad
        send(mix_grads.at[here, :], mix_grad_out.at[here, :], sems.at[1, step])
        receiver_total[...] += dot(jnp.concatenate(placed, 1), mix_grad)
        for part in range(blocks_per_turn):
            block = step * blocks_per_turn + part
            start = window(slots, block, reach, core)
            place = row_hot(senders[pl.ds(block, 1), :], nodes)
            table_grad[pl.ds(start, nodes), :] += dot(
                place, mix_grad[part * lanes : (part + 1) * lanes, :]
            )
        return carry

    lax.fori_loop(0, turns, backward, 0)
    send(table_grad.at[0:nodes, :], own_grad, last_sems.at[1])
    first = reach
    for part in (to_lon, to_inner, to_outer):
        part[...] = table_grad[first : first + part.shape[0], :].astype(bf16)
        first += part.shape[0]
    receiver_grad[...] = receiver_total[...].astype(bf16)
    for step in range(turns):
        here = pl.ds(step * turn_rows, turn_rows)
        finish(sender_rows.at[here, :], sender_rows_out.at[here, :], sems.at[0, step])
        finish(mix_grads.at[here, :], mix_grad_out.at[here, :], sems.at[1, step])
    finish(mesh_out, mesh_hbm, last_sems.at[0])
    finish(table_grad.at[0:nodes, :], own_grad, last_sems.at[1])


def encode_back_kernel(
    live_ref,
    place_ref,
    receivers,
    export,
    state_part,
    own_grad,
    from_inner,
    from_outer,
    from_left,
    from_right,
    edge_sender,
    update_normed,
    update_scale,
    gain,
    update_weight,
    normed_all,
    scale_all,
    mix_slope,
    pre_slope,
    inputs,
    hidden,
    message_weight,
    sender_weight,
    edge_grad,
    given,
    kept,
    upstream,
    grads,
):
    nodes, width = state_part.shape
    live = live_ref[0]
    arrived = from_left[...].astype(f32) + from_right[...].astype(f32)
    copies = arrived.shape[0]
    arrived += from_inner[0:copies, :].astype(f32) + from_outer[0:copies, :].astype(f32)
    table_grad = own_grad[...] + dot(row_hot(export[...], nodes), arrived.astype(bf16))
    state_grad = state_part[...] + back_dot(table_grad.astype(bf16), edge_sender[...])
    update_grad = norm_back(update_normed[...], update_scale[:, 0:1], state_grad * gain[...])
    upstream[0:nodes, :] = back_dot(update_grad.astype(bf16), update_weight[...]).astype(bf16)
    upstream[nodes:, :] = jnp.zeros_like(upstream[nodes:, :])
    turn_rows = blocks_per_turn * lanes
    variables = inputs.shape[1]
    grads[0:width, :] = jnp.zeros_like(grads[0:width, :])
    grads[width : 2 * width, :] = edge_grad[...].astype(f32)
    grads[2 * width :, :] = jnp.zeros_like(grads[2 * width :, :])

    def turn(step, carry):
        received = [
            lane_hot(live_row(receivers, step * blocks_per_turn + part, live), upstream.shape[0])
            for part in range(blocks_per_turn)
        ]
        here = pl.ds(pl.multiple_of(step * turn_rows, turn_rows), turn_rows)
        arriving = dot(jnp.concatenate(received, 0), upstream[...])
        product_grad = norm_back(
            normed_all[here, :].astype(f32), scale_all[here, 0:1], arriving
        ).astype(bf16)
        mix_grad = back_dot(product_grad, message_weight[...]) * mix_slope[here, :].astype(f32)
        mix_grad = mix_grad.astype(bf16)
        grads[0:width, :] += cross_dot(hidden[here, :], mix_grad)
        pre_grad = back_dot(mix_grad, sender_weight[...]) * pre_slope[here, :].astype(f32)
        grads[2 * width : 2 * width + variables, :] += cross_dot(
            inputs[here, :], pre_grad.astype(bf16)
        )
        return carry

    lax.fori_loop(0, receivers.shape[0] // blocks_per_turn, turn, 0)
    core, near, far = place_ref[0], place_ref[1], place_ref[2]
    piece = grads.shape[0] // 16
    for block in range(16):
        half, first, second = block // 4 % 2, block // 2 % 2, block % 2
        bits = (first ^ near, second ^ far) if half == 0 else (first ^ far, second ^ near)
        side = core ^ (1 - block // 8)
        origin = (((side * 2 + half) * 2 + bits[0]) * 2 + bits[1]) * piece
        rows = grads[pl.ds(pl.multiple_of(origin, 16), piece), :].astype(bf16)
        target = given if block < 8 else kept
        target[block % 8 * piece : (block % 8 + 1) * piece, :] = rows


def order_kernel(
    place_ref, mine, other, sender_grad, edge_grad, grid_grad, grads, last, sems
):
    core, near, far = place_ref[0], place_ref[1], place_ref[2]
    piece = grads.shape[0] // 16
    for block in range(16):
        half, first, second = block // 4 % 2, block // 2 % 2, block % 2
        bits = (first ^ near, second ^ far) if half == 0 else (first ^ far, second ^ near)
        side = core ^ (block // 8)
        origin = (((side * 2 + half) * 2 + bits[0]) * 2 + bits[1]) * piece
        source = mine if block < 8 else other
        rows = source[block % 8 * piece : (block % 8 + 1) * piece, :].astype(f32)
        grads[pl.ds(pl.multiple_of(origin, 16), piece), :] = rows
    width = sender_grad.shape[0]
    last[...] = grads[2 * width : 2 * width + last.shape[0], :]
    copies = (
        (grads.at[0:width, :], sender_grad, sems.at[0]),
        (grads.at[width : 2 * width, :], edge_grad, sems.at[1]),
        (last, grid_grad, sems.at[2]),
    )
    for copy in copies:
        send(*copy)
    for copy in copies:
        finish(*copy)


def call(kernel, operands, outs, scratch, scalars, mib):
    smem = pl.BlockSpec(memory_space=pltpu.SMEM)
    vmem = pl.BlockSpec(memory_space=pltpu.VMEM)
    hbm = pl.BlockSpec(memory_space=pl.ANY)
    return pl.pallas_call(
        kernel,
        out_shape=[jax.ShapeDtypeStruct(shape, dtype) for shape, dtype, _ in outs],
        in_specs=[smem] * scalars + [vmem] * (len(operands) - scalars),
        out_specs=[hbm if kind else vmem for _, _, kind in outs],
        scratch_shapes=[pltpu.VMEM(*shape) if isinstance(shape, tuple) else shape for shape in scratch],
        compiler_params=pltpu.CompilerParams(vmem_limit_bytes=mib << 20),
        cost_estimate=pl.CostEstimate(flops=4 << 30, bytes_accessed=8 << 20, transcendentals=0),
    )(*operands)


def shifted(x, step):
    size = lax.axis_size("lon")
    return lax.ppermute(x, "lon", [(i, (i + step) % size) for i in range(size)])


def partner(x, axis, flip):
    return lax.ppermute(x, axis, [(i, i ^ flip) for i in range(lax.axis_size(axis))])


def inner(x):
    return partner(x, "lat", 1)


def outer(x):
    ends = range(1, lax.axis_size("lat") - 1, 2)
    return lax.ppermute(x, "lat", [(i, i + 1) for i in ends] + [(i + 1, i) for i in ends])


def around(rows):
    left, right = shifted(rows, 1), shifted(rows, -1)
    above, below = inner(rows), outer(rows)
    left, right, above, below = lax.optimization_barrier((left, right, above, below))
    corners = jnp.concatenate([left, right], 0)
    return left, right, above, inner(corners), below, outer(corners)


def add(left, right):
    return (left.astype(f32) + right.astype(f32)).astype(bf16)


def half_chain(values, flips):
    one, two = flips
    for flip in flips:
        half = values.shape[0] // 2
        values = add(values[:half], partner(values[half:], "lat", 2 * flip))
    for scale in (1, 4):
        for flip in flips:
            values = add(values, partner(values, "lon", scale * flip))
    for flip in flips[::-1]:
        values = jnp.concatenate([values, partner(values, "lat", 2 * flip)], 0)
    return values


def summed(given, kept):
    values = add(kept, inner(given))
    half = values.shape[0] // 2
    values = jnp.concatenate(
        [half_chain(values[:half], (1, 3)), half_chain(values[half:], (3, 1))], 0
    )
    return values, inner(values)


def local(
    grid_in,
    grid_export,
    mesh_init,
    encode_senders,
    encode_slots,
    encode_receivers,
    encode_live,
    mesh_export,
    process_senders,
    process_slots,
    process_receivers,
    process_live,
    grid_weight,
    sender_weight,
    receiver_weight,
    message_weight,
    update_weight,
    encode_gain,
    edge_sender,
    edge_receiver,
    edge_message,
    node_update,
    node_gain,
    cotangent,
):
    grid_count, variables = grid_in.shape
    nodes, width = mesh_init.shape
    copies = mesh_export.shape[0]
    edges = encode_senders.shape[0] * encode_senders.shape[1]
    index = lax.axis_index("lat")
    place = jnp.stack([index & 1, (index >> 1 ^ index >> 2) & 1, index >> 2 & 1]).astype(jnp.int32)
    select = (grid_export[:, None] == jnp.arange(grid_count)[None, :]).astype(bf16)
    grid_near = around(dot(select, grid_in).astype(bf16))
    export = mesh_export[None]
    encode_gain, node_gain = encode_gain[None], node_gain[None]
    turns = encode_senders.shape[0] // blocks_per_turn
    saved = [
        ((edges, variables), bf16),
        ((edges, width), bf16),
        ((edges, width), bf16),
        ((edges, width), bf16),
        ((edges, width), bf16),
        ((edges, lanes), f32),
        ((nodes, width), f32),
        ((nodes, lanes), f32),
    ]
    state, picked, inputs, hidden, pre_slope, mix_slope, normed, scale, *update = call(
        encode_kernel,
        (
            encode_live,
            place,
            encode_slots,
            grid_in,
            *grid_near,
            mesh_init,
            encode_senders,
            encode_receivers,
            export,
            grid_weight,
            sender_weight,
            receiver_weight,
            message_weight,
            update_weight,
            encode_gain,
        ),
        [((nodes, width), bf16, 0), ((copies, width), bf16, 0)] + [each + (1,) for each in saved],
        [
            ((grid_count + 8 * lanes + grid_count - lanes, variables), bf16),
            ((256, width), bf16),
            ((nodes, width), f32),
        ]
        + saved
        + [pltpu.SemaphoreType.DMA((6, turns)), pltpu.SemaphoreType.DMA((2,))],
        3,
        20,
    )
    near = around(picked)
    (
        mesh_out,
        own_grad,
        to_lon,
        to_inner,
        to_outer,
        sender_rows,
        mix_grad,
        receiver_grad,
    ) = call(
        process_kernel,
        (
            process_live,
            place,
            process_slots,
            state,
            *near,
            process_senders,
            process_receivers,
            edge_sender,
            edge_receiver,
            edge_message,
            node_update,
            node_gain,
            cotangent,
        ),
        [
            ((nodes, width), bf16, 1),
            ((nodes, width), f32, 1),
            ((2 * copies, width), bf16, 0),
            ((3 * copies, width), bf16, 0),
            ((3 * copies, width), bf16, 0),
            ((edges, width), bf16, 1),
            ((edges, width), bf16, 1),
            ((nodes, width), bf16, 0),
        ],
        [
            ((256 + 8 * copies + 128, width), bf16),
            ((256, width), bf16),
            ((nodes, width), f32),
            ((edges, width), f32),
            ((edges, width), f32),
            ((edges, lanes), f32),
            ((256, width), bf16),
            ((256 + 8 * copies + 128, width), f32),
            ((nodes, width), f32),
            ((nodes, width), bf16),
            ((edges, width), bf16),
            ((edges, width), bf16),
            pltpu.SemaphoreType.DMA((2, turns)),
            pltpu.SemaphoreType.DMA((2,)),
        ],
        3,
        26,
    )
    from_inner, from_outer = inner(to_inner), outer(to_outer)
    to_left, to_right = [
        (
            to_lon[side * copies : (side + 1) * copies].astype(f32)
            + from_inner[(side + 1) * copies : (side + 2) * copies].astype(f32)
            + from_outer[(side + 1) * copies : (side + 2) * copies].astype(f32)
        ).astype(bf16)
        for side in (0, 1)
    ]
    from_right, from_left = shifted(to_left, -1), shifted(to_right, 1)
    state_part = cotangent.astype(f32) + back_dot(receiver_grad, edge_receiver)
    edge_grad = cross_dot(sender_rows, mix_grad).astype(bf16)
    given, kept = call(
        encode_back_kernel,
        (
            encode_live,
            place,
            encode_receivers,
            export,
            state_part,
            own_grad,
            from_inner,
            from_outer,
            from_left,
            from_right,
            edge_sender,
            update[0],
            update[1],
            encode_gain,
            update_weight,
            normed,
            scale,
            mix_slope,
            pre_slope,
            inputs,
            hidden,
            message_weight,
            sender_weight,
            edge_grad,
        ),
        [((640, width), bf16, 0)] * 2,
        [((256, width), bf16), ((1280, width), f32)],
        2,
        16,
    )
    mine, other = summed(given, kept)
    sender_grad, edge_grad, grid_grad = call(
        order_kernel,
        (place, mine, other),
        [((width, width), f32, 1), ((width, width), f32, 1), ((variables, width), f32, 1)],
        [((1280, width), f32), ((variables, width), f32), pltpu.SemaphoreType.DMA((3,))],
        1,
        8,
    )
    return mesh_out, grid_grad, sender_grad, edge_grad


def solution(mesh):
    tiles, shared = P(("lat", "lon")), P()
    wide = P(("lat", "lon"), None)
    return jax.shard_map(
        local,
        mesh=mesh,
        in_specs=(
            (wide, tiles, wide, wide, tiles, wide, tiles, tiles, wide, tiles, wide, tiles)
            + (shared,) * 11
            + (wide,)
        ),
        out_specs=(wide, shared, shared, shared),
        check_vma=False,
    )
```

```python
import jax
import jax.numpy as jnp
from jax import lax
from jax.experimental import pallas as pl
from jax.experimental.pallas import tpu as pltpu
from jax.sharding import PartitionSpec as P

norm_epsilon = 1e-05
blocks_per_turn = 4
lanes = 128
f32 = jnp.float32
bf16 = jnp.bfloat16


def dot(left, right):
    return jnp.dot(left, right, preferred_element_type=f32)


def back_dot(left, weight):
    return lax.dot_general(left, weight, (((1,), (1,)), ((), ())), preferred_element_type=f32)


def cross_dot(left, right):
    return lax.dot_general(left, right, (((0,), (0,)), ((), ())), preferred_element_type=f32)


def sigmoid(values):
    return 0.5 * jnp.tanh(0.5 * values) + 0.5


def row_mean(values):
    return jnp.mean(values, axis=-1, keepdims=True)


def normalise(values):
    center = values - row_mean(values)
    scale = lax.rsqrt(row_mean(center * center) + norm_epsilon)
    return center * scale, scale


def norm_back(normed, scale, upstream):
    inner = row_mean(upstream * normed)
    return scale * (upstream - row_mean(upstream) - normed * inner)


def lane_hot(row, width):
    spread = jnp.transpose(jnp.broadcast_to(row.astype(f32), (lanes, lanes)))
    column = lax.broadcasted_iota(jnp.int32, (lanes, lanes), 1).astype(f32)
    parts = [
        jnp.where(spread == column + float(start), 1.0, 0.0).astype(bf16)
        for start in range(0, width, lanes)
    ]
    return jnp.concatenate(parts, 1)


def row_hot(row, count):
    index = lax.broadcasted_iota(jnp.int32, (count, lanes), 0)
    return jnp.where(index == row, 1.0, 0.0).astype(bf16)


def window(slots, block, own_rows, place_ref):
    core, odd = place_ref[0], place_ref[3]
    slot = slots[block]
    band = jnp.where(slot >= 6, 2, jnp.where(slot >= 3, 1, 0))
    sector = slot - 3 * band
    close = (sector == 2) == (odd == 0)
    side = jnp.where(sector == 1, 0, jnp.where(close, 1, 2))
    inside = (band == 2) == (core == 0)
    place = jnp.where(band == 1, -1, jnp.where(inside, 2, 5)) + side
    return pl.multiple_of(jnp.where(slot == 4, 0, own_rows + lanes * place), lanes)


def fill(table, own, near):
    table[0 : own.shape[0], :] = own[...]
    first = own.shape[0] + -own.shape[0] % lanes
    if first > own.shape[0]:
        table[own.shape[0] : first, :] = jnp.zeros_like(table[own.shape[0] : first, :])
    for part in near:
        table[first : first + part.shape[0], :] = part[...]
        first += part.shape[0]
    table[first:, :] = jnp.zeros_like(table[first:, :])


def send(source, target, sem):
    pltpu.make_async_copy(source, target, sem).start()


def finish(source, target, sem):
    pltpu.make_async_copy(source, target, sem).wait()


def prepare_kernel(live_ref, senders, receivers, state, weight, *refs):
    count = (len(refs) - 1) // 2
    targets, (terms, *hots), sems = refs[:count], refs[count:-1], refs[-1]
    nodes = state.shape[0]
    terms[0:nodes, :] = dot(state[...], weight[...]).astype(bf16)
    terms[nodes:, :] = jnp.zeros_like(terms[nodes:, :])
    hot_rows(live_ref, senders, receivers, *hots)
    copies = [
        (source, target, sems.at[index])
        for index, (source, target) in enumerate(zip((terms, *hots), targets))
    ]
    for copy in copies:
        send(*copy)
    for copy in copies:
        finish(*copy)


def hot_rows(
    live_ref, senders, receivers, send_hot, receive_hot, place_hot, sender_place_hot=None
):
    for block in range(senders.shape[0]):
        here = slice(block * lanes, (block + 1) * lanes)
        begins = senders[block : block + 1, :]
        ends = jnp.where(block < live_ref[0], receivers[block : block + 1, :], -1)
        send_hot[here, :] = lane_hot(begins, send_hot.shape[1])
        receive_hot[here, :] = lane_hot(ends, receive_hot.shape[1])
        place_hot[:, here] = row_hot(ends, place_hot.shape[0])
        if sender_place_hot is not None:
            sender_place_hot[:, here] = row_hot(begins, sender_place_hot.shape[0])


def encode_kernel(
    live_ref,
    place_ref,
    slots,
    grid_own,
    near_close,
    near_far,
    near_inner,
    near_outer,
    base,
    senders,
    receivers,
    export,
    gain,
    receiver_weight,
    grid_weight,
    sender_weight,
    message_weight,
    update_weight,
    state,
    picked,
    inputs_out,
    hidden_out,
    pre_slope_out,
    mix_slope_out,
    normed_out,
    scale_out,
    update_normed_out,
    update_scale_out,
    table,
    total,
    inputs,
    hidden,
    pre_slope,
    mix_slope,
    normed_all,
    scale_all,
    update_normed,
    update_scale,
    projected,
    send_hot,
    receive_hot,
    place_hot,
    sems,
    last_sems,
):
    own = grid_own.shape[0]
    nodes = base.shape[0]
    projected[0:nodes, :] = dot(base[...], receiver_weight[...]).astype(bf16)
    projected[nodes:, :] = jnp.zeros_like(projected[nodes:, :])
    hot_rows(live_ref, senders, receivers, send_hot, receive_hot, place_hot)
    fill(table, grid_own, (near_close, near_far, near_inner, near_outer))
    total[...] = jnp.zeros_like(total)
    turn_rows = blocks_per_turn * lanes
    turns = slots.shape[0] // blocks_per_turn
    saved = (
        (inputs, inputs_out),
        (hidden, hidden_out),
        (pre_slope, pre_slope_out),
        (mix_slope, mix_slope_out),
        (normed_all, normed_out),
        (scale_all, scale_out),
    )
    for step in range(turns):
        here = pl.ds(step * turn_rows, turn_rows)
        gathered = []
        for block in range(step * blocks_per_turn, (step + 1) * blocks_per_turn):
            start = window(slots, block, own, place_ref)
            pick = send_hot[block * lanes : (block + 1) * lanes, :]
            gathered.append(dot(pick, table[pl.ds(start, own), :]).astype(bf16))
        rows = jnp.concatenate(gathered, 0)
        inputs[here, :] = rows
        pre = dot(rows, grid_weight[...])
        gate = sigmoid(pre)
        pre_slope[here, :] = (gate * (1.0 + pre * (1.0 - gate))).astype(bf16)
        embedded = (pre * gate).astype(bf16)
        hidden[here, :] = embedded
        sent = dot(embedded, sender_weight[...]).astype(bf16).astype(f32)
        mix = sent + dot(receive_hot[here, :], projected[...])
        gate = sigmoid(mix)
        mix_slope[here, :] = (gate * (1.0 + mix * (1.0 - gate))).astype(bf16)
        product = dot((mix * gate).astype(bf16), message_weight[...])
        normed, scale = normalise(product)
        normed = normed.astype(bf16)
        normed_all[here, :] = normed
        scale_all[here, :] = jnp.broadcast_to(scale, (turn_rows, lanes))
        total[...] += dot(place_hot[:, here], normed)
        for index, (source, target) in enumerate(saved):
            send(source.at[here, :], target.at[here, :], sems.at[index, step])
    update = dot(total[...].astype(bf16), update_weight[...])
    normed, scale = normalise(update)
    update_normed[...] = normed
    update_scale[...] = jnp.broadcast_to(scale, update_scale.shape)
    send(update_normed, update_normed_out, last_sems.at[0])
    send(update_scale, update_scale_out, last_sems.at[1])
    new_state = (base[...].astype(f32) + normed * gain[...]).astype(bf16)
    state[...] = new_state
    padded_state = jnp.concatenate(
        [new_state, jnp.zeros((256 - nodes, new_state.shape[1]), bf16)], 0
    )
    picked[...] = dot(lane_hot(export[...], 256), padded_state).astype(bf16)
    for step in range(turns):
        here = pl.ds(step * turn_rows, turn_rows)
        for index, (source, target) in enumerate(saved):
            finish(source.at[here, :], target.at[here, :], sems.at[index, step])
    finish(update_normed, update_normed_out, last_sems.at[0])
    finish(update_scale, update_scale_out, last_sems.at[1])


def process_kernel(
    place_ref,
    slots,
    state,
    near_close,
    near_far,
    near_inner,
    near_outer,
    terms,
    send_hot,
    receive_hot,
    place_hot,
    sender_place_hot,
    edge_sender,
    edge_message,
    node_update,
    gain,
    cotangent,
    mesh_hbm,
    own_grad,
    to_lon,
    to_inner,
    to_outer,
    sender_rows_out,
    mix_grad_out,
    receiver_grad,
    table,
    total,
    slope,
    normed_all,
    scale_all,
    upstream,
    table_grad,
    receiver_total,
    mesh_out,
    sender_rows,
    mix_grads,
    sems,
    last_sems,
):
    nodes = state.shape[0]
    reach = 256
    fill(table, state, (near_close, near_far, near_inner, near_outer))
    total[...] = jnp.zeros_like(total)
    turn_rows = blocks_per_turn * lanes
    turns = slots.shape[0] // blocks_per_turn

    for step in range(turns):
        here = pl.ds(step * turn_rows, turn_rows)
        gathered = []
        for block in range(step * blocks_per_turn, (step + 1) * blocks_per_turn):
            start = window(slots, block, reach, place_ref)
            pick = send_hot[block * lanes : (block + 1) * lanes, :]
            gathered.append(dot(pick, table[pl.ds(start, reach), :]).astype(bf16))
        rows = jnp.concatenate(gathered, 0)
        sender_rows[here, :] = rows
        sent = dot(rows, edge_sender[...]).astype(bf16).astype(f32)
        mix = sent + dot(receive_hot[here, :], terms[...])
        gate = sigmoid(mix)
        slope[here, :] = gate * (1.0 + mix * (1.0 - gate))
        product = dot((mix * gate).astype(bf16), edge_message[...])
        normed, scale = normalise(product)
        normed_all[here, :] = normed
        scale_all[here, :] = jnp.broadcast_to(scale, (turn_rows, lanes))
        total[...] += dot(place_hot[:, here], normed.astype(bf16))
        send(sender_rows.at[here, :], sender_rows_out.at[here, :], sems.at[0, step])
    update = dot(total[...].astype(bf16), node_update[...])
    normed, scale = normalise(update)
    mesh_out[...] = (state[...].astype(f32) + normed * gain[...]).astype(bf16)
    send(mesh_out, mesh_hbm, last_sems.at[0])
    update_grad = norm_back(normed, scale, cotangent[...].astype(f32) * gain[...])
    upstream[0:nodes, :] = back_dot(update_grad.astype(bf16), node_update[...]).astype(bf16)
    upstream[nodes:, :] = jnp.zeros_like(upstream[nodes:, :])
    table_grad[...] = jnp.zeros_like(table_grad)
    receiver_total[...] = jnp.zeros_like(receiver_total)

    for step in range(turns):
        here = pl.ds(step * turn_rows, turn_rows)
        arriving = dot(receive_hot[here, :], upstream[...])
        product_grad = norm_back(normed_all[here, :], scale_all[here, 0:1], arriving)
        mix_grad = back_dot(product_grad.astype(bf16), edge_message[...]) * slope[here, :]
        mix_grad = mix_grad.astype(bf16)
        mix_grads[here, :] = mix_grad
        send(mix_grads.at[here, :], mix_grad_out.at[here, :], sems.at[1, step])
        receiver_total[...] += dot(place_hot[:, here], mix_grad)
        for part in range(blocks_per_turn):
            block = step * blocks_per_turn + part
            start = window(slots, block, reach, place_ref)
            table_grad[pl.ds(start, nodes), :] += dot(
                sender_place_hot[:, block * lanes : (block + 1) * lanes],
                mix_grad[part * lanes : (part + 1) * lanes, :],
            )
    send(table_grad.at[0:nodes, :], own_grad, last_sems.at[1])
    first = reach
    for part in (to_lon, to_inner, to_outer):
        part[...] = table_grad[first : first + part.shape[0], :].astype(bf16)
        first += part.shape[0]
    receiver_grad[...] = receiver_total[...].astype(bf16)
    for step in range(turns):
        here = pl.ds(step * turn_rows, turn_rows)
        finish(sender_rows.at[here, :], sender_rows_out.at[here, :], sems.at[0, step])
        finish(mix_grads.at[here, :], mix_grad_out.at[here, :], sems.at[1, step])
    finish(mesh_out, mesh_hbm, last_sems.at[0])
    finish(table_grad.at[0:nodes, :], own_grad, last_sems.at[1])


def encode_back_kernel(
    live_ref,
    place_ref,
    receivers,
    export,
    state_part,
    own_grad,
    from_inner,
    from_outer,
    from_close,
    from_far,
    edge_sender,
    update_normed,
    update_scale,
    gain,
    update_weight,
    normed_all,
    scale_all,
    mix_slope,
    pre_slope,
    inputs,
    hidden,
    message_weight,
    sender_weight,
    edge_grad,
    given,
    kept,
    upstream,
    grads,
):
    nodes, width = state_part.shape
    arrived = from_close[...].astype(f32) + from_far[...].astype(f32)
    copies = arrived.shape[0]
    arrived += from_inner[0:copies, :].astype(f32) + from_outer[0:copies, :].astype(f32)
    table_grad = own_grad[...] + dot(row_hot(export[...], nodes), arrived.astype(bf16))
    state_grad = state_part[...] + back_dot(table_grad.astype(bf16), edge_sender[...])
    update_grad = norm_back(update_normed[...], update_scale[:, 0:1], state_grad * gain[...])
    upstream[0:nodes, :] = back_dot(update_grad.astype(bf16), update_weight[...]).astype(bf16)
    upstream[nodes:, :] = jnp.zeros_like(upstream[nodes:, :])
    turn_rows = blocks_per_turn * lanes
    variables = inputs.shape[1]
    grads[0:width, :] = jnp.zeros_like(grads[0:width, :])
    grads[width : 2 * width, :] = edge_grad[...].astype(f32)
    grads[2 * width :, :] = jnp.zeros_like(grads[2 * width :, :])

    for step in range(receivers.shape[0] // blocks_per_turn):
        here = pl.ds(step * turn_rows, turn_rows)
        received = [
            lane_hot(jnp.where(block < live_ref[0], receivers[block : block + 1, :], -1), 256)
            for block in range(step * blocks_per_turn, (step + 1) * blocks_per_turn)
        ]
        arriving = dot(jnp.concatenate(received, 0), upstream[...])
        product_grad = norm_back(
            normed_all[here, :].astype(f32), scale_all[here, 0:1], arriving
        ).astype(bf16)
        mix_grad = back_dot(product_grad, message_weight[...]) * mix_slope[here, :].astype(f32)
        mix_grad = mix_grad.astype(bf16)
        grads[0:width, :] += cross_dot(hidden[here, :], mix_grad)
        pre_grad = back_dot(mix_grad, sender_weight[...]) * pre_slope[here, :].astype(f32)
        grads[2 * width : 2 * width + variables, :] += cross_dot(
            inputs[here, :], pre_grad.astype(bf16)
        )
    arrange(place_ref, grads, given, kept)


def origin(place_ref, side, turn, piece):
    block = (place_ref[0] ^ side) * 4 + (place_ref[1 + side] ^ turn)
    return pl.ds(pl.multiple_of(block * piece, piece), piece)


def arrange(place_ref, grads, given, kept):
    piece = grads.shape[0] // 8
    for side, target in ((1, given), (0, kept)):
        for turn in range(4):
            rows = grads[origin(place_ref, side, turn, piece), :]
            target[turn * piece : (turn + 1) * piece, :] = rows.astype(bf16)


def order(place_ref, mine, other, grads):
    piece = grads.shape[0] // 8
    for side, source in ((0, mine), (1, other)):
        for turn in range(4):
            rows = source[turn * piece : (turn + 1) * piece, :].astype(f32)
            grads[origin(place_ref, side, turn, piece), :] = rows


def order_kernel(
    place_ref, mine, other, sender_grad, edge_grad, grid_grad, grads, last, sems
):
    order(place_ref, mine, other, grads)
    width = sender_grad.shape[0]
    last[...] = grads[2 * width : 2 * width + last.shape[0], :]
    copies = (
        (grads.at[0:width, :], sender_grad, sems.at[0]),
        (grads.at[width : 2 * width, :], edge_grad, sems.at[1]),
        (last, grid_grad, sems.at[2]),
    )
    for copy in copies:
        send(*copy)
    for copy in copies:
        finish(*copy)


def call(kernel, operands, outs, scratch, scalars, mib):
    smem = pl.BlockSpec(memory_space=pltpu.SMEM)
    vmem = pl.BlockSpec(memory_space=pltpu.VMEM)
    free = pl.BlockSpec(memory_space=pl.ANY)
    return pl.pallas_call(
        kernel,
        out_shape=[jax.ShapeDtypeStruct(shape, dtype) for shape, dtype, _ in outs],
        in_specs=[smem] * scalars + [vmem] * (len(operands) - scalars),
        out_specs=[free if kind else vmem for _, _, kind in outs],
        scratch_shapes=[pltpu.VMEM(*shape) if isinstance(shape, tuple) else shape for shape in scratch],
        compiler_params=pltpu.CompilerParams(vmem_limit_bytes=mib << 20),
        cost_estimate=pl.CostEstimate(flops=4 << 30, bytes_accessed=8 << 20, transcendentals=0),
    )(*operands)


def partner(x, axis, flip):
    return lax.ppermute(x, axis, [(i, i ^ flip) for i in range(lax.axis_size(axis))])


def inner(x):
    return partner(x, "lat", 1)


def outer(x):
    ends = range(1, lax.axis_size("lat") - 1, 2)
    return lax.ppermute(x, "lat", [(i, i + 1) for i in ends] + [(i + 1, i) for i in ends])


def close(x):
    return partner(x, "lon", 1)


def far(x):
    size = lax.axis_size("lon")
    ends = range(1, size, 2)
    return lax.ppermute(
        x, "lon", [(i, (i + 1) % size) for i in ends] + [((i + 1) % size, i) for i in ends]
    )


def around(rows):
    beside = close(rows), far(rows)
    column = jnp.concatenate((rows,) + beside, 0)
    return beside + (inner(column), outer(column))


def add(left, right):
    return (left.astype(f32) + right.astype(f32)).astype(bf16)


flips = {"x1": 32, "x3": 96, "y1": 4, "y3": 12, "z1": 1, "z3": 3}
stages = (
    (("x1", "y1"), ("x3", "y3")),
    (("z1", "x3"), ("z3", "x1")),
    (("y3", "z3"), ("y1", "z1")),
)


def met(x, stage, turn):
    pairs = []
    for device in range(lax.axis_size("lat") * lax.axis_size("lon")):
        first, second = stages[stage][device // 16 % 2]
        flip = (turn & 1) * flips[first] ^ (turn >> 1) * flips[second]
        pairs.append((device, device ^ flip))
    return lax.ppermute(x, ("lat", "lon"), pairs)


def added(own, one, two, three):
    pair = own.astype(f32) + one.astype(f32)
    return (pair + (two.astype(f32) + three.astype(f32))).astype(bf16)


def summed(given, kept):
    values = add(kept, inner(given))
    piece = values.shape[0] // 4
    own, *others = [values[turn * piece : (turn + 1) * piece] for turn in range(4)]
    values = added(own, *[met(part, 0, turn) for turn, part in zip((1, 2, 3), others)])
    for stage in (1, 2):
        values = added(values, *[met(values, stage, turn) for turn in (1, 2, 3)])
    values = jnp.concatenate([values] + [met(values, 0, turn) for turn in (1, 2, 3)], 0)
    return values, inner(values)


def local(
    grid_in,
    grid_export,
    mesh_init,
    encode_senders,
    encode_slots,
    encode_receivers,
    encode_live,
    mesh_export,
    process_senders,
    process_slots,
    process_receivers,
    process_live,
    grid_weight,
    sender_weight,
    receiver_weight,
    message_weight,
    update_weight,
    encode_gain,
    edge_sender,
    edge_receiver,
    edge_message,
    node_update,
    node_gain,
    cotangent,
):
    grid_count, variables = grid_in.shape
    nodes, width = mesh_init.shape
    copies = mesh_export.shape[0]
    edges = encode_senders.shape[0] * encode_senders.shape[1]
    core, chip, row = [
        part.astype(jnp.int32)
        for part in (
            lax.axis_index("lat") & 1,
            lax.axis_index("lat") >> 1,
            lax.axis_index("lon") >> 2,
        )
    ]
    odd = lax.axis_index("lon").astype(jnp.int32) & 1
    plain = (chip & 1 ^ chip >> 1) | (row & 1 ^ row >> 1) << 1
    wrapped = chip >> 1 | row >> 1 << 1
    first, second = jnp.where(core == 0, plain, wrapped), jnp.where(core == 0, wrapped, plain)
    place = jnp.stack([core, first, second, odd])
    select = (grid_export[:, None] == jnp.arange(grid_count)[None, :]).astype(bf16)
    grid_near = around(dot(select, grid_in).astype(bf16))
    export = mesh_export[None]
    encode_gain, node_gain = encode_gain[None], node_gain[None]
    turns = encode_senders.shape[0] // blocks_per_turn
    saved = [
        ((edges, variables), bf16),
        ((edges, width), bf16),
        ((edges, width), bf16),
        ((edges, width), bf16),
        ((edges, width), bf16),
        ((edges, lanes), f32),
        ((nodes, width), f32),
        ((nodes, lanes), f32),
    ]
    state, picked, inputs, hidden, pre_slope, mix_slope, normed, scale, *update = call(
        encode_kernel,
        (
            encode_live,
            place,
            encode_slots,
            grid_in,
            *grid_near,
            mesh_init,
            encode_senders,
            encode_receivers,
            export,
            encode_gain,
            receiver_weight,
            grid_weight,
            sender_weight,
            message_weight,
            update_weight,
        ),
        [((nodes, width), bf16, 0), ((copies, width), bf16, 0)] + [each + (1,) for each in saved],
        [
            ((grid_count + 8 * lanes + grid_count - lanes, variables), bf16),
            ((nodes, width), f32),
        ]
        + saved
        + [
            ((256, width), bf16),
            ((edges, grid_count), bf16),
            ((edges, 256), bf16),
            ((nodes, edges), bf16),
            pltpu.SemaphoreType.DMA((6, turns)),
            pltpu.SemaphoreType.DMA((2,)),
        ],
        3,
        44,
    )
    prepared = [
        ((256, width), bf16),
        ((edges, 256), bf16),
        ((edges, 256), bf16),
        ((nodes, edges), bf16),
        ((nodes, edges), bf16),
    ]
    terms, process_send, process_receive, process_place, process_sender_place = call(
        prepare_kernel,
        (process_live, process_senders, process_receivers, state, edge_receiver),
        [each + (1,) for each in prepared],
        prepared + [pltpu.SemaphoreType.DMA((5,))],
        1,
        16,
    )
    near = around(picked)
    (
        mesh_out,
        own_grad,
        to_lon,
        to_inner,
        to_outer,
        sender_rows,
        mix_grad,
        receiver_grad,
    ) = call(
        process_kernel,
        (
            place,
            process_slots,
            state,
            *near,
            terms,
            process_send,
            process_receive,
            process_place,
            process_sender_place,
            edge_sender,
            edge_message,
            node_update,
            node_gain,
            cotangent,
        ),
        [
            ((nodes, width), bf16, 1),
            ((nodes, width), f32, 1),
            ((2 * copies, width), bf16, 0),
            ((3 * copies, width), bf16, 0),
            ((3 * copies, width), bf16, 0),
            ((edges, width), bf16, 1),
            ((edges, width), bf16, 1),
            ((nodes, width), bf16, 0),
        ],
        [
            ((256 + 8 * copies + 128, width), bf16),
            ((nodes, width), f32),
            ((edges, width), f32),
            ((edges, width), f32),
            ((edges, lanes), f32),
            ((256, width), bf16),
            ((256 + 8 * copies + 128, width), f32),
            ((nodes, width), f32),
            ((nodes, width), bf16),
            ((edges, width), bf16),
            ((edges, width), bf16),
            pltpu.SemaphoreType.DMA((2, turns)),
            pltpu.SemaphoreType.DMA((2,)),
        ],
        2,
        26,
    )
    from_inner, from_outer = inner(to_inner), outer(to_outer)
    to_close, to_far = [
        (
            to_lon[side * copies : (side + 1) * copies].astype(f32)
            + from_inner[(side + 1) * copies : (side + 2) * copies].astype(f32)
            + from_outer[(side + 1) * copies : (side + 2) * copies].astype(f32)
        ).astype(bf16)
        for side in (0, 1)
    ]
    from_close, from_far = close(to_close), far(to_far)
    state_part = cotangent.astype(f32) + back_dot(receiver_grad, edge_receiver)
    edge_grad = cross_dot(sender_rows, mix_grad).astype(bf16)
    given, kept = call(
        encode_back_kernel,
        (
            encode_live,
            place,
            encode_receivers,
            export,
            state_part,
            own_grad,
            from_inner,
            from_outer,
            from_close,
            from_far,
            edge_sender,
            update[0],
            update[1],
            encode_gain,
            update_weight,
            normed,
            scale,
            mix_slope,
            pre_slope,
            inputs,
            hidden,
            message_weight,
            sender_weight,
            edge_grad,
        ),
        [((640, width), bf16, 0)] * 2,
        [((256, width), bf16), ((1280, width), f32)],
        2,
        16,
    )
    mine, other = summed(given, kept)
    sender_grad, edge_grad, grid_grad = call(
        order_kernel,
        (place, mine, other),
        [((width, width), f32, 1), ((width, width), f32, 1), ((variables, width), f32, 1)],
        [((1280, width), f32), ((variables, width), f32), pltpu.SemaphoreType.DMA((3,))],
        1,
        8,
    )
    return mesh_out, grid_grad, sender_grad, edge_grad


def solution(mesh):
    tiles, shared = P(("lat", "lon")), P()
    wide = P(("lat", "lon"), None)
    return jax.shard_map(
        local,
        mesh=mesh,
        in_specs=(
            (wide, tiles, wide, wide, tiles, wide, tiles, tiles, wide, tiles, wide, tiles)
            + (shared,) * 11
            + (wide,)
        ),
        out_specs=(wide, shared, shared, shared),
        check_vma=False,
    )
```

```python
import jax
import jax.numpy as jnp
from jax import lax
from jax.experimental import pallas as pl
from jax.experimental.pallas import tpu as pltpu
from jax.sharding import PartitionSpec as P

norm_epsilon = 1e-05
lanes = 128
f32 = jnp.float32
bf16 = jnp.bfloat16


def dot(left, right):
    return jnp.dot(left, right, preferred_element_type=f32)


def back_dot(left, weight):
    return lax.dot_general(left, weight, (((1,), (1,)), ((), ())), preferred_element_type=f32)


def cross_dot(left, right):
    return lax.dot_general(left, right, (((0,), (0,)), ((), ())), preferred_element_type=f32)


def sigmoid(values):
    return 0.5 * jnp.tanh(0.5 * values) + 0.5


def row_mean(values):
    return jnp.mean(values, axis=-1, keepdims=True)


def normalise(values):
    center = values - row_mean(values)
    scale = lax.rsqrt(row_mean(center * center) + norm_epsilon)
    return center * scale, scale


def norm_back(normed, scale, upstream):
    inner = row_mean(upstream * normed)
    return scale * (upstream - row_mean(upstream) - normed * inner)


def lane_hot(row, width):
    spread = jnp.transpose(jnp.broadcast_to(row.astype(f32), (lanes, lanes)))
    column = lax.broadcasted_iota(jnp.int32, (lanes, lanes), 1).astype(f32)
    parts = [
        jnp.where(spread == column + float(start), 1.0, 0.0).astype(bf16)
        for start in range(0, width, lanes)
    ]
    return jnp.concatenate(parts, 1)


def row_hot(row, count):
    index = lax.broadcasted_iota(jnp.int32, (count, lanes), 0)
    return jnp.where(index == row, 1.0, 0.0).astype(bf16)


def window(slots, block, own_rows, place_ref):
    core, odd = place_ref[0], place_ref[3]
    slot = slots[block]
    band = jnp.where(slot >= 6, 2, jnp.where(slot >= 3, 1, 0))
    sector = slot - 3 * band
    close = (sector == 2) == (odd == 0)
    side = jnp.where(sector == 1, 0, jnp.where(close, 1, 2))
    inside = (band == 2) == (core == 0)
    place = jnp.where(band == 1, -1, jnp.where(inside, 2, 5)) + side
    return pl.multiple_of(jnp.where(slot == 4, 0, own_rows + lanes * place), lanes)


def fill(table, own, near):
    table[0 : own.shape[0], :] = own[...]
    first = own.shape[0] + -own.shape[0] % lanes
    if first > own.shape[0]:
        table[own.shape[0] : first, :] = jnp.zeros_like(table[own.shape[0] : first, :])
    for part in near:
        table[first : first + part.shape[0], :] = part[...]
        first += part.shape[0]
    table[first:, :] = jnp.zeros_like(table[first:, :])


def send(source, target, sem):
    pltpu.make_async_copy(source, target, sem).start()


def finish(source, target, sem):
    pltpu.make_async_copy(source, target, sem).wait()


def prepare_kernel(live_ref, senders, receivers, state, weight, terms, *hots):
    nodes = state.shape[0]
    terms[0:nodes, :] = dot(state[...], weight[...]).astype(bf16)
    terms[nodes:, :] = jnp.zeros_like(terms[nodes:, :])
    block = lax.broadcasted_iota(jnp.int32, receivers.shape, 0)
    hot_rows(senders, jnp.where(block < live_ref[0], receivers[...], -1), *hots)


def hot_rows(senders, ends, send_hot, receive_hot, place_hot, sender_place_hot=None):
    for block in range(senders.shape[0]):
        here = slice(block * lanes, (block + 1) * lanes)
        begin_row, end_row = senders[block : block + 1, :], ends[block : block + 1, :]
        send_hot[here, :] = lane_hot(begin_row, send_hot.shape[1])
        receive_hot[here, :] = lane_hot(end_row, receive_hot.shape[1])
        place_hot[:, here] = row_hot(end_row, place_hot.shape[0])
        if sender_place_hot is not None:
            sender_place_hot[:, here] = row_hot(begin_row, sender_place_hot.shape[0])


def ends_kernel(live_ref, receivers, ends):
    block = lax.broadcasted_iota(jnp.int32, ends.shape, 0)
    ends[...] = jnp.where(block < live_ref[0], receivers[...], -1)


def encode_kernel(
    place_ref,
    slots,
    grid_columns,
    near_close,
    near_far,
    near_inner,
    near_inner_sides,
    near_outer,
    near_outer_sides,
    senders,
    ends,
    export,
    gain,
    base,
    receiver_weight,
    grid_weight,
    sender_weight,
    message_weight,
    update_weight,
    state,
    picked,
    inputs,
    hidden,
    pre_slope,
    mix_slope,
    normed_all,
    scale_all,
    update_normed,
    update_scale,
    table,
    projected,
    send_hot,
    receive_hot,
    place_hot,
):
    own = grid_columns.shape[1]
    nodes, width = base.shape
    projected[0:nodes, :] = dot(base[...], receiver_weight[...]).astype(bf16)
    projected[nodes:, :] = jnp.zeros_like(projected[nodes:, :])
    hot_rows(senders, ends, send_hot, receive_hot, place_hot)
    equal = lax.broadcasted_iota(jnp.int32, (own, own), 0) == lax.broadcasted_iota(
        jnp.int32, (own, own), 1
    )
    identity = jnp.where(equal, 1.0, 0.0).astype(bf16)
    grid_own = back_dot(identity, grid_columns[...]).astype(bf16)
    near = near_close, near_far, near_inner, near_inner_sides, near_outer, near_outer_sides
    fill(table, grid_own, near)
    for block in range(senders.shape[0]):
        here = slice(block * lanes, (block + 1) * lanes)
        start = window(slots, block, own, place_ref)
        inputs[here, :] = dot(send_hot[here, :], table[pl.ds(start, own), :]).astype(bf16)
    pre = dot(inputs[...], grid_weight[...])
    gate = sigmoid(pre)
    pre_slope[...] = (gate * (1.0 + pre * (1.0 - gate))).astype(bf16)
    hidden[...] = (pre * gate).astype(bf16)
    mix = dot(hidden[...], sender_weight[...]) + dot(receive_hot[...], projected[...])
    gate = sigmoid(mix)
    mix_slope[...] = (gate * (1.0 + mix * (1.0 - gate))).astype(bf16)
    product = dot((mix * gate).astype(bf16), message_weight[...])
    normed, scale = normalise(product)
    normed_all[...] = normed.astype(bf16)
    scale_all[...] = jnp.broadcast_to(scale, scale_all.shape)
    total = dot(place_hot[...], normed_all[...])
    update = dot(total.astype(bf16), update_weight[...])
    normed, scale = normalise(update)
    update_normed[...] = normed
    update_scale[...] = jnp.broadcast_to(scale, update_scale.shape)
    new_state = (base[...].astype(f32) + normed * gain[...]).astype(bf16)
    state[...] = new_state
    padded_state = jnp.concatenate([new_state, jnp.zeros((256 - nodes, width), bf16)], 0)
    picked[...] = dot(lane_hot(export[...], 256), padded_state).astype(bf16)


def process_kernel(
    place_ref,
    slots,
    state,
    near_close,
    near_far,
    near_inner,
    near_inner_sides,
    near_outer,
    near_outer_sides,
    terms,
    send_hot,
    receive_hot,
    place_hot,
    sender_place_hot,
    edge_sender,
    edge_message,
    node_update,
    gain,
    cotangent,
    mesh_far,
    own_grad,
    to_lon,
    to_inner,
    to_outer,
    to_outer_sides,
    sender_rows,
    mix_grads,
    table,
    slope,
    normed_all,
    upstream,
    table_grad,
    mesh_out,
    sem,
):
    nodes = state.shape[0]
    reach = 256
    near = near_close, near_far, near_inner, near_inner_sides, near_outer, near_outer_sides
    fill(table, state, near)
    blocks = slots.shape[0]
    starts = [window(slots, block, reach, place_ref) for block in range(blocks)]
    for block in range(blocks):
        here = slice(block * lanes, (block + 1) * lanes)
        picked = dot(send_hot[here, :], table[pl.ds(starts[block], reach), :])
        sender_rows[here, :] = picked.astype(bf16)
    mix = dot(sender_rows[...], edge_sender[...]) + dot(receive_hot[...], terms[...])
    gate = sigmoid(mix)
    slope[...] = (gate * (1.0 + mix * (1.0 - gate))).astype(bf16)
    product = dot((mix * gate).astype(bf16), edge_message[...])
    normed, edge_scale = normalise(product)
    normed_all[...] = normed.astype(bf16)
    total = dot(place_hot[...], normed_all[...])
    update = dot(total.astype(bf16), node_update[...])
    normed, scale = normalise(update)
    update_grad = norm_back(normed, scale, cotangent[...].astype(f32) * gain[...])
    upstream[0:nodes, :] = back_dot(update_grad.astype(bf16), node_update[...]).astype(bf16)
    upstream[nodes:, :] = jnp.zeros_like(upstream[nodes:, :])
    mesh_out[...] = (state[...].astype(f32) + normed * gain[...]).astype(bf16)
    send(mesh_out, mesh_far, sem)
    table_grad[...] = jnp.zeros_like(table_grad)
    arriving = dot(receive_hot[...], upstream[...])
    product_grad = norm_back(normed_all[...].astype(f32), edge_scale, arriving)
    mix_grad = back_dot(product_grad.astype(bf16), edge_message[...]) * slope[...].astype(f32)
    mix_grads[...] = mix_grad.astype(bf16)
    for block in range(blocks):
        here = slice(block * lanes, (block + 1) * lanes)
        table_grad[pl.ds(starts[block], nodes), :] += dot(
            sender_place_hot[:, here], mix_grads[here, :]
        )
    own_grad[...] = table_grad[0:nodes, :]
    first = reach
    for part in (to_lon, to_inner, to_outer, to_outer_sides):
        part[...] = table_grad[first : first + part.shape[0], :].astype(bf16)
        first += part.shape[0]
    finish(mesh_out, mesh_far, sem)


def edge_kernel(
    sender_rows, mix_grads, place_hot, edge_receiver, cotangent, edge_grad, state_part
):
    edge_grad[...] = cross_dot(sender_rows[...], mix_grads[...]).astype(bf16)
    receiver_grad = dot(place_hot[...], mix_grads[...]).astype(bf16)
    state_part[...] = cotangent[...].astype(f32) + back_dot(receiver_grad, edge_receiver[...])


def encode_back_kernel(
    place_ref,
    ends,
    export,
    state_part,
    own_grad,
    from_inner,
    from_close,
    from_far,
    from_outer,
    edge_sender,
    update_normed,
    update_scale,
    gain,
    update_weight,
    normed_all,
    scale_all,
    mix_slope,
    pre_slope,
    inputs,
    hidden,
    message_weight,
    sender_weight,
    edge_grad,
    given,
    kept,
    upstream,
    grads,
):
    nodes, width = state_part.shape
    arrived = from_close[...].astype(f32) + from_far[...].astype(f32)
    copies = arrived.shape[0]
    arrived += from_inner[0:copies, :].astype(f32) + from_outer[0:copies, :].astype(f32)
    table_grad = own_grad[...] + dot(row_hot(export[...], nodes), arrived.astype(bf16))
    state_grad = state_part[...] + back_dot(table_grad.astype(bf16), edge_sender[...])
    update_grad = norm_back(update_normed[...], update_scale[:, 0:1], state_grad * gain[...])
    upstream[0:nodes, :] = back_dot(update_grad.astype(bf16), update_weight[...]).astype(bf16)
    upstream[nodes:, :] = jnp.zeros_like(upstream[nodes:, :])
    variables = inputs.shape[1]
    grads[width : 2 * width, :] = edge_grad[...].astype(f32)
    grads[2 * width :, :] = jnp.zeros_like(grads[2 * width :, :])

    received = [lane_hot(ends[block : block + 1, :], 256) for block in range(ends.shape[0])]
    arriving = dot(jnp.concatenate(received, 0), upstream[...])
    product_grad = norm_back(
        normed_all[...].astype(f32), scale_all[:, 0:1], arriving
    ).astype(bf16)
    mix_grad = back_dot(product_grad, message_weight[...]) * mix_slope[...].astype(f32)
    mix_grad = mix_grad.astype(bf16)
    grads[0:width, :] = cross_dot(hidden[...], mix_grad)
    pre_grad = back_dot(mix_grad, sender_weight[...]) * pre_slope[...].astype(f32)
    grads[2 * width : 2 * width + variables, :] = cross_dot(
        inputs[...], pre_grad.astype(bf16)
    )
    arrange(place_ref, grads, given, kept)


def origin(place_ref, side, turn, piece):
    block = (place_ref[0] ^ side) * 4 + (place_ref[1 + side] ^ turn)
    return pl.ds(pl.multiple_of(block * piece, piece), piece)


def arrange(place_ref, grads, given, kept):
    piece = grads.shape[0] // 8
    for side, target in ((1, given), (0, kept)):
        for turn in range(4):
            rows = grads[origin(place_ref, side, turn, piece), :]
            target[turn * piece : (turn + 1) * piece, :] = rows.astype(bf16)


def order(place_ref, mine, other, grads):
    piece = grads.shape[0] // 8
    for side, source in ((0, mine), (1, other)):
        for turn in range(4):
            rows = source[turn * piece : (turn + 1) * piece, :].astype(f32)
            grads[origin(place_ref, side, turn, piece), :] = rows


def order_kernel(
    place_ref, mine, other, sender_grad, edge_grad, grid_grad, grads, last, sems
):
    order(place_ref, mine, other, grads)
    width = sender_grad.shape[0]
    last[...] = grads[2 * width : 2 * width + last.shape[0], :]
    copies = (
        (grads.at[0:width, :], sender_grad, sems.at[0]),
        (grads.at[width : 2 * width, :], edge_grad, sems.at[1]),
        (last, grid_grad, sems.at[2]),
    )
    for copy in copies:
        send(*copy)
    for copy in copies:
        finish(*copy)


def call(kernel, operands, outs, scratch, scalars, mib, work=4):
    smem = pl.BlockSpec(memory_space=pltpu.SMEM)
    vmem = pl.BlockSpec(memory_space=pltpu.VMEM)
    free = pl.BlockSpec(memory_space=pl.ANY)
    return pl.pallas_call(
        kernel,
        out_shape=[jax.ShapeDtypeStruct(shape, dtype) for shape, dtype, _ in outs],
        in_specs=[smem] * scalars + [vmem] * (len(operands) - scalars),
        out_specs=[free if kind else vmem for _, _, kind in outs],
        scratch_shapes=[pltpu.VMEM(*shape) if isinstance(shape, tuple) else shape for shape in scratch],
        compiler_params=pltpu.CompilerParams(vmem_limit_bytes=mib << 20),
        cost_estimate=pl.CostEstimate(flops=work << 30, bytes_accessed=8 << 20, transcendentals=0),
    )(*operands)


def partner(x, axis, flip):
    return lax.ppermute(x, axis, [(i, i ^ flip) for i in range(lax.axis_size(axis))])


def inner(x):
    return partner(x, "lat", 1)


def outer(x):
    ends = range(1, lax.axis_size("lat") - 1, 2)
    return lax.ppermute(x, "lat", [(i, i + 1) for i in ends] + [(i + 1, i) for i in ends])


def close(x):
    return partner(x, "lon", 1)


def far(x):
    size = lax.axis_size("lon")
    ends = range(1, size, 2)
    return lax.ppermute(
        x, "lon", [(i, (i + 1) % size) for i in ends] + [((i + 1) % size, i) for i in ends]
    )


def around(rows):
    lat, lon = (inner(rows), outer(rows)), (close(rows), far(rows))
    *lat, near_close, near_far = lax.optimization_barrier(lat + lon)
    sides = jnp.concatenate([near_close, near_far], 0)
    return near_close, near_far, lat[0], inner(sides), lat[1], outer(sides)


def add(left, right):
    return (left.astype(f32) + right.astype(f32)).astype(bf16)


flips = {"x1": 32, "x3": 96, "y1": 4, "y3": 12, "z1": 1, "z3": 3}
stages = (
    (("x1", "y3"), ("x3", "y1")),
    (("z1", "x3"), ("z3", "x1")),
    (("y1", "z3"), ("y3", "z1")),
)


def met(x, stage, turn):
    pairs = []
    for device in range(lax.axis_size("lat") * lax.axis_size("lon")):
        first, second = stages[stage][device // 16 % 2]
        flip = (turn & 1) * flips[first] ^ (turn >> 1) * flips[second]
        pairs.append((device, device ^ flip))
    return lax.ppermute(x, ("lat", "lon"), pairs)


def added(own, one, two, three):
    pair = own.astype(f32) + one.astype(f32)
    return (pair + (two.astype(f32) + three.astype(f32))).astype(bf16)


def summed(given, kept):
    values = add(kept, inner(given))
    piece = values.shape[0] // 4
    own, *others = [values[turn * piece : (turn + 1) * piece] for turn in range(4)]
    values = added(own, *[met(part, 0, turn) for turn, part in zip((1, 2, 3), others)])
    for stage in (1, 2):
        values = added(values, *[met(values, stage, turn) for turn in (1, 2, 3)])
    values = jnp.concatenate([values] + [met(values, 0, turn) for turn in (1, 2, 3)], 0)
    return values, inner(values)


def local(
    grid_in,
    grid_export,
    mesh_init,
    encode_senders,
    encode_slots,
    encode_receivers,
    encode_live,
    mesh_export,
    process_senders,
    process_slots,
    process_receivers,
    process_live,
    grid_weight,
    sender_weight,
    receiver_weight,
    message_weight,
    update_weight,
    encode_gain,
    edge_sender,
    edge_receiver,
    edge_message,
    node_update,
    node_gain,
    cotangent,
):
    grid_count, variables = grid_in.shape
    nodes, width = mesh_init.shape
    copies = mesh_export.shape[0]
    edges = encode_senders.shape[0] * encode_senders.shape[1]
    core, chip, row = [
        part.astype(jnp.int32)
        for part in (
            lax.axis_index("lat") & 1,
            lax.axis_index("lat") >> 1,
            lax.axis_index("lon") >> 2,
        )
    ]
    odd = lax.axis_index("lon").astype(jnp.int32) & 1
    even = (chip & 1 ^ chip >> 1) | row >> 1 << 1
    uneven = chip >> 1 | (row & 1 ^ row >> 1) << 1
    first, second = jnp.where(core == 0, even, uneven), jnp.where(core == 0, uneven, even)
    place = jnp.stack([core, first, second, odd])
    select = (grid_export[:, None] == jnp.arange(grid_count)[None, :]).astype(bf16)
    grid_near = around(dot(select, grid_in).astype(bf16))
    export = mesh_export[None]
    encode_gain, node_gain = encode_gain[None], node_gain[None]
    saved = [
        ((edges, variables), bf16, 0),
        ((edges, width), bf16, 0),
        ((edges, width), bf16, 0),
        ((edges, width), bf16, 0),
        ((edges, width), bf16, 0),
        ((edges, lanes), f32, 0),
        ((nodes, width), f32, 0),
        ((nodes, lanes), f32, 0),
    ]
    (ends,) = call(
        ends_kernel,
        (encode_live, encode_receivers),
        [(encode_receivers.shape, jnp.int32, 0)],
        [],
        1,
        16,
        30,
    )
    state, picked, inputs, hidden, pre_slope, mix_slope, normed, scale, *update = call(
        encode_kernel,
        (
            place,
            encode_slots,
            jnp.transpose(grid_in),
            *grid_near,
            encode_senders,
            ends,
            export,
            encode_gain,
            mesh_init,
            receiver_weight,
            grid_weight,
            sender_weight,
            message_weight,
            update_weight,
        ),
        [((nodes, width), bf16, 0), ((copies, width), bf16, 0)] + saved,
        [
            ((grid_count + 8 * lanes + grid_count - lanes, variables), bf16),
            ((256, width), bf16),
            ((edges, grid_count), bf16),
            ((edges, 256), bf16),
            ((nodes, edges), bf16),
        ],
        2,
        20,
    )
    terms, process_send, process_receive, process_place, process_sender_place = call(
        prepare_kernel,
        (process_live, process_senders, process_receivers, state, edge_receiver),
        [
            ((256, width), bf16, 0),
            ((edges, 256), bf16, 0),
            ((edges, 256), bf16, 0),
            ((nodes, edges), bf16, 0),
            ((nodes, edges), bf16, 0),
        ],
        [],
        1,
        16,
    )
    near = around(picked)
    (
        mesh_out,
        own_grad,
        to_lon,
        to_inner,
        to_outer,
        to_outer_sides,
        sender_rows,
        mix_grad,
    ) = call(
        process_kernel,
        (
            place,
            process_slots,
            state,
            *near,
            terms,
            process_send,
            process_receive,
            process_place,
            process_sender_place,
            edge_sender,
            edge_message,
            node_update,
            node_gain,
            cotangent,
        ),
        [
            ((nodes, width), bf16, 1),
            ((nodes, width), f32, 0),
            ((2 * copies, width), bf16, 0),
            ((3 * copies, width), bf16, 0),
            ((copies, width), bf16, 0),
            ((2 * copies, width), bf16, 0),
            ((edges, width), bf16, 0),
            ((edges, width), bf16, 0),
        ],
        [
            ((256 + 8 * copies + 128, width), bf16),
            ((edges, width), bf16),
            ((edges, width), bf16),
            ((256, width), bf16),
            ((256 + 8 * copies + 128, width), f32),
            ((nodes, width), bf16),
            pltpu.SemaphoreType.DMA,
        ],
        2,
        26,
    )
    from_outer_sides = outer(to_outer_sides)
    from_outer, from_inner = outer(to_outer), inner(to_inner)
    to_close, to_far = [
        (
            to_lon[side * copies : (side + 1) * copies].astype(f32)
            + from_inner[(side + 1) * copies : (side + 2) * copies].astype(f32)
            + from_outer_sides[side * copies : (side + 1) * copies].astype(f32)
        ).astype(bf16)
        for side in (0, 1)
    ]
    from_close, from_far = close(to_close), far(to_far)
    edge_grad, state_part = call(
        edge_kernel,
        (sender_rows, mix_grad, process_place, edge_receiver, cotangent),
        [((width, width), bf16, 0), ((nodes, width), f32, 0)],
        [],
        0,
        16,
    )
    given, kept = call(
        encode_back_kernel,
        (
            place,
            ends,
            export,
            state_part,
            own_grad,
            from_inner,
            from_close,
            from_far,
            from_outer,
            edge_sender,
            update[0],
            update[1],
            encode_gain,
            update_weight,
            normed,
            scale,
            mix_slope,
            pre_slope,
            inputs,
            hidden,
            message_weight,
            sender_weight,
            edge_grad,
        ),
        [((640, width), bf16, 0)] * 2,
        [((256, width), bf16), ((1280, width), f32)],
        1,
        16,
    )
    mine, other = summed(given, kept)
    sender_grad, edge_grad, grid_grad = call(
        order_kernel,
        (place, mine, other),
        [((width, width), f32, 1), ((width, width), f32, 1), ((variables, width), f32, 1)],
        [((1280, width), f32), ((variables, width), f32), pltpu.SemaphoreType.DMA((3,))],
        1,
        8,
    )
    return mesh_out, grid_grad, sender_grad, edge_grad


def solution(mesh):
    tiles, shared = P(("lat", "lon")), P()
    wide = P(("lat", "lon"), None)
    return jax.shard_map(
        local,
        mesh=mesh,
        in_specs=(
            (wide, tiles, wide, wide, tiles, wide, tiles, tiles, wide, tiles, wide, tiles)
            + (shared,) * 11
            + (wide,)
        ),
        out_specs=(wide, shared, shared, shared),
        check_vma=False,
    )
```

```python
import jax
import jax.numpy as jnp
from jax import lax
from jax.experimental import pallas as pl
from jax.experimental.pallas import tpu as pltpu
from jax.sharding import PartitionSpec as P

norm_epsilon = 1e-05
lanes = 128
f32 = jnp.float32
bf16 = jnp.bfloat16


def dot(left, right):
    return jnp.dot(left, right, preferred_element_type=f32)


def back_dot(left, weight):
    return lax.dot_general(left, weight, (((1,), (1,)), ((), ())), preferred_element_type=f32)


def cross_dot(left, right):
    return lax.dot_general(left, right, (((0,), (0,)), ((), ())), preferred_element_type=f32)


def sigmoid(values):
    return 0.5 * jnp.tanh(0.5 * values) + 0.5


def row_mean(values):
    return jnp.mean(values, axis=-1, keepdims=True)


def normalise(values):
    center = values - row_mean(values)
    scale = lax.rsqrt(row_mean(center * center) + norm_epsilon)
    return center * scale, scale


def norm_back(normed, scale, upstream):
    inner = row_mean(upstream * normed)
    return scale * (upstream - row_mean(upstream) - normed * inner)


def lane_hot(row, width):
    spread = jnp.transpose(jnp.broadcast_to(row.astype(f32), (lanes, lanes)))
    column = lax.broadcasted_iota(jnp.int32, (lanes, lanes), 1).astype(f32)
    parts = [
        jnp.where(spread == column + float(start), 1.0, 0.0).astype(bf16)
        for start in range(0, width, lanes)
    ]
    return jnp.concatenate(parts, 1)


def row_hot(row, count):
    index = lax.broadcasted_iota(jnp.int32, (count, lanes), 0)
    return jnp.where(index == row, 1.0, 0.0).astype(bf16)


def window(slots, block, own_rows, place_ref):
    core, odd = place_ref[0], place_ref[3]
    slot = slots[block]
    band = jnp.where(slot >= 6, 2, jnp.where(slot >= 3, 1, 0))
    sector = slot - 3 * band
    close = (sector == 2) == (odd == 0)
    side = jnp.where(sector == 1, 0, jnp.where(close, 1, 2))
    inside = (band == 2) == (core == 0)
    place = jnp.where(band == 1, -1, jnp.where(inside, 2, 5)) + side
    return pl.multiple_of(jnp.where(slot == 4, 0, own_rows + lanes * place), lanes)


def fill(table, own, near):
    table[0 : own.shape[0], :] = own[...]
    first = own.shape[0] + -own.shape[0] % lanes
    if first > own.shape[0]:
        table[own.shape[0] : first, :] = jnp.zeros_like(table[own.shape[0] : first, :])
    for part in near:
        table[first : first + part.shape[0], :] = part[...]
        first += part.shape[0]
    table[first:, :] = jnp.zeros_like(table[first:, :])


def send(source, target, sem):
    pltpu.make_async_copy(source, target, sem).start()


def finish(source, target, sem):
    pltpu.make_async_copy(source, target, sem).wait()


def prepare_kernel(live_ref, senders, receivers, state, weight, terms, *hots):
    nodes = state.shape[0]
    terms[0:nodes, :] = dot(state[...], weight[...]).astype(bf16)
    terms[nodes:, :] = jnp.zeros_like(terms[nodes:, :])
    block = lax.broadcasted_iota(jnp.int32, receivers.shape, 0)
    hot_rows(senders, jnp.where(block < live_ref[0], receivers[...], -1), *hots)


def hot_rows(senders, ends, send_hot, receive_hot, place_hot, sender_place_hot=None):
    for block in range(senders.shape[0]):
        here = slice(block * lanes, (block + 1) * lanes)
        begin_row, end_row = senders[block : block + 1, :], ends[block : block + 1, :]
        send_hot[here, :] = lane_hot(begin_row, send_hot.shape[1])
        receive_hot[here, :] = lane_hot(end_row, receive_hot.shape[1])
        place_hot[:, here] = row_hot(end_row, place_hot.shape[0])
        if sender_place_hot is not None:
            sender_place_hot[:, here] = row_hot(begin_row, sender_place_hot.shape[0])


def ends_kernel(live_ref, receivers, ends):
    block = lax.broadcasted_iota(jnp.int32, ends.shape, 0)
    ends[...] = jnp.where(block < live_ref[0], receivers[...], -1)


def encode_kernel(
    place_ref,
    slots,
    grid_columns,
    near_close,
    near_far,
    near_inner,
    near_inner_sides,
    near_outer,
    near_outer_sides,
    senders,
    ends,
    export,
    gain,
    base,
    receiver_weight,
    grid_weight,
    sender_weight,
    message_weight,
    update_weight,
    state,
    picked,
    inputs,
    hidden,
    pre_slope,
    mix_slope,
    normed_all,
    scale_all,
    update_normed,
    update_scale,
    table,
    projected,
    send_hot,
    receive_hot,
    place_hot,
):
    own = grid_columns.shape[1]
    nodes, width = base.shape
    projected[0:nodes, :] = dot(base[...], receiver_weight[...]).astype(bf16)
    projected[nodes:, :] = jnp.zeros_like(projected[nodes:, :])
    hot_rows(senders, ends, send_hot, receive_hot, place_hot)
    equal = lax.broadcasted_iota(jnp.int32, (own, own), 0) == lax.broadcasted_iota(
        jnp.int32, (own, own), 1
    )
    identity = jnp.where(equal, 1.0, 0.0).astype(bf16)
    grid_own = back_dot(identity, grid_columns[...]).astype(bf16)
    near = near_close, near_far, near_inner, near_inner_sides, near_outer, near_outer_sides
    fill(table, grid_own, near)
    for block in range(senders.shape[0]):
        here = slice(block * lanes, (block + 1) * lanes)
        start = window(slots, block, own, place_ref)
        inputs[here, :] = dot(send_hot[here, :], table[pl.ds(start, own), :]).astype(bf16)
    pre = dot(inputs[...], grid_weight[...])
    gate = sigmoid(pre)
    pre_slope[...] = (gate * (1.0 + pre * (1.0 - gate))).astype(bf16)
    hidden[...] = (pre * gate).astype(bf16)
    mix = dot(hidden[...], sender_weight[...]) + dot(receive_hot[...], projected[...])
    gate = sigmoid(mix)
    mix_slope[...] = (gate * (1.0 + mix * (1.0 - gate))).astype(bf16)
    product = dot((mix * gate).astype(bf16), message_weight[...])
    normed, scale = normalise(product)
    normed_all[...] = normed.astype(bf16)
    scale_all[...] = jnp.broadcast_to(scale, scale_all.shape)
    total = dot(place_hot[...], normed_all[...])
    update = dot(total.astype(bf16), update_weight[...])
    normed, scale = normalise(update)
    update_normed[...] = normed
    update_scale[...] = jnp.broadcast_to(scale, update_scale.shape)
    new_state = (base[...].astype(f32) + normed * gain[...]).astype(bf16)
    state[...] = new_state
    padded_state = jnp.concatenate([new_state, jnp.zeros((256 - nodes, width), bf16)], 0)
    picked[...] = dot(lane_hot(export[...], 256), padded_state).astype(bf16)


def process_kernel(
    place_ref,
    slots,
    state,
    near_close,
    near_far,
    near_inner,
    near_inner_sides,
    near_outer,
    near_outer_sides,
    terms,
    send_hot,
    receive_hot,
    place_hot,
    sender_place_hot,
    edge_sender,
    edge_message,
    node_update,
    gain,
    cotangent,
    mesh_far,
    own_grad,
    to_lon,
    to_inner,
    to_outer,
    to_outer_sides,
    sender_rows,
    mix_grads,
    table,
    slope,
    normed_all,
    upstream,
    table_grad,
    mesh_out,
    sem,
):
    nodes = state.shape[0]
    reach = 256
    near = near_close, near_far, near_inner, near_inner_sides, near_outer, near_outer_sides
    fill(table, state, near)
    blocks = slots.shape[0]
    starts = [window(slots, block, reach, place_ref) for block in range(blocks)]
    for block in range(blocks):
        here = slice(block * lanes, (block + 1) * lanes)
        picked = dot(send_hot[here, :], table[pl.ds(starts[block], reach), :])
        sender_rows[here, :] = picked.astype(bf16)
    mix = dot(sender_rows[...], edge_sender[...]) + dot(receive_hot[...], terms[...])
    gate = sigmoid(mix)
    slope[...] = (gate * (1.0 + mix * (1.0 - gate))).astype(bf16)
    product = dot((mix * gate).astype(bf16), edge_message[...])
    normed, edge_scale = normalise(product)
    normed_all[...] = normed.astype(bf16)
    total = dot(place_hot[...], normed_all[...])
    update = dot(total.astype(bf16), node_update[...])
    normed, scale = normalise(update)
    update_grad = norm_back(normed, scale, cotangent[...].astype(f32) * gain[...])
    upstream[0:nodes, :] = back_dot(update_grad.astype(bf16), node_update[...]).astype(bf16)
    upstream[nodes:, :] = jnp.zeros_like(upstream[nodes:, :])
    mesh_out[...] = (state[...].astype(f32) + normed * gain[...]).astype(bf16)
    send(mesh_out, mesh_far, sem)
    table_grad[...] = jnp.zeros_like(table_grad)
    arriving = dot(receive_hot[...], upstream[...])
    product_grad = norm_back(normed_all[...].astype(f32), edge_scale, arriving)
    mix_grad = back_dot(product_grad.astype(bf16), edge_message[...]) * slope[...].astype(f32)
    mix_grads[...] = mix_grad.astype(bf16)
    for block in range(blocks):
        here = slice(block * lanes, (block + 1) * lanes)
        table_grad[pl.ds(starts[block], nodes), :] += dot(
            sender_place_hot[:, here], mix_grads[here, :]
        )
    own_grad[...] = table_grad[0:nodes, :]
    first = reach
    for part in (to_lon, to_inner, to_outer, to_outer_sides):
        part[...] = table_grad[first : first + part.shape[0], :].astype(bf16)
        first += part.shape[0]
    finish(mesh_out, mesh_far, sem)


def edge_kernel(
    sender_rows, mix_grads, place_hot, edge_receiver, cotangent, edge_grad, state_part
):
    edge_grad[...] = cross_dot(sender_rows[...], mix_grads[...]).astype(bf16)
    receiver_grad = dot(place_hot[...], mix_grads[...]).astype(bf16)
    state_part[...] = cotangent[...].astype(f32) + back_dot(receiver_grad, edge_receiver[...])


def encode_back_kernel(
    place_ref,
    ends,
    export,
    state_part,
    own_grad,
    from_inner,
    from_close,
    from_far,
    from_outer,
    edge_sender,
    update_normed,
    update_scale,
    gain,
    update_weight,
    normed_all,
    scale_all,
    mix_slope,
    pre_slope,
    inputs,
    hidden,
    message_weight,
    sender_weight,
    edge_grad,
    given,
    kept,
    upstream,
    grads,
):
    nodes, width = state_part.shape
    arrived = from_close[...].astype(f32) + from_far[...].astype(f32)
    copies = arrived.shape[0]
    arrived += from_inner[0:copies, :].astype(f32) + from_outer[0:copies, :].astype(f32)
    table_grad = own_grad[...] + dot(row_hot(export[...], nodes), arrived.astype(bf16))
    state_grad = state_part[...] + back_dot(table_grad.astype(bf16), edge_sender[...])
    update_grad = norm_back(update_normed[...], update_scale[:, 0:1], state_grad * gain[...])
    upstream[0:nodes, :] = back_dot(update_grad.astype(bf16), update_weight[...]).astype(bf16)
    upstream[nodes:, :] = jnp.zeros_like(upstream[nodes:, :])
    variables = inputs.shape[1]
    grads[width : 2 * width, :] = edge_grad[...].astype(f32)
    grads[2 * width :, :] = jnp.zeros_like(grads[2 * width :, :])

    received = [lane_hot(ends[block : block + 1, :], 256) for block in range(ends.shape[0])]
    arriving = dot(jnp.concatenate(received, 0), upstream[...])
    product_grad = norm_back(
        normed_all[...].astype(f32), scale_all[:, 0:1], arriving
    ).astype(bf16)
    mix_grad = back_dot(product_grad, message_weight[...]) * mix_slope[...].astype(f32)
    mix_grad = mix_grad.astype(bf16)
    grads[0:width, :] = cross_dot(hidden[...], mix_grad)
    pre_grad = back_dot(mix_grad, sender_weight[...]) * pre_slope[...].astype(f32)
    grads[2 * width : 2 * width + variables, :] = cross_dot(
        inputs[...], pre_grad.astype(bf16)
    )
    arrange(place_ref, grads, given, kept)


def owner(place_ref, side, turn):
    return (place_ref[0] ^ side) * 4 + (place_ref[1 + side] ^ turn)


def rows_of(block, count, first=0):
    return pl.ds(pl.multiple_of(first + block * count, 32), count)


def arrange(place_ref, grads, given, kept):
    width = grads.shape[1]
    for side, target in ((1, given), (0, kept)):
        for turn in range(4):
            block = owner(place_ref, side, turn)
            first = turn * 160
            for count, base in ((64, 0), (64, width), (32, 2 * width)):
                rows = grads[rows_of(block, count, base), :]
                target[first : first + count, :] = rows.astype(bf16)
                first += count


def order(place_ref, side, source, sender_grad, edge_grad, parts, sems):
    copies = []
    for turn in range(4):
        block = owner(place_ref, side, turn)
        parts[turn] = source[turn * 160 : turn * 160 + 128, :].astype(f32)
        for index, target in enumerate((sender_grad, edge_grad)):
            copies.append(
                (
                    parts.at[turn, index * 64 : index * 64 + 64, :],
                    target.at[rows_of(block, 64), :],
                    sems.at[turn, index],
                )
            )
            send(*copies[-1])
    return copies


def order_mine_kernel(place_ref, mine, sender_grad, edge_grad, parts, sems):
    for copy in order(place_ref, 0, mine, sender_grad, edge_grad, parts, sems):
        finish(*copy)


def order_other_kernel(
    place_ref,
    mine,
    other,
    sender_in,
    edge_in,
    sender_grad,
    edge_grad,
    grid_grad,
    parts,
    grid_rows,
    last,
    sems,
    last_sem,
):
    copies = order(place_ref, 1, other, sender_grad, edge_grad, parts, sems)
    for side, source in ((0, mine), (1, other)):
        for turn in range(4):
            rows = source[turn * 160 + 128 : (turn + 1) * 160, :].astype(f32)
            grid_rows[rows_of(owner(place_ref, side, turn), 32), :] = rows
    last[...] = grid_rows[0 : last.shape[0], :]
    send(last, grid_grad, last_sem)
    for copy in copies:
        finish(*copy)
    finish(last, grid_grad, last_sem)


def call(kernel, operands, outs, scratch, scalars, mib, work=4, kept_places={}):
    smem = pl.BlockSpec(memory_space=pltpu.SMEM)
    vmem = pl.BlockSpec(memory_space=pltpu.VMEM)
    free = pl.BlockSpec(memory_space=pl.ANY)
    return pl.pallas_call(
        kernel,
        out_shape=[jax.ShapeDtypeStruct(shape, dtype) for shape, dtype, _ in outs],
        in_specs=[smem] * scalars
        + [free if index in kept_places else vmem for index in range(scalars, len(operands))],
        input_output_aliases=kept_places,
        out_specs=[free if kind else vmem for _, _, kind in outs],
        scratch_shapes=[pltpu.VMEM(*shape) if isinstance(shape, tuple) else shape for shape in scratch],
        compiler_params=pltpu.CompilerParams(vmem_limit_bytes=mib << 20),
        cost_estimate=pl.CostEstimate(flops=work << 30, bytes_accessed=8 << 20, transcendentals=0),
    )(*operands)


def partner(x, axis, flip):
    return lax.ppermute(x, axis, [(i, i ^ flip) for i in range(lax.axis_size(axis))])


def inner(x):
    return partner(x, "lat", 1)


def outer(x):
    ends = range(1, lax.axis_size("lat") - 1, 2)
    return lax.ppermute(x, "lat", [(i, i + 1) for i in ends] + [(i + 1, i) for i in ends])


def close(x):
    return partner(x, "lon", 1)


def far(x):
    size = lax.axis_size("lon")
    ends = range(1, size, 2)
    return lax.ppermute(
        x, "lon", [(i, (i + 1) % size) for i in ends] + [((i + 1) % size, i) for i in ends]
    )


def around(rows):
    near_outer, near_inner, near_close, near_far = outer(rows), inner(rows), close(rows), far(rows)
    near_inner, near_close, near_far = lax.optimization_barrier((near_inner, near_close, near_far))
    sides = jnp.concatenate([near_close, near_far], 0)
    return near_close, near_far, near_inner, inner(sides), near_outer, outer(sides)


def add(left, right):
    return (left.astype(f32) + right.astype(f32)).astype(bf16)


flips = {"x1": 32, "x3": 96, "y1": 4, "y3": 12, "z1": 1, "z3": 3}
stages = (
    (("x1", "y1"), ("x3", "y3")),
    (("z1", "x3"), ("z3", "x1")),
    (("y3", "z3"), ("y1", "z1")),
)


def met(x, stage, turn):
    pairs = []
    for device in range(lax.axis_size("lat") * lax.axis_size("lon")):
        first, second = stages[stage][device // 16 % 2]
        flip = (turn & 1) * flips[first] ^ (turn >> 1) * flips[second]
        pairs.append((device, device ^ flip))
    return lax.ppermute(x, ("lat", "lon"), pairs)


def added(own, one, two, three):
    pair = own.astype(f32) + one.astype(f32)
    return (pair + (two.astype(f32) + three.astype(f32))).astype(bf16)


def summed(given, kept):
    values = add(kept, inner(given))
    piece = values.shape[0] // 4
    own, *others = [values[turn * piece : (turn + 1) * piece] for turn in range(4)]
    values = added(own, *[met(part, 0, turn) for turn, part in zip((1, 2, 3), others)])
    for stage in (1, 2):
        values = added(values, *[met(values, stage, turn) for turn in (1, 2, 3)])
    values = jnp.concatenate([values] + [met(values, 0, turn) for turn in (1, 2, 3)], 0)
    return values


def local(
    grid_in,
    grid_export,
    mesh_init,
    encode_senders,
    encode_slots,
    encode_receivers,
    encode_live,
    mesh_export,
    process_senders,
    process_slots,
    process_receivers,
    process_live,
    grid_weight,
    sender_weight,
    receiver_weight,
    message_weight,
    update_weight,
    encode_gain,
    edge_sender,
    edge_receiver,
    edge_message,
    node_update,
    node_gain,
    cotangent,
):
    grid_count, variables = grid_in.shape
    nodes, width = mesh_init.shape
    copies = mesh_export.shape[0]
    edges = encode_senders.shape[0] * encode_senders.shape[1]
    core, chip, row = [
        part.astype(jnp.int32)
        for part in (
            lax.axis_index("lat") & 1,
            lax.axis_index("lat") >> 1,
            lax.axis_index("lon") >> 2,
        )
    ]
    odd = lax.axis_index("lon").astype(jnp.int32) & 1
    plain = (chip & 1 ^ chip >> 1) | (row & 1 ^ row >> 1) << 1
    wrapped = chip >> 1 | row >> 1 << 1
    first, second = jnp.where(core == 0, plain, wrapped), jnp.where(core == 0, wrapped, plain)
    place = jnp.stack([core, first, second, odd])
    select = (grid_export[:, None] == jnp.arange(grid_count)[None, :]).astype(bf16)
    grid_near = around(dot(select, grid_in).astype(bf16))
    export = mesh_export[None]
    encode_gain, node_gain = encode_gain[None], node_gain[None]
    saved = [
        ((edges, variables), bf16, 0),
        ((edges, width), bf16, 0),
        ((edges, width), bf16, 0),
        ((edges, width), bf16, 0),
        ((edges, width), bf16, 0),
        ((edges, lanes), f32, 0),
        ((nodes, width), f32, 0),
        ((nodes, lanes), f32, 0),
    ]
    (ends,) = call(
        ends_kernel,
        (encode_live, encode_receivers),
        [(encode_receivers.shape, jnp.int32, 0)],
        [],
        1,
        16,
        30,
    )
    state, picked, inputs, hidden, pre_slope, mix_slope, normed, scale, *update = call(
        encode_kernel,
        (
            place,
            encode_slots,
            jnp.transpose(grid_in),
            *grid_near,
            encode_senders,
            ends,
            export,
            encode_gain,
            mesh_init,
            receiver_weight,
            grid_weight,
            sender_weight,
            message_weight,
            update_weight,
        ),
        [((nodes, width), bf16, 0), ((copies, width), bf16, 0)] + saved,
        [
            ((grid_count + 8 * lanes + grid_count - lanes, variables), bf16),
            ((256, width), bf16),
            ((edges, grid_count), bf16),
            ((edges, 256), bf16),
            ((nodes, edges), bf16),
        ],
        2,
        20,
    )
    terms, process_send, process_receive, process_place, process_sender_place = call(
        prepare_kernel,
        (process_live, process_senders, process_receivers, state, edge_receiver),
        [
            ((256, width), bf16, 0),
            ((edges, 256), bf16, 0),
            ((edges, 256), bf16, 0),
            ((nodes, edges), bf16, 0),
            ((nodes, edges), bf16, 0),
        ],
        [],
        1,
        16,
    )
    near = around(picked)
    (
        mesh_out,
        own_grad,
        to_lon,
        to_inner,
        to_outer,
        to_outer_sides,
        sender_rows,
        mix_grad,
    ) = call(
        process_kernel,
        (
            place,
            process_slots,
            state,
            *near,
            terms,
            process_send,
            process_receive,
            process_place,
            process_sender_place,
            edge_sender,
            edge_message,
            node_update,
            node_gain,
            cotangent,
        ),
        [
            ((nodes, width), bf16, 1),
            ((nodes, width), f32, 0),
            ((2 * copies, width), bf16, 0),
            ((3 * copies, width), bf16, 0),
            ((copies, width), bf16, 0),
            ((2 * copies, width), bf16, 0),
            ((edges, width), bf16, 0),
            ((edges, width), bf16, 0),
        ],
        [
            ((256 + 8 * copies + 128, width), bf16),
            ((edges, width), bf16),
            ((edges, width), bf16),
            ((256, width), bf16),
            ((256 + 8 * copies + 128, width), f32),
            ((nodes, width), bf16),
            pltpu.SemaphoreType.DMA,
        ],
        2,
        26,
    )
    from_outer_sides = outer(to_outer_sides)
    from_outer, from_inner = outer(to_outer), inner(to_inner)
    to_close, to_far = [
        (
            to_lon[side * copies : (side + 1) * copies].astype(f32)
            + from_inner[(side + 1) * copies : (side + 2) * copies].astype(f32)
            + from_outer_sides[side * copies : (side + 1) * copies].astype(f32)
        ).astype(bf16)
        for side in (0, 1)
    ]
    from_close, from_far = close(to_close), far(to_far)
    edge_grad, state_part = call(
        edge_kernel,
        (sender_rows, mix_grad, process_place, edge_receiver, cotangent),
        [((width, width), bf16, 0), ((nodes, width), f32, 0)],
        [],
        0,
        16,
    )
    given, kept = call(
        encode_back_kernel,
        (
            place,
            ends,
            export,
            state_part,
            own_grad,
            from_inner,
            from_close,
            from_far,
            from_outer,
            edge_sender,
            update[0],
            update[1],
            encode_gain,
            update_weight,
            normed,
            scale,
            mix_slope,
            pre_slope,
            inputs,
            hidden,
            message_weight,
            sender_weight,
            edge_grad,
        ),
        [((640, width), bf16, 0)] * 2,
        [((256, width), bf16), ((1280, width), f32)],
        1,
        16,
    )
    mine = summed(given, kept)
    other = inner(mine)
    halves = [((width, width), f32, 1)] * 2
    scratch = [((4, 128, width), f32), pltpu.SemaphoreType.DMA((4, 2))]
    parts = call(order_mine_kernel, (place, mine), halves, scratch, 1, 8)
    sender_grad, edge_grad, grid_grad = call(
        order_other_kernel,
        (place, mine, other, *parts),
        halves + [((variables, width), f32, 1)],
        scratch[:1]
        + [((256, width), f32), ((variables, width), f32)]
        + scratch[1:]
        + [pltpu.SemaphoreType.DMA],
        1,
        8,
        kept_places={3: 0, 4: 1},
    )
    return mesh_out, grid_grad, sender_grad, edge_grad


def solution(mesh):
    tiles, shared = P(("lat", "lon")), P()
    wide = P(("lat", "lon"), None)
    return jax.shard_map(
        local,
        mesh=mesh,
        in_specs=(
            (wide, tiles, wide, wide, tiles, wide, tiles, tiles, wide, tiles, wide, tiles)
            + (shared,) * 11
            + (wide,)
        ),
        out_specs=(wide, shared, shared, shared),
        check_vma=False,
    )
```

```python
import jax
import jax.numpy as jnp
from jax import lax
from jax.experimental import pallas as pl
from jax.experimental.pallas import tpu as pltpu
from jax.sharding import PartitionSpec as P

norm_epsilon = 1e-05
lanes = 128
f32 = jnp.float32
bf16 = jnp.bfloat16


def dot(left, right):
    return jnp.dot(left, right, preferred_element_type=f32)


def back_dot(left, weight):
    return lax.dot_general(left, weight, (((1,), (1,)), ((), ())), preferred_element_type=f32)


def cross_dot(left, right):
    return lax.dot_general(left, right, (((0,), (0,)), ((), ())), preferred_element_type=f32)


def sigmoid(values):
    return 0.5 * jnp.tanh(0.5 * values) + 0.5


def row_mean(values):
    return jnp.mean(values, axis=-1, keepdims=True)


def normalise(values):
    center = values - row_mean(values)
    scale = lax.rsqrt(row_mean(center * center) + norm_epsilon)
    return center * scale, scale


def norm_back(normed, scale, upstream):
    inner = row_mean(upstream * normed)
    return scale * (upstream - row_mean(upstream) - normed * inner)


def lane_hot(row, width):
    spread = jnp.transpose(jnp.broadcast_to(row.astype(f32), (lanes, lanes)))
    column = lax.broadcasted_iota(jnp.int32, (lanes, lanes), 1).astype(f32)
    parts = [
        jnp.where(spread == column + float(start), 1.0, 0.0).astype(bf16)
        for start in range(0, width, lanes)
    ]
    return jnp.concatenate(parts, 1)


def row_hot(row, count):
    index = lax.broadcasted_iota(jnp.int32, (count, lanes), 0)
    return jnp.where(index == row, 1.0, 0.0).astype(bf16)


def window(slots, block, own_rows, place_ref):
    core, odd = place_ref[0], place_ref[3]
    slot = slots[block]
    band = jnp.where(slot >= 6, 2, jnp.where(slot >= 3, 1, 0))
    sector = slot - 3 * band
    close = (sector == 2) == (odd == 0)
    side = jnp.where(sector == 1, 0, jnp.where(close, 1, 2))
    inside = (band == 2) == (core == 0)
    place = jnp.where(band == 1, -1, jnp.where(inside, 2, 5)) + side
    return pl.multiple_of(jnp.where(slot == 4, 0, own_rows + lanes * place), lanes)


def fill(table, own, near):
    table[0 : own.shape[0], :] = own[...]
    first = own.shape[0] + -own.shape[0] % lanes
    if first > own.shape[0]:
        table[own.shape[0] : first, :] = jnp.zeros_like(table[own.shape[0] : first, :])
    for part in near:
        table[first : first + part.shape[0], :] = part[...]
        first += part.shape[0]
    table[first:, :] = jnp.zeros_like(table[first:, :])


def send(source, target, sem):
    pltpu.make_async_copy(source, target, sem).start()


def finish(source, target, sem):
    pltpu.make_async_copy(source, target, sem).wait()


def prepare_kernel(live_ref, senders, receivers, state, weight, terms, *hots):
    nodes = state.shape[0]
    terms[0:nodes, :] = dot(state[...], weight[...]).astype(bf16)
    terms[nodes:, :] = jnp.zeros_like(terms[nodes:, :])
    block = lax.broadcasted_iota(jnp.int32, receivers.shape, 0)
    hot_rows(senders, jnp.where(block < live_ref[0], receivers[...], -1), *hots)


def hot_rows(senders, ends, send_hot, receive_hot, place_hot, sender_place_hot=None):
    for block in range(senders.shape[0]):
        here = slice(block * lanes, (block + 1) * lanes)
        begin_row, end_row = senders[block : block + 1, :], ends[block : block + 1, :]
        send_hot[here, :] = lane_hot(begin_row, send_hot.shape[1])
        receive_hot[here, :] = lane_hot(end_row, receive_hot.shape[1])
        place_hot[:, here] = row_hot(end_row, place_hot.shape[0])
        if sender_place_hot is not None:
            sender_place_hot[:, here] = row_hot(begin_row, sender_place_hot.shape[0])


def ends_kernel(live_ref, receivers, ends):
    block = lax.broadcasted_iota(jnp.int32, ends.shape, 0)
    ends[...] = jnp.where(block < live_ref[0], receivers[...], -1)


def encode_kernel(
    place_ref,
    slots,
    grid_columns,
    near_close,
    near_far,
    near_inner,
    near_inner_sides,
    near_outer,
    near_outer_sides,
    senders,
    ends,
    export,
    gain,
    base,
    receiver_weight,
    grid_weight,
    sender_weight,
    message_weight,
    update_weight,
    state,
    picked,
    inputs,
    hidden,
    pre_kept,
    mix_kept,
    normed_all,
    scale_all,
    update_normed,
    update_scale,
    table,
    projected,
    send_hot,
    receive_hot,
    place_hot,
):
    own = grid_columns.shape[1]
    nodes, width = base.shape
    projected[0:nodes, :] = dot(base[...], receiver_weight[...]).astype(bf16)
    projected[nodes:, :] = jnp.zeros_like(projected[nodes:, :])
    hot_rows(senders, ends, send_hot, receive_hot, place_hot)
    equal = lax.broadcasted_iota(jnp.int32, (own, own), 0) == lax.broadcasted_iota(
        jnp.int32, (own, own), 1
    )
    identity = jnp.where(equal, 1.0, 0.0).astype(bf16)
    grid_own = back_dot(identity, grid_columns[...]).astype(bf16)
    near = near_close, near_far, near_inner, near_inner_sides, near_outer, near_outer_sides
    fill(table, grid_own, near)
    for block in range(senders.shape[0]):
        here = slice(block * lanes, (block + 1) * lanes)
        start = window(slots, block, own, place_ref)
        inputs[here, :] = dot(send_hot[here, :], table[pl.ds(start, own), :]).astype(bf16)
    pre = dot(inputs[...], grid_weight[...])
    gate = sigmoid(pre)
    pre_kept[...] = pre.astype(bf16)
    hidden[...] = (pre * gate).astype(bf16)
    mix = dot(hidden[...], sender_weight[...]) + dot(receive_hot[...], projected[...])
    gate = sigmoid(mix)
    mix_kept[...] = mix.astype(bf16)
    product = dot((mix * gate).astype(bf16), message_weight[...])
    normed, scale = normalise(product)
    normed_all[...] = normed.astype(bf16)
    scale_all[...] = jnp.broadcast_to(scale, scale_all.shape)
    total = dot(place_hot[...], normed_all[...])
    update = dot(total.astype(bf16), update_weight[...])
    normed, scale = normalise(update)
    update_normed[...] = normed
    update_scale[...] = jnp.broadcast_to(scale, update_scale.shape)
    new_state = (base[...].astype(f32) + normed * gain[...]).astype(bf16)
    state[...] = new_state
    padded_state = jnp.concatenate([new_state, jnp.zeros((256 - nodes, width), bf16)], 0)
    picked[...] = dot(lane_hot(export[...], 256), padded_state).astype(bf16)


def process_kernel(
    place_ref,
    slots,
    state,
    near_close,
    near_far,
    near_inner,
    near_inner_sides,
    near_outer,
    near_outer_sides,
    terms,
    send_hot,
    receive_hot,
    place_hot,
    sender_place_hot,
    edge_sender,
    edge_message,
    node_update,
    gain,
    cotangent,
    mesh_far,
    own_grad,
    to_lon,
    to_inner,
    to_outer,
    to_outer_sides,
    sender_rows,
    mix_grads,
    table,
    slope,
    normed_all,
    upstream,
    table_grad,
    mesh_out,
    sem,
):
    nodes = state.shape[0]
    reach = 256
    near = near_close, near_far, near_inner, near_inner_sides, near_outer, near_outer_sides
    fill(table, state, near)
    blocks = slots.shape[0]
    starts = [window(slots, block, reach, place_ref) for block in range(blocks)]
    for block in range(blocks):
        here = slice(block * lanes, (block + 1) * lanes)
        picked = dot(send_hot[here, :], table[pl.ds(starts[block], reach), :])
        sender_rows[here, :] = picked.astype(bf16)
    mix = dot(sender_rows[...], edge_sender[...]) + dot(receive_hot[...], terms[...])
    gate = sigmoid(mix)
    slope[...] = (gate * (1.0 + mix * (1.0 - gate))).astype(bf16)
    product = dot((mix * gate).astype(bf16), edge_message[...])
    normed, edge_scale = normalise(product)
    normed_all[...] = normed.astype(bf16)
    total = dot(place_hot[...], normed_all[...])
    update = dot(total.astype(bf16), node_update[...])
    normed, scale = normalise(update)
    update_grad = norm_back(normed, scale, cotangent[...].astype(f32) * gain[...])
    upstream[0:nodes, :] = back_dot(update_grad.astype(bf16), node_update[...]).astype(bf16)
    upstream[nodes:, :] = jnp.zeros_like(upstream[nodes:, :])
    mesh_out[...] = (state[...].astype(f32) + normed * gain[...]).astype(bf16)
    send(mesh_out, mesh_far, sem)
    table_grad[...] = jnp.zeros_like(table_grad)
    arriving = dot(receive_hot[...], upstream[...])
    product_grad = norm_back(normed_all[...].astype(f32), edge_scale, arriving)
    mix_grad = back_dot(product_grad.astype(bf16), edge_message[...]) * slope[...].astype(f32)
    mix_grads[...] = mix_grad.astype(bf16)
    for block in range(blocks):
        here = slice(block * lanes, (block + 1) * lanes)
        table_grad[pl.ds(starts[block], nodes), :] += dot(
            sender_place_hot[:, here], mix_grads[here, :]
        )
    own_grad[...] = table_grad[0:nodes, :]
    first = reach
    for part in (to_lon, to_inner, to_outer, to_outer_sides):
        part[...] = table_grad[first : first + part.shape[0], :].astype(bf16)
        first += part.shape[0]
    finish(mesh_out, mesh_far, sem)


def edge_kernel(
    sender_rows,
    mix_grads,
    place_hot,
    edge_receiver,
    cotangent,
    ends,
    pre_kept,
    mix_kept,
    edge_grad,
    state_part,
    receive_hot,
    pre_slope,
    mix_slope,
):
    for block in range(ends.shape[0]):
        here = slice(block * lanes, (block + 1) * lanes)
        receive_hot[here, :] = lane_hot(ends[block : block + 1, :], receive_hot.shape[1])
    edge_grad[...] = cross_dot(sender_rows[...], mix_grads[...]).astype(bf16)
    receiver_grad = dot(place_hot[...], mix_grads[...]).astype(bf16)
    state_part[...] = cotangent[...].astype(f32) + back_dot(receiver_grad, edge_receiver[...])
    for kept, slope in ((pre_kept, pre_slope), (mix_kept, mix_slope)):
        value = kept[...].astype(f32)
        gate = sigmoid(value)
        slope[...] = (gate * (1.0 + value * (1.0 - gate))).astype(bf16)


def encode_back_kernel(
    place_ref,
    receive_hot,
    export,
    state_part,
    own_grad,
    from_inner,
    from_close,
    from_far,
    from_outer,
    edge_sender,
    update_normed,
    update_scale,
    gain,
    update_weight,
    normed_all,
    scale_all,
    mix_slope,
    pre_slope,
    inputs,
    hidden,
    message_weight,
    sender_weight,
    edge_grad,
    given,
    kept,
    upstream,
    grads,
):
    nodes, width = state_part.shape
    arrived = from_close[...].astype(f32) + from_far[...].astype(f32)
    copies = arrived.shape[0]
    arrived += from_inner[0:copies, :].astype(f32) + from_outer[0:copies, :].astype(f32)
    table_grad = own_grad[...] + dot(row_hot(export[...], nodes), arrived.astype(bf16))
    state_grad = state_part[...] + back_dot(table_grad.astype(bf16), edge_sender[...])
    update_grad = norm_back(update_normed[...], update_scale[:, 0:1], state_grad * gain[...])
    upstream[0:nodes, :] = back_dot(update_grad.astype(bf16), update_weight[...]).astype(bf16)
    upstream[nodes:, :] = jnp.zeros_like(upstream[nodes:, :])
    variables = inputs.shape[1]
    grads[width:, :] = jnp.zeros_like(grads[width:, :])
    arriving = dot(receive_hot[...], upstream[...])
    product_grad = norm_back(
        normed_all[...].astype(f32), scale_all[:, 0:1], arriving
    ).astype(bf16)
    mix_grad = back_dot(product_grad, message_weight[...]) * mix_slope[...].astype(f32)
    mix_grad = mix_grad.astype(bf16)
    grads[0:width, :] = cross_dot(hidden[...], mix_grad)
    pre_grad = back_dot(mix_grad, sender_weight[...]) * pre_slope[...].astype(f32)
    grads[width : width + variables, :] = cross_dot(
        inputs[...], pre_grad.astype(bf16)
    )
    arrange(place_ref, grads, edge_grad, given, kept)


def owner(place_ref, side, turn):
    return (place_ref[0] ^ side) * 4 + (place_ref[1 + side] ^ turn)


def rows_of(block, count, first=0):
    return pl.ds(pl.multiple_of(first + block * count, 32), count)


def arrange(place_ref, grads, edge_grad, given, kept):
    width = grads.shape[1]
    for side, target in ((1, given), (0, kept)):
        for turn in range(4):
            block = owner(place_ref, side, turn)
            first = turn * 160
            for count, source, base in ((64, grads, 0), (64, edge_grad, 0), (32, grads, width)):
                rows = source[rows_of(block, count, base), :]
                target[first : first + count, :] = rows.astype(bf16)
                first += count


def order(place_ref, side, source, sender_grad, edge_grad, parts, sems):
    copies = []
    for turn in range(4):
        block = owner(place_ref, side, turn)
        parts[turn] = source[turn * 160 : turn * 160 + 128, :].astype(f32)
        for index, target in enumerate((sender_grad, edge_grad)):
            copies.append(
                (
                    parts.at[turn, index * 64 : index * 64 + 64, :],
                    target.at[rows_of(block, 64), :],
                    sems.at[turn, index],
                )
            )
            send(*copies[-1])
    return copies


def order_mine_kernel(place_ref, mine, sender_grad, edge_grad, parts, sems):
    for copy in order(place_ref, 0, mine, sender_grad, edge_grad, parts, sems):
        finish(*copy)


def order_other_kernel(
    place_ref,
    mine,
    other,
    sender_in,
    edge_in,
    sender_grad,
    edge_grad,
    grid_grad,
    parts,
    grid_rows,
    last,
    sems,
    last_sem,
):
    copies = order(place_ref, 1, other, sender_grad, edge_grad, parts, sems)
    for side, source in ((0, mine), (1, other)):
        for turn in range(4):
            rows = source[turn * 160 + 128 : (turn + 1) * 160, :].astype(f32)
            grid_rows[rows_of(owner(place_ref, side, turn), 32), :] = rows
    last[...] = grid_rows[0 : last.shape[0], :]
    send(last, grid_grad, last_sem)
    for copy in copies:
        finish(*copy)
    finish(last, grid_grad, last_sem)


def call(kernel, operands, outs, scratch, scalars, mib, work=4, kept_places={}):
    smem = pl.BlockSpec(memory_space=pltpu.SMEM)
    vmem = pl.BlockSpec(memory_space=pltpu.VMEM)
    free = pl.BlockSpec(memory_space=pl.ANY)
    return pl.pallas_call(
        kernel,
        out_shape=[jax.ShapeDtypeStruct(shape, dtype) for shape, dtype, _ in outs],
        in_specs=[smem] * scalars
        + [free if index in kept_places else vmem for index in range(scalars, len(operands))],
        input_output_aliases=kept_places,
        out_specs=[free if kind else vmem for _, _, kind in outs],
        scratch_shapes=[pltpu.VMEM(*shape) if isinstance(shape, tuple) else shape for shape in scratch],
        compiler_params=pltpu.CompilerParams(vmem_limit_bytes=mib << 20),
        cost_estimate=pl.CostEstimate(flops=work << 30, bytes_accessed=8 << 20, transcendentals=0),
    )(*operands)


def partner(x, axis, flip):
    return lax.ppermute(x, axis, [(i, i ^ flip) for i in range(lax.axis_size(axis))])


def inner(x):
    return partner(x, "lat", 1)


def outer(x):
    ends = range(1, lax.axis_size("lat") - 1, 2)
    return lax.ppermute(x, "lat", [(i, i + 1) for i in ends] + [(i + 1, i) for i in ends])


def close(x):
    return partner(x, "lon", 1)


def far(x):
    size = lax.axis_size("lon")
    ends = range(1, size, 2)
    return lax.ppermute(
        x, "lon", [(i, (i + 1) % size) for i in ends] + [((i + 1) % size, i) for i in ends]
    )


def around(rows):
    near_outer, near_inner, near_close, near_far = outer(rows), inner(rows), close(rows), far(rows)
    near_inner, near_close, near_far = lax.optimization_barrier((near_inner, near_close, near_far))
    sides = jnp.concatenate([near_close, near_far], 0)
    return near_close, near_far, near_inner, inner(sides), near_outer, outer(sides)


def add(left, right):
    return (left.astype(f32) + right.astype(f32)).astype(bf16)


flips = {"x1": 32, "x3": 96, "y1": 4, "y3": 12, "z1": 1, "z3": 3}
stages = (
    (("x1", "y1"), ("x3", "y3")),
    (("z1", "x3"), ("z3", "x1")),
    (("y3", "z3"), ("y1", "z1")),
)


def met(x, stage, turn):
    pairs = []
    for device in range(lax.axis_size("lat") * lax.axis_size("lon")):
        first, second = stages[stage][device // 16 % 2]
        flip = (turn & 1) * flips[first] ^ (turn >> 1) * flips[second]
        pairs.append((device, device ^ flip))
    return lax.ppermute(x, ("lat", "lon"), pairs)


def added(own, one, two, three):
    pair = own.astype(f32) + one.astype(f32)
    return (pair + (two.astype(f32) + three.astype(f32))).astype(bf16)


def summed(given, kept):
    values = add(kept, inner(given))
    piece = values.shape[0] // 4
    own, *others = [values[turn * piece : (turn + 1) * piece] for turn in range(4)]
    values = added(own, *[met(part, 0, turn) for turn, part in zip((1, 2, 3), others)])
    for stage in (1, 2):
        values = added(values, *[met(values, stage, turn) for turn in (1, 2, 3)])
    values = jnp.concatenate([values] + [met(values, 0, turn) for turn in (1, 2, 3)], 0)
    return values


def local(
    grid_in,
    grid_export,
    mesh_init,
    encode_senders,
    encode_slots,
    encode_receivers,
    encode_live,
    mesh_export,
    process_senders,
    process_slots,
    process_receivers,
    process_live,
    grid_weight,
    sender_weight,
    receiver_weight,
    message_weight,
    update_weight,
    encode_gain,
    edge_sender,
    edge_receiver,
    edge_message,
    node_update,
    node_gain,
    cotangent,
):
    grid_count, variables = grid_in.shape
    nodes, width = mesh_init.shape
    copies = mesh_export.shape[0]
    edges = encode_senders.shape[0] * encode_senders.shape[1]
    core, chip, row = [
        part.astype(jnp.int32)
        for part in (
            lax.axis_index("lat") & 1,
            lax.axis_index("lat") >> 1,
            lax.axis_index("lon") >> 2,
        )
    ]
    odd = lax.axis_index("lon").astype(jnp.int32) & 1
    plain = (chip & 1 ^ chip >> 1) | (row & 1 ^ row >> 1) << 1
    wrapped = chip >> 1 | row >> 1 << 1
    first, second = jnp.where(core == 0, plain, wrapped), jnp.where(core == 0, wrapped, plain)
    place = jnp.stack([core, first, second, odd])
    select = (grid_export[:, None] == jnp.arange(grid_count)[None, :]).astype(bf16)
    grid_near = around(dot(select, grid_in).astype(bf16))
    export = mesh_export[None]
    encode_gain, node_gain = encode_gain[None], node_gain[None]
    saved = [
        ((edges, variables), bf16, 0),
        ((edges, width), bf16, 0),
        ((edges, width), bf16, 0),
        ((edges, width), bf16, 0),
        ((edges, width), bf16, 0),
        ((edges, lanes), f32, 0),
        ((nodes, width), f32, 0),
        ((nodes, lanes), f32, 0),
    ]
    (ends,) = call(
        ends_kernel,
        (encode_live, encode_receivers),
        [(encode_receivers.shape, jnp.int32, 0)],
        [],
        1,
        16,
        30,
    )
    state, picked, inputs, hidden, pre_kept, mix_kept, normed, scale, *update = call(
        encode_kernel,
        (
            place,
            encode_slots,
            jnp.transpose(grid_in),
            *grid_near,
            encode_senders,
            ends,
            export,
            encode_gain,
            mesh_init,
            receiver_weight,
            grid_weight,
            sender_weight,
            message_weight,
            update_weight,
        ),
        [((nodes, width), bf16, 0), ((copies, width), bf16, 0)] + saved,
        [
            ((grid_count + 8 * lanes + grid_count - lanes, variables), bf16),
            ((256, width), bf16),
            ((edges, grid_count), bf16),
            ((edges, 256), bf16),
            ((nodes, edges), bf16),
        ],
        2,
        20,
    )
    terms, process_send, process_receive, process_place, process_sender_place = call(
        prepare_kernel,
        (process_live, process_senders, process_receivers, state, edge_receiver),
        [
            ((256, width), bf16, 0),
            ((edges, 256), bf16, 0),
            ((edges, 256), bf16, 0),
            ((nodes, edges), bf16, 0),
            ((nodes, edges), bf16, 0),
        ],
        [],
        1,
        16,
    )
    near = around(picked)
    (
        mesh_out,
        own_grad,
        to_lon,
        to_inner,
        to_outer,
        to_outer_sides,
        sender_rows,
        mix_grad,
    ) = call(
        process_kernel,
        (
            place,
            process_slots,
            state,
            *near,
            terms,
            process_send,
            process_receive,
            process_place,
            process_sender_place,
            edge_sender,
            edge_message,
            node_update,
            node_gain,
            cotangent,
        ),
        [
            ((nodes, width), bf16, 1),
            ((nodes, width), f32, 0),
            ((2 * copies, width), bf16, 0),
            ((3 * copies, width), bf16, 0),
            ((copies, width), bf16, 0),
            ((2 * copies, width), bf16, 0),
            ((edges, width), bf16, 0),
            ((edges, width), bf16, 0),
        ],
        [
            ((256 + 8 * copies + 128, width), bf16),
            ((edges, width), bf16),
            ((edges, width), bf16),
            ((256, width), bf16),
            ((256 + 8 * copies + 128, width), f32),
            ((nodes, width), bf16),
            pltpu.SemaphoreType.DMA,
        ],
        2,
        26,
    )
    from_outer_sides = outer(to_outer_sides)
    from_outer, from_inner = outer(to_outer), inner(to_inner)
    to_close, to_far = [
        (
            to_lon[side * copies : (side + 1) * copies].astype(f32)
            + from_inner[(side + 1) * copies : (side + 2) * copies].astype(f32)
            + from_outer_sides[side * copies : (side + 1) * copies].astype(f32)
        ).astype(bf16)
        for side in (0, 1)
    ]
    from_close, from_far = close(to_close), far(to_far)
    edge_grad, state_part, receive_hot, pre_slope, mix_slope = call(
        edge_kernel,
        (sender_rows, mix_grad, process_place, edge_receiver, cotangent, ends, pre_kept, mix_kept),
        [((width, width), bf16, 0), ((nodes, width), f32, 0), ((edges, 256), bf16, 0)]
        + [((edges, width), bf16, 0)] * 2,
        [],
        0,
        16,
    )
    given, kept = call(
        encode_back_kernel,
        (
            place,
            receive_hot,
            export,
            state_part,
            own_grad,
            from_inner,
            from_close,
            from_far,
            from_outer,
            edge_sender,
            update[0],
            update[1],
            encode_gain,
            update_weight,
            normed,
            scale,
            mix_slope,
            pre_slope,
            inputs,
            hidden,
            message_weight,
            sender_weight,
            edge_grad,
        ),
        [((640, width), bf16, 0)] * 2,
        [((256, width), bf16), ((768, width), f32)],
        1,
        16,
    )
    mine = summed(given, kept)
    other = inner(mine)
    halves = [((width, width), f32, 1)] * 2
    scratch = [((4, 128, width), f32), pltpu.SemaphoreType.DMA((4, 2))]
    parts = call(order_mine_kernel, (place, mine), halves, scratch, 1, 8)
    sender_grad, edge_grad, grid_grad = call(
        order_other_kernel,
        (place, mine, other, *parts),
        halves + [((variables, width), f32, 1)],
        scratch[:1]
        + [((256, width), f32), ((variables, width), f32)]
        + scratch[1:]
        + [pltpu.SemaphoreType.DMA],
        1,
        8,
        kept_places={3: 0, 4: 1},
    )
    return mesh_out, grid_grad, sender_grad, edge_grad


def solution(mesh):
    tiles, shared = P(("lat", "lon")), P()
    wide = P(("lat", "lon"), None)
    return jax.shard_map(
        local,
        mesh=mesh,
        in_specs=(
            (wide, tiles, wide, wide, tiles, wide, tiles, tiles, wide, tiles, wide, tiles)
            + (shared,) * 11
            + (wide,)
        ),
        out_specs=(wide, shared, shared, shared),
        check_vma=False,
    )
```

```python
import jax
import jax.numpy as jnp
from jax import lax
from jax.experimental import pallas as pl
from jax.experimental.pallas import tpu as pltpu
from jax.sharding import PartitionSpec as P

norm_epsilon = 1e-05
lanes = 128
f32 = jnp.float32
bf16 = jnp.bfloat16


def dot(left, right):
    return jnp.dot(left, right, preferred_element_type=f32)


def back_dot(left, weight):
    return lax.dot_general(left, weight, (((1,), (1,)), ((), ())), preferred_element_type=f32)


def cross_dot(left, right):
    return lax.dot_general(left, right, (((0,), (0,)), ((), ())), preferred_element_type=f32)


def sigmoid(values):
    return 0.5 * jnp.tanh(0.5 * values) + 0.5


def row_mean(values):
    return jnp.mean(values, axis=-1, keepdims=True)


def normalise(values):
    center = values - row_mean(values)
    scale = lax.rsqrt(row_mean(center * center) + norm_epsilon)
    return center * scale, scale


def norm_back(normed, scale, upstream):
    inner = row_mean(upstream * normed)
    return scale * (upstream - row_mean(upstream) - normed * inner)


def lane_hot(row, width):
    spread = jnp.transpose(jnp.broadcast_to(row.astype(f32), (lanes, lanes)))
    column = lax.broadcasted_iota(jnp.int32, (lanes, lanes), 1).astype(f32)
    parts = [
        jnp.where(spread == column + float(start), 1.0, 0.0).astype(bf16)
        for start in range(0, width, lanes)
    ]
    return jnp.concatenate(parts, 1)


def row_hot(row, count):
    index = lax.broadcasted_iota(jnp.int32, (count, lanes), 0)
    return jnp.where(index == row, 1.0, 0.0).astype(bf16)


def window(slots, block, own_rows, place_ref):
    core, odd = place_ref[0], place_ref[3]
    slot = slots[block]
    band = jnp.where(slot >= 6, 2, jnp.where(slot >= 3, 1, 0))
    sector = slot - 3 * band
    close = (sector == 2) == (odd == 0)
    side = jnp.where(sector == 1, 0, jnp.where(close, 1, 2))
    inside = (band == 2) == (core == 0)
    place = jnp.where(band == 1, -1, jnp.where(inside, 2, 5)) + side
    return pl.multiple_of(jnp.where(slot == 4, 0, own_rows + lanes * place), lanes)


def fill(table, own, near):
    table[0 : own.shape[0], :] = own[...]
    first = own.shape[0] + -own.shape[0] % lanes
    if first > own.shape[0]:
        table[own.shape[0] : first, :] = jnp.zeros_like(table[own.shape[0] : first, :])
    for part in near:
        table[first : first + part.shape[0], :] = part[...]
        first += part.shape[0]
    table[first:, :] = jnp.zeros_like(table[first:, :])


def send(source, target, sem):
    pltpu.make_async_copy(source, target, sem).start()


def finish(source, target, sem):
    pltpu.make_async_copy(source, target, sem).wait()


def prepare_kernel(
    live_ref, senders, receivers, state, weight, pre_kept, mix_kept, terms, *refs
):
    pre_slope, mix_slope, *hots = refs
    for kept, slope in ((pre_kept, pre_slope), (mix_kept, mix_slope)):
        value = kept[...].astype(f32)
        gate = sigmoid(value)
        slope[...] = (gate * (1.0 + value * (1.0 - gate))).astype(bf16)
    nodes = state.shape[0]
    terms[0:nodes, :] = dot(state[...], weight[...]).astype(bf16)
    terms[nodes:, :] = jnp.zeros_like(terms[nodes:, :])
    block = lax.broadcasted_iota(jnp.int32, receivers.shape, 0)
    hot_rows(senders, jnp.where(block < live_ref[0], receivers[...], -1), *hots)


def hot_rows(senders, ends, send_hot, receive_hot, place_hot, sender_place_hot=None):
    for block in range(senders.shape[0]):
        here = slice(block * lanes, (block + 1) * lanes)
        begin_row, end_row = senders[block : block + 1, :], ends[block : block + 1, :]
        send_hot[here, :] = lane_hot(begin_row, send_hot.shape[1])
        receive_hot[here, :] = lane_hot(end_row, receive_hot.shape[1])
        place_hot[:, here] = row_hot(end_row, place_hot.shape[0])
        if sender_place_hot is not None:
            sender_place_hot[:, here] = row_hot(begin_row, sender_place_hot.shape[0])


def ends_kernel(live_ref, receivers, ends):
    block = lax.broadcasted_iota(jnp.int32, ends.shape, 0)
    ends[...] = jnp.where(block < live_ref[0], receivers[...], -1)


def encode_kernel(
    place_ref,
    slots,
    grid_columns,
    near_close,
    near_far,
    near_inner,
    near_inner_sides,
    near_outer,
    near_outer_sides,
    senders,
    ends,
    export,
    gain,
    base,
    receiver_weight,
    grid_weight,
    sender_weight,
    message_weight,
    update_weight,
    state,
    picked,
    inputs,
    hidden,
    pre_kept,
    mix_kept,
    normed_all,
    scale_all,
    update_normed,
    update_scale,
    table,
    projected,
    send_hot,
    receive_hot,
    place_hot,
):
    own = grid_columns.shape[1]
    nodes, width = base.shape
    projected[0:nodes, :] = dot(base[...], receiver_weight[...]).astype(bf16)
    projected[nodes:, :] = jnp.zeros_like(projected[nodes:, :])
    hot_rows(senders, ends, send_hot, receive_hot, place_hot)
    equal = lax.broadcasted_iota(jnp.int32, (own, own), 0) == lax.broadcasted_iota(
        jnp.int32, (own, own), 1
    )
    identity = jnp.where(equal, 1.0, 0.0).astype(bf16)
    grid_own = back_dot(identity, grid_columns[...]).astype(bf16)
    near = near_close, near_far, near_inner, near_inner_sides, near_outer, near_outer_sides
    fill(table, grid_own, near)
    for block in range(senders.shape[0]):
        here = slice(block * lanes, (block + 1) * lanes)
        start = window(slots, block, own, place_ref)
        inputs[here, :] = dot(send_hot[here, :], table[pl.ds(start, own), :]).astype(bf16)
    pre = dot(inputs[...], grid_weight[...])
    gate = sigmoid(pre)
    pre_kept[...] = pre.astype(bf16)
    hidden[...] = (pre * gate).astype(bf16)
    mix = dot(hidden[...], sender_weight[...]) + dot(receive_hot[...], projected[...])
    gate = sigmoid(mix)
    mix_kept[...] = mix.astype(bf16)
    product = dot((mix * gate).astype(bf16), message_weight[...])
    normed, scale = normalise(product)
    normed_all[...] = normed.astype(bf16)
    scale_all[...] = jnp.broadcast_to(scale, scale_all.shape)
    total = dot(place_hot[...], normed_all[...])
    update = dot(total.astype(bf16), update_weight[...])
    normed, scale = normalise(update)
    update_normed[...] = normed
    update_scale[...] = jnp.broadcast_to(scale, update_scale.shape)
    new_state = (base[...].astype(f32) + normed * gain[...]).astype(bf16)
    state[...] = new_state
    padded_state = jnp.concatenate([new_state, jnp.zeros((256 - nodes, width), bf16)], 0)
    picked[...] = dot(lane_hot(export[...], 256), padded_state).astype(bf16)


def process_kernel(
    place_ref,
    slots,
    state,
    near_close,
    near_far,
    near_inner,
    near_inner_sides,
    near_outer,
    near_outer_sides,
    terms,
    send_hot,
    receive_hot,
    place_hot,
    sender_place_hot,
    edge_sender,
    edge_message,
    node_update,
    gain,
    cotangent,
    mesh_far,
    own_grad,
    to_lon,
    to_inner,
    to_outer,
    to_outer_sides,
    sender_rows,
    mix_grads,
    table,
    slope,
    normed_all,
    upstream,
    table_grad,
    mesh_out,
    sem,
):
    nodes = state.shape[0]
    reach = 256
    near = near_close, near_far, near_inner, near_inner_sides, near_outer, near_outer_sides
    fill(table, state, near)
    blocks = slots.shape[0]
    starts = [window(slots, block, reach, place_ref) for block in range(blocks)]
    for block in range(blocks):
        here = slice(block * lanes, (block + 1) * lanes)
        picked = dot(send_hot[here, :], table[pl.ds(starts[block], reach), :])
        sender_rows[here, :] = picked.astype(bf16)
    mix = dot(sender_rows[...], edge_sender[...]) + dot(receive_hot[...], terms[...])
    gate = sigmoid(mix)
    slope[...] = (gate * (1.0 + mix * (1.0 - gate))).astype(bf16)
    product = dot((mix * gate).astype(bf16), edge_message[...])
    normed, edge_scale = normalise(product)
    normed_all[...] = normed.astype(bf16)
    total = dot(place_hot[...], normed_all[...])
    update = dot(total.astype(bf16), node_update[...])
    normed, scale = normalise(update)
    update_grad = norm_back(normed, scale, cotangent[...].astype(f32) * gain[...])
    upstream[0:nodes, :] = back_dot(update_grad.astype(bf16), node_update[...]).astype(bf16)
    upstream[nodes:, :] = jnp.zeros_like(upstream[nodes:, :])
    mesh_out[...] = (state[...].astype(f32) + normed * gain[...]).astype(bf16)
    send(mesh_out, mesh_far, sem)
    table_grad[...] = jnp.zeros_like(table_grad)
    arriving = dot(receive_hot[...], upstream[...])
    product_grad = norm_back(normed_all[...].astype(f32), edge_scale, arriving)
    mix_grad = back_dot(product_grad.astype(bf16), edge_message[...]) * slope[...].astype(f32)
    mix_grads[...] = mix_grad.astype(bf16)
    for block in range(blocks):
        here = slice(block * lanes, (block + 1) * lanes)
        table_grad[pl.ds(starts[block], nodes), :] += dot(
            sender_place_hot[:, here], mix_grads[here, :]
        )
    own_grad[...] = table_grad[0:nodes, :]
    first = reach
    for part in (to_lon, to_inner, to_outer, to_outer_sides):
        part[...] = table_grad[first : first + part.shape[0], :].astype(bf16)
        first += part.shape[0]
    finish(mesh_out, mesh_far, sem)


def edge_kernel(
    sender_rows,
    mix_grads,
    place_hot,
    edge_receiver,
    cotangent,
    ends,
    edge_grad,
    state_part,
    receive_hot,
):
    for block in range(ends.shape[0]):
        here = slice(block * lanes, (block + 1) * lanes)
        receive_hot[here, :] = lane_hot(ends[block : block + 1, :], receive_hot.shape[1])
    edge_grad[...] = cross_dot(sender_rows[...], mix_grads[...]).astype(bf16)
    receiver_grad = dot(place_hot[...], mix_grads[...]).astype(bf16)
    state_part[...] = cotangent[...].astype(f32) + back_dot(receiver_grad, edge_receiver[...])


def encode_back_kernel(
    place_ref,
    receive_hot,
    export,
    state_part,
    own_grad,
    from_inner,
    from_close,
    from_far,
    from_outer,
    edge_sender,
    update_normed,
    update_scale,
    gain,
    update_weight,
    normed_all,
    scale_all,
    mix_slope,
    pre_slope,
    inputs,
    hidden,
    message_weight,
    sender_weight,
    edge_grad,
    given,
    kept,
    upstream,
    grads,
):
    nodes, width = state_part.shape
    arrived = from_close[...].astype(f32) + from_far[...].astype(f32)
    copies = arrived.shape[0]
    arrived += from_inner[0:copies, :].astype(f32) + from_outer[0:copies, :].astype(f32)
    table_grad = own_grad[...] + dot(row_hot(export[...], nodes), arrived.astype(bf16))
    state_grad = state_part[...] + back_dot(table_grad.astype(bf16), edge_sender[...])
    update_grad = norm_back(update_normed[...], update_scale[:, 0:1], state_grad * gain[...])
    upstream[0:nodes, :] = back_dot(update_grad.astype(bf16), update_weight[...]).astype(bf16)
    upstream[nodes:, :] = jnp.zeros_like(upstream[nodes:, :])
    variables = inputs.shape[1]
    grads[width:, :] = jnp.zeros_like(grads[width:, :])
    arriving = dot(receive_hot[...], upstream[...])
    product_grad = norm_back(
        normed_all[...].astype(f32), scale_all[:, 0:1], arriving
    ).astype(bf16)
    mix_grad = back_dot(product_grad, message_weight[...]) * mix_slope[...].astype(f32)
    mix_grad = mix_grad.astype(bf16)
    grads[0:width, :] = cross_dot(hidden[...], mix_grad)
    pre_grad = back_dot(mix_grad, sender_weight[...]) * pre_slope[...].astype(f32)
    grads[width : width + variables, :] = cross_dot(
        inputs[...], pre_grad.astype(bf16)
    )
    arrange(place_ref, grads, edge_grad, given, kept)


def owner(place_ref, side, turn):
    return (place_ref[0] ^ side) * 4 + (place_ref[1 + side] ^ turn)


def rows_of(block, count, first=0):
    return pl.ds(pl.multiple_of(first + block * count, 32), count)


def arrange(place_ref, grads, edge_grad, given, kept):
    width = grads.shape[1]
    for side, target in ((1, given), (0, kept)):
        for turn in range(4):
            block = owner(place_ref, side, turn)
            first = turn * 160
            for count, source, base in ((64, grads, 0), (64, edge_grad, 0), (32, grads, width)):
                rows = source[rows_of(block, count, base), :]
                target[first : first + count, :] = rows.astype(bf16)
                first += count


def order(place_ref, side, source, sender_grad, edge_grad, parts, sems):
    copies = []
    for turn in range(4):
        block = owner(place_ref, side, turn)
        parts[turn] = source[turn * 160 : turn * 160 + 128, :].astype(f32)
        for index, target in enumerate((sender_grad, edge_grad)):
            copies.append(
                (
                    parts.at[turn, index * 64 : index * 64 + 64, :],
                    target.at[rows_of(block, 64), :],
                    sems.at[turn, index],
                )
            )
            send(*copies[-1])
    return copies


def order_mine_kernel(place_ref, mine, sender_grad, edge_grad, parts, sems):
    for copy in order(place_ref, 0, mine, sender_grad, edge_grad, parts, sems):
        finish(*copy)


def order_other_kernel(
    place_ref,
    mine,
    other,
    sender_in,
    edge_in,
    sender_grad,
    edge_grad,
    grid_grad,
    parts,
    grid_rows,
    last,
    sems,
    last_sem,
):
    copies = order(place_ref, 1, other, sender_grad, edge_grad, parts, sems)
    for side, source in ((0, mine), (1, other)):
        for turn in range(4):
            rows = source[turn * 160 + 128 : (turn + 1) * 160, :].astype(f32)
            grid_rows[rows_of(owner(place_ref, side, turn), 32), :] = rows
    last[...] = grid_rows[0 : last.shape[0], :]
    send(last, grid_grad, last_sem)
    for copy in copies:
        finish(*copy)
    finish(last, grid_grad, last_sem)


def call(kernel, operands, outs, scratch, scalars, mib, work=4, kept_places={}):
    smem = pl.BlockSpec(memory_space=pltpu.SMEM)
    vmem = pl.BlockSpec(memory_space=pltpu.VMEM)
    free = pl.BlockSpec(memory_space=pl.ANY)
    return pl.pallas_call(
        kernel,
        out_shape=[jax.ShapeDtypeStruct(shape, dtype) for shape, dtype, _ in outs],
        in_specs=[smem] * scalars
        + [free if index in kept_places else vmem for index in range(scalars, len(operands))],
        input_output_aliases=kept_places,
        out_specs=[free if kind else vmem for _, _, kind in outs],
        scratch_shapes=[pltpu.VMEM(*shape) if isinstance(shape, tuple) else shape for shape in scratch],
        compiler_params=pltpu.CompilerParams(vmem_limit_bytes=mib << 20),
        cost_estimate=pl.CostEstimate(flops=work << 30, bytes_accessed=8 << 20, transcendentals=0),
    )(*operands)


def partner(x, axis, flip):
    return lax.ppermute(x, axis, [(i, i ^ flip) for i in range(lax.axis_size(axis))])


def inner(x):
    return partner(x, "lat", 1)


def outer(x):
    ends = range(1, lax.axis_size("lat") - 1, 2)
    return lax.ppermute(x, "lat", [(i, i + 1) for i in ends] + [(i + 1, i) for i in ends])


def close(x):
    return partner(x, "lon", 1)


def far(x):
    size = lax.axis_size("lon")
    ends = range(1, size, 2)
    return lax.ppermute(
        x, "lon", [(i, (i + 1) % size) for i in ends] + [((i + 1) % size, i) for i in ends]
    )


def around(rows):
    near_outer, near_inner, near_close, near_far = outer(rows), inner(rows), close(rows), far(rows)
    near_inner, near_close, near_far = lax.optimization_barrier((near_inner, near_close, near_far))
    sides = jnp.concatenate([near_close, near_far], 0)
    return near_close, near_far, near_inner, inner(sides), near_outer, outer(sides)


def add(left, right):
    return (left.astype(f32) + right.astype(f32)).astype(bf16)


flips = {"x1": 32, "x3": 96, "y1": 4, "y3": 12, "z1": 1, "z3": 3}
stages = (
    (("x1", "y1"), ("x3", "y3")),
    (("z1", "x3"), ("z3", "x1")),
    (("y3", "z3"), ("y1", "z1")),
)


def met(x, stage, turn):
    pairs = []
    for device in range(lax.axis_size("lat") * lax.axis_size("lon")):
        first, second = stages[stage][device // 16 % 2]
        flip = (turn & 1) * flips[first] ^ (turn >> 1) * flips[second]
        pairs.append((device, device ^ flip))
    return lax.ppermute(x, ("lat", "lon"), pairs)


def added(own, one, two, three):
    pair = own.astype(f32) + one.astype(f32)
    return (pair + (two.astype(f32) + three.astype(f32))).astype(bf16)


def summed(given, kept):
    values = add(kept, inner(given))
    piece = values.shape[0] // 4
    own, *others = [values[turn * piece : (turn + 1) * piece] for turn in range(4)]
    values = added(own, *[met(part, 0, turn) for turn, part in zip((1, 2, 3), others)])
    for stage in (1, 2):
        values = added(values, *[met(values, stage, turn) for turn in (1, 2, 3)])
    values = jnp.concatenate([values] + [met(values, 0, turn) for turn in (1, 2, 3)], 0)
    return values


def local(
    grid_in,
    grid_export,
    mesh_init,
    encode_senders,
    encode_slots,
    encode_receivers,
    encode_live,
    mesh_export,
    process_senders,
    process_slots,
    process_receivers,
    process_live,
    grid_weight,
    sender_weight,
    receiver_weight,
    message_weight,
    update_weight,
    encode_gain,
    edge_sender,
    edge_receiver,
    edge_message,
    node_update,
    node_gain,
    cotangent,
):
    grid_count, variables = grid_in.shape
    nodes, width = mesh_init.shape
    copies = mesh_export.shape[0]
    edges = encode_senders.shape[0] * encode_senders.shape[1]
    core, chip, row = [
        part.astype(jnp.int32)
        for part in (
            lax.axis_index("lat") & 1,
            lax.axis_index("lat") >> 1,
            lax.axis_index("lon") >> 2,
        )
    ]
    odd = lax.axis_index("lon").astype(jnp.int32) & 1
    plain = (chip & 1 ^ chip >> 1) | (row & 1 ^ row >> 1) << 1
    wrapped = chip >> 1 | row >> 1 << 1
    first, second = jnp.where(core == 0, plain, wrapped), jnp.where(core == 0, wrapped, plain)
    place = jnp.stack([core, first, second, odd])
    select = (grid_export[:, None] == jnp.arange(grid_count)[None, :]).astype(bf16)
    grid_near = around(dot(select, grid_in).astype(bf16))
    export = mesh_export[None]
    encode_gain, node_gain = encode_gain[None], node_gain[None]
    saved = [
        ((edges, variables), bf16, 0),
        ((edges, width), bf16, 0),
        ((edges, width), bf16, 0),
        ((edges, width), bf16, 0),
        ((edges, width), bf16, 0),
        ((edges, lanes), f32, 0),
        ((nodes, width), f32, 0),
        ((nodes, lanes), f32, 0),
    ]
    (ends,) = call(
        ends_kernel,
        (encode_live, encode_receivers),
        [(encode_receivers.shape, jnp.int32, 0)],
        [],
        1,
        16,
        30,
    )
    state, picked, inputs, hidden, pre_kept, mix_kept, normed, scale, *update = call(
        encode_kernel,
        (
            place,
            encode_slots,
            jnp.transpose(grid_in),
            *grid_near,
            encode_senders,
            ends,
            export,
            encode_gain,
            mesh_init,
            receiver_weight,
            grid_weight,
            sender_weight,
            message_weight,
            update_weight,
        ),
        [((nodes, width), bf16, 0), ((copies, width), bf16, 0)] + saved,
        [
            ((grid_count + 8 * lanes + grid_count - lanes, variables), bf16),
            ((256, width), bf16),
            ((edges, grid_count), bf16),
            ((edges, 256), bf16),
            ((nodes, edges), bf16),
        ],
        2,
        20,
    )
    terms, pre_slope, mix_slope, process_send, process_receive, process_place, process_sender_place = call(
        prepare_kernel,
        (process_live, process_senders, process_receivers, state, edge_receiver, pre_kept, mix_kept),
        [
            ((256, width), bf16, 0),
            ((edges, width), bf16, 0),
            ((edges, width), bf16, 0),
            ((edges, 256), bf16, 0),
            ((edges, 256), bf16, 0),
            ((nodes, edges), bf16, 0),
            ((nodes, edges), bf16, 0),
        ],
        [],
        1,
        16,
    )
    near = around(picked)
    (
        mesh_out,
        own_grad,
        to_lon,
        to_inner,
        to_outer,
        to_outer_sides,
        sender_rows,
        mix_grad,
    ) = call(
        process_kernel,
        (
            place,
            process_slots,
            state,
            *near,
            terms,
            process_send,
            process_receive,
            process_place,
            process_sender_place,
            edge_sender,
            edge_message,
            node_update,
            node_gain,
            cotangent,
        ),
        [
            ((nodes, width), bf16, 1),
            ((nodes, width), f32, 0),
            ((2 * copies, width), bf16, 0),
            ((3 * copies, width), bf16, 0),
            ((copies, width), bf16, 0),
            ((2 * copies, width), bf16, 0),
            ((edges, width), bf16, 0),
            ((edges, width), bf16, 0),
        ],
        [
            ((256 + 8 * copies + 128, width), bf16),
            ((edges, width), bf16),
            ((edges, width), bf16),
            ((256, width), bf16),
            ((256 + 8 * copies + 128, width), f32),
            ((nodes, width), bf16),
            pltpu.SemaphoreType.DMA,
        ],
        2,
        26,
    )
    from_outer_sides = outer(to_outer_sides)
    from_outer, from_inner = outer(to_outer), inner(to_inner)
    to_close, to_far = [
        (
            to_lon[side * copies : (side + 1) * copies].astype(f32)
            + from_inner[(side + 1) * copies : (side + 2) * copies].astype(f32)
            + from_outer_sides[side * copies : (side + 1) * copies].astype(f32)
        ).astype(bf16)
        for side in (0, 1)
    ]
    from_close, from_far = close(to_close), far(to_far)
    edge_grad, state_part, receive_hot = call(
        edge_kernel,
        (sender_rows, mix_grad, process_place, edge_receiver, cotangent, ends),
        [((width, width), bf16, 0), ((nodes, width), f32, 0), ((edges, 256), bf16, 0)],
        [],
        0,
        16,
    )
    given, kept = call(
        encode_back_kernel,
        (
            place,
            receive_hot,
            export,
            state_part,
            own_grad,
            from_inner,
            from_close,
            from_far,
            from_outer,
            edge_sender,
            update[0],
            update[1],
            encode_gain,
            update_weight,
            normed,
            scale,
            mix_slope,
            pre_slope,
            inputs,
            hidden,
            message_weight,
            sender_weight,
            edge_grad,
        ),
        [((640, width), bf16, 0)] * 2,
        [((256, width), bf16), ((768, width), f32)],
        1,
        16,
    )
    mine = summed(given, kept)
    other = inner(mine)
    halves = [((width, width), f32, 1)] * 2
    scratch = [((4, 128, width), f32), pltpu.SemaphoreType.DMA((4, 2))]
    parts = call(order_mine_kernel, (place, mine), halves, scratch, 1, 8)
    sender_grad, edge_grad, grid_grad = call(
        order_other_kernel,
        (place, mine, other, *parts),
        halves + [((variables, width), f32, 1)],
        scratch[:1]
        + [((256, width), f32), ((variables, width), f32)]
        + scratch[1:]
        + [pltpu.SemaphoreType.DMA],
        1,
        8,
        kept_places={3: 0, 4: 1},
    )
    return mesh_out, grid_grad, sender_grad, edge_grad


def solution(mesh):
    tiles, shared = P(("lat", "lon")), P()
    wide = P(("lat", "lon"), None)
    return jax.shard_map(
        local,
        mesh=mesh,
        in_specs=(
            (wide, tiles, wide, wide, tiles, wide, tiles, tiles, wide, tiles, wide, tiles)
            + (shared,) * 11
            + (wide,)
        ),
        out_specs=(wide, shared, shared, shared),
        check_vma=False,
    )
```
